128 devices in a mesh: gx: 8 (over z, core), gy: 16 (over x, y).
Axes of the slice: x: 4, y: 4, z: 4, core: 2. Of those that a mesh axis runs over, the one named last changes fastest.
Arguments:
- pressure_previous: float32 [128, 512, 128], P('gx', 'gy'), may hold values from -6 to 6
- pressure_current: float32 [128, 512, 128], P('gx', 'gy'), may hold values from -6 to 6
- adjoint_next: float32 [128, 512, 128], P('gx', 'gy'), may hold values from -6 to 6
- adjoint_current: float32 [128, 512, 128], P('gx', 'gy'), may hold values from -6 to 6
- inverse_modulus: float32 [128, 512, 128], P('gx', 'gy'), may hold values from 0.5 to 2
- inverse_density: float32 [128, 512, 128], P('gx', 'gy'), may hold values from 0.5 to 2
- face_mask: int32 [6, 16, 64, 16], P(None, 'gx', 'gy'), may hold values 0 or 1
Outputs:
- density_kernel: float32 [128, 512, 128], P('gx', 'gy')
- modulus_kernel: float32 [128, 512, 128], P('gx', 'gy')
- impedance_kernel: float32 [128, 512, 128], P('gx', 'gy')
The draws below stay inside these ranges and needn't reach their ends.
All inputs are finite; a program needn't handle non-finite values. No bound on the sum of `face_mask` on one device may be relied on, other than what follows from the above.
Results may differ from the reference program's by a relative error of at most 0.0001.
Values sent between devices are 32-bit elements; how exact they have to be, the bound alone decides.
A program may use at most 128 MiB of HBM per device.

```python
import math
import jax
import jax.numpy as jnp
import numpy as np
from jax import lax

NODES = 8
EZD = 16
STEPS = 8
NEX = 16
NEY = 64
NX = 128
NY = 512
NZ = 128


def set_ends(drawn, own_key, least, high):
    dims = drawn.shape
    spot = [jax.random.randint(jax.random.fold_in(own_key, axis), (), 0, dims[axis]) for axis in range(len(dims))]
    drawn = drawn.at[tuple(spot)].set(least)
    longest = dims.index(max(dims))
    spot[longest] = (spot[longest] + 1) % dims[longest]
    return drawn.at[tuple(spot)].set(high)


def block_levels(stream_key, dims, cuts, smallest, high):
    loudness = 1.0
    for dim, parts in cuts:
        heights = jax.random.uniform(jax.random.fold_in(jax.random.fold_in(stream_key, 6), dim), (parts,), jnp.float32, smallest / len(cuts), high / len(cuts))
        loudness = loudness * jnp.repeat(jnp.exp(heights), dims[dim] // parts).reshape((-1,) + (1,) * (len(dims) - 1 - dim))
    return loudness


def bell_draw(own_key, extent, scale, most, cuts=(), held_as=jnp.bfloat16):
    values = jax.random.normal(own_key, extent, jnp.float32) * scale
    if len(cuts) > 0:
        values = block_levels(own_key, extent, cuts, -0.22, 0.18) * values
    return jnp.clip(values, min=-most, max=most).astype(held_as)


def setup_inputs(seed: int = 0) -> dict:
    keys = jax.random.split(jax.random.key(seed), 8)
    return {
        "pressure_previous": bell_draw(keys[0], (NX, NY, NZ), 1.0, 6.0, ((0, 8), (1, 16)), jnp.float32),
        "pressure_current": bell_draw(keys[1], (NX, NY, NZ), 1.0, 6.0, ((0, 8), (1, 16)), jnp.float32),
        "adjoint_next": bell_draw(keys[2], (NX, NY, NZ), 1.0, 6.0, ((0, 8), (1, 16)), jnp.float32),
        "adjoint_current": bell_draw(keys[3], (NX, NY, NZ), 1.0, 6.0, ((0, 8), (1, 16)), jnp.float32),
        "inverse_modulus": jnp.clip(jnp.exp(math.log(2.0) - 1.3862944 * jax.random.uniform(keys[4], (NX, NY, NZ), jnp.float32) ** block_levels(keys[4], (NX, NY, NZ), ((0, 8), (1, 16)), -0.2, 0.2)), 0.5, 2.0),
        "inverse_density": jnp.clip(jnp.exp(math.log(2.0) - 1.3862944 * jax.random.uniform(keys[5], (NX, NY, NZ), jnp.float32) ** block_levels(keys[5], (NX, NY, NZ), ((0, 8), (1, 16)), -0.2, 0.2)), 0.5, 2.0),
        "face_mask": set_ends((jax.random.randint(keys[6], (6, NEX, NEY, EZD), 0, 3) < 1).astype(jnp.int32), jax.random.fold_in(keys[6], 1), 0, 1),
    }


TIME_STEP = 0.01
GLL_POINTS = (-1.0, -0.8717401485096066, -0.5917001814331423, -0.2092992179024789, 0.2092992179024789, 0.5917001814331423, 0.8717401485096066, 1.0)
GLL_WEIGHTS = (0.03571428571428571, 0.2107042271435061, 0.3411226924835044, 0.4124587946587038, 0.4124587946587038, 0.3411226924835044, 0.2107042271435061, 0.03571428571428571)


def gll_derivative():
    points = np.array(GLL_POINTS)
    previous_poly = np.ones(NODES)
    current_poly = points.copy()
    for degree in range(1, NODES - 1):
        next_poly = ((2 * degree + 1) * points * current_poly - degree * previous_poly) / (degree + 1)
        previous_poly, current_poly = current_poly, next_poly
    matrix = np.zeros((NODES, NODES))
    for row_index in range(NODES):
        for col_index in range(NODES):
            if row_index != col_index:
                matrix[row_index, col_index] = current_poly[row_index] / (current_poly[col_index] * (points[row_index] - points[col_index]))
    matrix[0, 0] = -NODES * (NODES - 1) / 4.0
    matrix[NODES - 1, NODES - 1] = NODES * (NODES - 1) / 4.0
    return matrix


def node_weights(length):
    return jnp.tile(jnp.asarray(GLL_WEIGHTS, jnp.float32), length // NODES)


def weight_cube(local_shape):
    return node_weights(local_shape[0])[:, None, None] * node_weights(local_shape[1])[None, :, None] * node_weights(local_shape[2])[None, None, :]


def spread(element_values):
    values = element_values.astype(jnp.float32)
    for direction in range(3):
        values = jnp.repeat(values, NODES, axis=direction)
    return values


def face_damping(face_mask, local_shape):
    weights_first = node_weights(local_shape[0])[:, None, None]
    weights_second = node_weights(local_shape[1])[None, :, None]
    weights_third = node_weights(local_shape[2])[None, None, :]
    place_first = (jnp.arange(local_shape[0]) % NODES)[:, None, None]
    place_second = (jnp.arange(local_shape[1]) % NODES)[None, :, None]
    place_third = (jnp.arange(local_shape[2]) % NODES)[None, None, :]
    factors = (
        (place_first == 0).astype(jnp.float32) * weights_second * weights_third,
        (place_first == NODES - 1).astype(jnp.float32) * weights_second * weights_third,
        (place_second == 0).astype(jnp.float32) * weights_first * weights_third,
        (place_second == NODES - 1).astype(jnp.float32) * weights_first * weights_third,
        (place_third == 0).astype(jnp.float32) * weights_first * weights_second,
        (place_third == NODES - 1).astype(jnp.float32) * weights_first * weights_second,
    )
    total = jnp.zeros(local_shape, jnp.float32)
    for face_index in range(6):
        total = total + spread(face_mask[face_index]) * factors[face_index]
    return total


def pair_sum(values, direction):
    length = values.shape[direction]
    zero_plane = jnp.zeros_like(lax.slice_in_dim(values, 0, 1, axis=direction))
    before = jnp.concatenate([zero_plane, lax.slice_in_dim(values, 0, length - 1, axis=direction)], axis=direction)
    following = jnp.concatenate([lax.slice_in_dim(values, 1, length, axis=direction), zero_plane], axis=direction)
    broadcast_shape = [1] * values.ndim
    broadcast_shape[direction] = length
    places = (jnp.arange(length) % NODES).reshape(broadcast_shape)
    return values + jnp.where(places == 0, before, 0.0) + jnp.where(places == NODES - 1, following, 0.0)


def assemble(values):
    for direction in range(3):
        values = pair_sum(values, direction)
    return values


def along_first(values, matrix):
    size_x, size_y, size_z = values.shape
    split = values.reshape(size_x // NODES, NODES, size_y, size_z)
    result = jnp.einsum("mn,anyz->amyz", matrix, split, precision=lax.Precision.HIGHEST)
    return result.reshape(values.shape)


def along_second(values, matrix):
    size_x, size_y, size_z = values.shape
    split = values.reshape(size_x, size_y // NODES, NODES, size_z)
    result = jnp.einsum("mn,xanz->xamz", matrix, split, precision=lax.Precision.HIGHEST)
    return result.reshape(values.shape)


def along_third(values, matrix):
    size_x, size_y, size_z = values.shape
    split = values.reshape(size_x, size_y, size_z // NODES, NODES)
    result = jnp.einsum("mn,xyan->xyam", matrix, split, precision=lax.Precision.HIGHEST)
    return result.reshape(values.shape)


def gradients(values, derivative):
    return along_first(values, derivative), along_second(values, derivative), along_third(values, derivative)


def transpose_sum(first, second, third, coefficient, derivative):
    return along_first(coefficient * first, derivative.T) + along_second(coefficient * second, derivative.T) + along_third(coefficient * third, derivative.T)


def advance(current, earlier, image, scale, rate):
    return 2.0 * current - earlier - scale * image - rate * (current - earlier)


def reference(pressure_previous, pressure_current, adjoint_next, adjoint_current, inverse_modulus, inverse_density, face_mask):
    local_shape = pressure_previous.shape
    derivative = jnp.asarray(gll_derivative(), jnp.float32)
    cube = weight_cube(local_shape)
    coefficient = inverse_density * cube
    multiplicity = assemble(jnp.ones(local_shape, jnp.float32))
    mass = assemble(inverse_modulus * cube)
    damping = assemble(face_damping(face_mask, local_shape))
    scale = TIME_STEP * TIME_STEP / mass
    rate = TIME_STEP * damping / mass
    later = assemble(adjoint_next) / multiplicity
    adjoint_states = {STEPS: assemble(adjoint_current) / multiplicity}
    for step_index in range(STEPS, 1, -1):
        current = adjoint_states[step_index]
        first, second, third = gradients(current, derivative)
        image = assemble(transpose_sum(first, second, third, coefficient, derivative))
        adjoint_states[step_index - 1] = advance(current, later, image, scale, rate)
        later = current
    earlier = assemble(pressure_previous) / multiplicity
    current = assemble(pressure_current) / multiplicity
    density_kernel = jnp.zeros(local_shape, jnp.float32)
    modulus_kernel = jnp.zeros(local_shape, jnp.float32)
    impedance_kernel = jnp.zeros(local_shape, jnp.float32)
    for step_index in range(1, STEPS + 1):
        first, second, third = gradients(current, derivative)
        image = assemble(transpose_sum(first, second, third, coefficient, derivative))
        following = advance(current, earlier, image, scale, rate)
        adjoint_now = adjoint_states[step_index]
        adj_first, adj_second, adj_third = gradients(adjoint_now, derivative)
        density_kernel = density_kernel + TIME_STEP * cube * (first * adj_first + second * adj_second + third * adj_third)
        modulus_kernel = modulus_kernel + adjoint_now * (following - 2.0 * current + earlier)
        impedance_kernel = impedance_kernel + rate * adjoint_now * (following - earlier)
        earlier, current = current, following
    return density_kernel, modulus_kernel, impedance_kernel
```

```python
import functools

import jax
import jax.numpy as jnp
import numpy as np
from jax import lax
from jax.experimental import pallas as pl
from jax.experimental.pallas import tpu as pltpu
from jax.sharding import PartitionSpec as P

MESH = pl.DeviceIdType.MESH
F32 = jnp.float32
BF16 = jnp.bfloat16
NODES = 8
STEPS = 8
LANES = 128
CHUNK = 2

TIME_STEP = 0.01
GLL_POINTS = (
    -1.0,
    -0.8717401485096066,
    -0.5917001814331423,
    -0.2092992179024789,
    0.2092992179024789,
    0.5917001814331423,
    0.8717401485096066,
    1.0,
)
GLL_WEIGHTS = (
    0.03571428571428571,
    0.2107042271435061,
    0.3411226924835044,
    0.4124587946587038,
    0.4124587946587038,
    0.3411226924835044,
    0.2107042271435061,
    0.03571428571428571,
)


def gll_derivative():
    points = np.array(GLL_POINTS)
    previous_poly = np.ones(NODES)
    current_poly = points.copy()
    for degree in range(1, NODES - 1):
        next_poly = ((2 * degree + 1) * points * current_poly - degree * previous_poly) / (
            degree + 1
        )
        previous_poly, current_poly = (current_poly, next_poly)
    matrix = np.zeros((NODES, NODES))
    for row_index in range(NODES):
        for col_index in range(NODES):
            if row_index != col_index:
                matrix[row_index, col_index] = current_poly[row_index] / (
                    current_poly[col_index] * (points[row_index] - points[col_index])
                )
    matrix[0, 0] = -NODES * (NODES - 1) / 4.0
    matrix[NODES - 1, NODES - 1] = NODES * (NODES - 1) / 4.0
    return matrix


DERIVATIVE = gll_derivative()


def halves(matrix):
    near, far = matrix[:4, :4], matrix[:4, 7:3:-1]
    return (near - far) / 2, (near + far) / 2


FORWARD = halves(DERIVATIVE)
BACKWARD = halves(DERIVATIVE.T)


def apply_eight(values, blocks):
    odd, even = blocks
    sums = [values[j] + values[7 - j] for j in range(4)]
    diffs = [values[j] - values[7 - j] for j in range(4)]
    low, high = [], []
    for i in range(4):
        a = diffs[0] * float(odd[i, 0])
        b = sums[0] * float(even[i, 0])
        for j in range(1, 4):
            a = a + diffs[j] * float(odd[i, j])
            b = b + sums[j] * float(even[i, j])
        low.append(a + b)
        high.append(a - b)
    return low + high[::-1]


def third_tables():
    count = LANES // NODES
    block = np.kron(np.eye(count), DERIVATIVE)
    assembly = np.eye(LANES)
    for k in range(1, count):
        assembly[8 * k, 8 * k - 1] = 1.0
        assembly[8 * k - 1, 8 * k] = 1.0
    tables = []
    for table in (block.T, block @ assembly):
        high = table.astype(BF16)
        low = (table - high.astype(np.float64)).astype(BF16)
        both = np.concatenate([high, low], axis=1)
        tables.append(np.concatenate([both, both], axis=0))
    return np.stack(tables)


def roll_sub(values, shift):
    shift %= 8
    return values if shift == 0 else pltpu.roll(values, shift, values.ndim - 2)


def kernel(
    shape_xy,
    up_ref,
    uc_ref,
    an_ref,
    ac_ref,
    im_ref,
    id_ref,
    fm_ref,
    tab_ref,
    dens_ref,
    mod_ref,
    imp_ref,
    nat,
    mask,
    table,
    cx,
    cy,
    cz,
    scale,
    keep,
    kx,
    ky,
    uf,
    vf,
    aa,
    va,
    gu,
    ga,
    acc,
    fx,
    fy,
    sp_x,
    sp_y,
    kn_x,
    kn_y,
    sums,
    xs0,
    ys0,
    ds0,
    xr0,
    yr0,
    dr0,
    xrk,
    yrk,
    xs,
    ys,
    ds,
    xr,
    yr,
    dr,
    in_sem,
    out_sem,
    send0,
    recv0,
    sendk,
    recvk,
    send,
    recv,
):
    count_x, count_y = shape_xy
    gx, gy = lax.axis_index("gx"), lax.axis_index("gy")

    in_x = {0: gx > 0, 1: gx < count_x - 1}
    in_y = {0: gy > 0, 1: gy < count_y - 1}
    other_x = gx + 1 - 2 * lax.rem(gx, 2)
    other_y = gy + 1 - 2 * lax.rem(gy, 2)

    def target_x(side):
        here = in_x[side]
        step = 2 * side - 1
        device = (jnp.where(here, gx + step, gx), jnp.where(here, gy, other_y))
        return device, jnp.where(here, 1 - side, side)

    def target_y(side):
        here = in_y[side]
        step = 2 * side - 1
        device = (jnp.where(here, gx, other_x), jnp.where(here, gy + step, gy))
        return device, jnp.where(here, 1 - side, side)

    def target_d(side_x, side_y):
        hx, hy = in_x[side_x], in_y[side_y]
        both_out = jnp.logical_not(jnp.logical_or(hx, hy))
        dx = jnp.where(both_out, count_x - 1 - gx, jnp.where(hx, gx + 2 * side_x - 1, gx))
        dy = jnp.where(hy, gy + 2 * side_y - 1, gy)
        slot_x = jnp.where(jnp.logical_or(hx, both_out), 1 - side_x, side_x)
        slot_y = jnp.where(hy, 1 - side_y, side_y)
        return (dx, dy), slot_x * 2 + slot_y

    targets_x = [target_x(0), target_x(1)]
    targets_y = [target_y(0), target_y(1)]
    targets_d = [target_d(0, 0), target_d(0, 1), target_d(1, 0), target_d(1, 1)]

    loads = []
    for k, ref in enumerate((id_ref, im_ref, uc_ref, up_ref, ac_ref, an_ref)):
        for half in range(2):
            loads.append(
                pltpu.make_async_copy(
                    ref.at[pl.ds(8 * half, 8)],
                    nat.at[k, :, pl.ds(32 * half, 32), :],
                    in_sem.at[2 * k + half],
                )
            )
    loads.append(pltpu.make_async_copy(fm_ref, mask, in_sem.at[12]))
    loads.append(pltpu.make_async_copy(tab_ref, table, in_sem.at[13]))
    for load in loads:
        load.start()
    barrier = pltpu.get_barrier_semaphore()
    for device, _ in targets_x + targets_y + targets_d:
        pl.semaphore_signal(barrier, inc=1, device_id=device, device_id_type=MESH)

    sub = lax.broadcasted_iota(jnp.int32, (8, LANES), 0)
    lane = lax.broadcasted_iota(jnp.int32, (8, LANES), 1)
    ey = sub % 4
    low_x = sub < 4
    zplace = lane % 8
    z_low = jnp.logical_and(zplace == 0, lane > 0)
    z_high = jnp.logical_and(zplace == 7, lane < LANES - 1)
    zero = jnp.zeros((8, LANES), F32)
    wz = zero
    for j in range(NODES):
        wz = jnp.where(zplace == j, F32(GLL_WEIGHTS[j]), wz)

    def one_if(flag):
        return jnp.where(flag, 1, 0)

    halo_x = [sub < 4 * one_if(in_x[0]), sub >= 8 - 4 * one_if(in_x[1])]
    halo_y = [ey < one_if(in_y[0]), ey >= 4 - one_if(in_y[1])]
    halo_d = [
        jnp.logical_and(halo_x[0], halo_y[0]),
        jnp.logical_and(halo_x[0], halo_y[1]),
        jnp.logical_and(halo_x[1], halo_y[0]),
        jnp.logical_and(halo_x[1], halo_y[1]),
    ]
    node_d = ((0, 0, 0, 1), (0, 7, 3, -1), (7, 0, 4, 1), (7, 7, 7, -1))

    def sum_third(values):
        before = pltpu.roll(values, 1, values.ndim - 1)
        after = pltpu.roll(values, LANES - 1, values.ndim - 1)
        return values + jnp.where(z_low, before, jnp.where(z_high, after, 0.0))

    def join_x(first, last):
        return (
            first + jnp.where(low_x, 0.0, roll_sub(last, 4)),
            last + jnp.where(low_x, roll_sub(first, 4), 0.0),
        )

    def join_y(first, last):
        return (
            first + jnp.where(ey == 0, 0.0, roll_sub(last, 1)),
            last + jnp.where(ey == 3, 0.0, roll_sub(first, 7)),
        )

    def pack_x(first, last):
        return (
            jnp.where(low_x, first[0:4], roll_sub(first[4:8], 4)),
            jnp.where(low_x, roll_sub(last[0:4], 4), last[4:8]),
        )

    def unpack_x(side, packed):
        turned = roll_sub(packed, 4)
        pair = [packed, turned] if side == 0 else [turned, packed]
        return jnp.concatenate(pair, axis=0)

    def pack_y(first, last):
        first = first.reshape(2, 4, 8, LANES)
        last = last.reshape(2, 4, 8, LANES)
        low, high = first[:, 0], roll_sub(last[:, 0], 5)
        for j in range(1, 4):
            low = jnp.where(ey == j, roll_sub(first[:, j], j), low)
            high = jnp.where(ey == j, roll_sub(last[:, j], 5 + j), high)
        return low, high

    def unpack_y(side, packed):
        rows = [roll_sub(packed, 3 * side - j) for j in range(4)]
        return jnp.stack(rows, axis=1).reshape(8, 8, LANES)

    def corner_lines(n00, n07, n70, n77):
        return jnp.where(low_x, jnp.where(ey == 0, n00, n07), jnp.where(ey == 0, n70, n77))

    def messages(src, dst, ssem, rsem):
        out = []
        for side in range(2):
            device, slot = targets_x[side]
            out.append((src[0].at[side], dst[0].at[slot], side, slot, device))
        for side in range(2):
            device, slot = targets_y[side]
            out.append((src[1].at[side], dst[1].at[slot], 2 + side, 2 + slot, device))
        if src[2] is not None:
            for k in range(4):
                device, slot = targets_d[k]
                out.append((src[2], dst[2].at[slot], 4 + k, 4 + slot, device))
        return [
            pltpu.make_async_remote_copy(
                src_ref=a,
                dst_ref=b,
                send_sem=ssem.at[i],
                recv_sem=rsem.at[j],
                device_id=device,
                device_id_type=MESH,
            )
            for a, b, i, j, device in out
        ]

    def arrive(src, dst, ssem, rsem):
        pairs = [(src[0].at[side], dst[0].at[side], side) for side in range(2)]
        pairs += [(src[1].at[side], dst[1].at[side], 2 + side) for side in range(2)]
        if src[2] is not None:
            pairs += [(src[2], dst[2].at[k], 4 + k) for k in range(4)]
        for a, b, i in pairs:
            copy = pltpu.make_async_remote_copy(
                src_ref=a,
                dst_ref=b,
                send_sem=ssem.at[i],
                recv_sem=rsem.at[i],
                device_id=targets_x[0][0],
                device_id_type=MESH,
            )
            copy.wait_recv()
            copy.wait_send()

    homes = (cz, scale, keep, uf, vf.at[1], aa.at[8], va)

    def natural(k, ix, iy):
        return nat[k, ix, pl.ds(iy, 8, stride=8), :]

    half_x = [jnp.where(jnp.logical_or(halo_x[0], jnp.logical_not(low_x)), 0.5, 1.0), 1.0]
    half_x_high = jnp.where(jnp.logical_or(halo_x[1], low_x), 0.5, 1.0)
    half_y_low = jnp.where(jnp.logical_or(halo_y[0], ey != 0), 0.5, 1.0)
    half_y_high = jnp.where(jnp.logical_or(halo_y[1], ey != 3), 0.5, 1.0)
    half_z = jnp.where(jnp.logical_or(z_low, z_high), 0.5, 1.0)

    def share(ix, iy):
        value = half_z
        if ix == 0:
            value = value * half_x[0]
        if ix == 7:
            value = value * half_x_high
        if iy == 0:
            value = value * half_y_low
        if iy == 7:
            value = value * half_y_high
        return value

    for load in loads[0:2]:
        load.wait()
    for ix in range(8):
        for iy in range(8):
            raw = natural(0, ix, iy) * (wz * float(GLL_WEIGHTS[ix] * GLL_WEIGHTS[iy]))
            summed = sum_third(raw)
            cz[ix, iy] = raw
            cx[ix, iy] = summed
            cy[ix, iy] = summed
    for load in loads[2:4]:
        load.wait()
    for ix in range(8):
        for iy in range(8):
            raw = natural(1, ix, iy) * (wz * float(GLL_WEIGHTS[ix] * GLL_WEIGHTS[iy]))
            scale[ix, iy] = sum_third(raw)
    loads[12].wait()
    loads[13].wait()
    spread = jnp.where(
        lax.broadcasted_iota(jnp.int32, (16, LANES), 1) // 8
        == lax.broadcasted_iota(jnp.int32, (16, LANES), 0),
        1.0,
        0.0,
    ).astype(F32)
    faces = []
    for f in range(6):
        cells = jnp.concatenate([mask[f, 0], mask[f, 1]], axis=0).astype(F32)
        faces.append(jnp.dot(cells, spread, preferred_element_type=F32))
    third_face = sum_third(jnp.where(zplace == 0, faces[4], jnp.where(zplace == 7, faces[5], 0.0)))
    faces = [sum_third(wz * face) for face in faces[:4]]
    for ix in range(8):
        for iy in range(8):
            value = third_face * float(GLL_WEIGHTS[ix] * GLL_WEIGHTS[iy])
            if ix == 0:
                value = value + faces[0] * float(GLL_WEIGHTS[iy])
            if ix == 7:
                value = value + faces[1] * float(GLL_WEIGHTS[iy])
            if iy == 0:
                value = value + faces[2] * float(GLL_WEIGHTS[ix])
            if iy == 7:
                value = value + faces[3] * float(GLL_WEIGHTS[ix])
            keep[ix, iy] = value
    for k in range(2, 6):
        for load in loads[2 * k : 2 * k + 2]:
            load.wait()
        home = homes[k + 1]
        for ix in range(8):
            for iy in range(8):
                home[ix, iy] = sum_third(natural(k, ix, iy) * share(ix, iy))

    def join_first(home):
        first, last = join_x(home[0], home[7])
        home[0] = first
        home[7] = last

    def join_second(home):
        first, last = join_y(home[:, 0], home[:, 7])
        home[:, 0] = first
        home[:, 7] = last

    for f, home in enumerate(homes):
        join_first(home)
        join_second(home)
        xs0[0, f], xs0[1, f] = pack_x(home[0], home[7])
        ys0[0, f], ys0[1, f] = pack_y(home[:, 0], home[:, 7])
        ds0[f] = corner_lines(home[0, 0], home[0, 7], home[7, 0], home[7, 7])
    join_first(cy)
    xs0[0, 7], xs0[1, 7] = pack_x(cy[0], cy[7])
    join_second(cx)
    ys0[0, 7], ys0[1, 7] = pack_y(cx[:, 0], cx[:, 7])

    pl.semaphore_wait(barrier, 8)
    for copy in messages((xs0, ys0, ds0), (xr0, yr0, dr0), send0, recv0):
        copy.start()
    arrive((xs0, ys0, ds0), (xr0, yr0, dr0), send0, recv0)

    def add_x(home, f):
        home[0] = home[0] + jnp.where(halo_x[0], unpack_x(0, xr0[0, f]), 0.0)
        home[7] = home[7] + jnp.where(halo_x[1], unpack_x(1, xr0[1, f]), 0.0)

    def add_y(home, f):
        home[:, 0] = home[:, 0] + jnp.where(halo_y[0], unpack_y(0, yr0[0, f]), 0.0)
        home[:, 7] = home[:, 7] + jnp.where(halo_y[1], unpack_y(1, yr0[1, f]), 0.0)

    for f, home in enumerate(homes):
        add_x(home, f)
        add_y(home, f)
        for k, (ix, iy, _, turn) in enumerate(node_d):
            home[ix, iy] = home[ix, iy] + jnp.where(halo_d[k], roll_sub(dr0[k, f], turn), 0.0)
    add_x(cy, 7)
    add_y(cx, 7)

    for ix in range(8):
        mass = scale[ix]
        one_over = 1.0 / mass
        scale[ix] = (TIME_STEP * TIME_STEP) * one_over
        keep[ix] = 1.0 - TIME_STEP * keep[ix] * one_over
        vf[1, ix] = uf[ix] - vf[1, ix]
        va[ix] = aa[8, ix] - va[ix]

    end_x = [
        jnp.where(low_x, F32(DERIVATIVE[i, 0]), F32(DERIVATIVE[i, 7])) for i in range(8)
    ]
    end_y = [
        jnp.where(ey < 2, F32(DERIVATIVE[i, 0]), F32(DERIVATIVE[i, 7])) for i in range(8)
    ]
    for c in range(0, 8, CHUNK):
        here = slice(c, c + CHUNK)
        rows = apply_eight([end_x[i] * cx[i, here] for i in range(8)], BACKWARD)
        for j in range(8):
            kx[j, here] = rows[j]
        rows = apply_eight([end_y[i] * cy[here, i] for i in range(8)], BACKWARD)
        for j in range(8):
            ky[here, j] = rows[j]
    fx[0], fx[1] = kx[0], kx[7]
    fy[0], fy[1] = ky[:, 0], ky[:, 7]

    def put_faces(side_x, side_y, fx0, fx1, fy0, fy1):
        side_x[0], side_x[1] = pack_x(fx0, fx1)
        side_y[0], side_y[1] = pack_y(fy0, fy1)

    xsk, ysk = xs0.at[:, 0], ys0.at[:, 0]
    put_faces(xsk, ysk, fx[0], fx[1], fy[0], fy[1])
    for copy in messages((xsk, ysk, None), (xrk, yrk, None), sendk, recvk):
        copy.start()

    def third(source, gradient):
        def times(values, which):
            high = values.astype(BF16)
            low = (values - high.astype(F32)).astype(BF16)
            both = jnp.dot(
                jnp.concatenate([high, low], axis=1), table[which], preferred_element_type=F32
            )
            return both[:, :LANES] + both[:, LANES:]

        slope = times(source[...].reshape(512, LANES), 0)
        gradient[2] = slope.reshape(8, 8, 8, LANES)
        if acc is not None:
            flux = cz[...].reshape(512, LANES) * slope
            acc[...] = times(flux, 1).reshape(8, 8, 8, LANES)

    def first_part(source, gradient, halos):
        for c in range(0, 8, CHUNK):
            here = slice(c, c + CHUNK)
            slopes = apply_eight([source[j, here] for j in range(8)], FORWARD)
            for j in range(8):
                gradient[0, j, here] = slopes[j]
            image = apply_eight([cx[j, here] * slopes[j] for j in range(8)], BACKWARD)
            if halos is None:
                fx[0, here], fx[1, here] = image[0], image[7]
            image[0], image[7] = join_x(image[0], image[7])
            if halos is not None:
                image[0] = image[0] + halos[0][here]
                image[7] = image[7] + halos[1][here]
            for j in range(8):
                acc[j, here] = acc[j, here] + image[j]

    def second_part(source, gradient, halos, v_from, u_to, v_to):
        for c in range(0, 8, CHUNK):
            here = slice(c, c + CHUNK)
            now = [source[here, j] for j in range(8)]
            slopes = apply_eight(now, FORWARD)
            for j in range(8):
                gradient[1, here, j] = slopes[j]
            image = apply_eight([cy[here, j] * slopes[j] for j in range(8)], BACKWARD)
            if halos is None:
                fy[0, here], fy[1, here] = image[0], image[7]
            image[0], image[7] = join_y(image[0], image[7])
            if halos is not None:
                image[0] = image[0] + halos[0][here]
                image[7] = image[7] + halos[1][here]
            for j in range(8):
                change = keep[here, j] * v_from[here, j] - scale[here, j] * (acc[here, j] + image[j])
                v_to[here, j] = change
                u_to[here, j] = now[j] + change

    def begin(field, turn, source, gradient, v_from, u_to, v_to):
        slot = lax.rem(turn, 2)
        third(source, gradient)
        first_part(source, gradient, None)
        second_part(source, gradient, None, v_from, u_to, v_to)
        own_x = [fx[0], fx[1]]
        own_y = [fy[0], fy[1]]
        to_x, to_y, to_d = xs.at[field, slot], ys.at[field, slot], ds.at[field, slot]
        put_faces(to_x.at[:, 0], to_y.at[:, 0], own_x[0], own_x[1], own_y[0], own_y[1])
        next_x = kx[0] * u_to[0]
        next_y = ky[:, 0] * u_to[:, 0]
        for j in range(1, 8):
            next_x = next_x + kx[j] * u_to[j]
            next_y = next_y + ky[:, j] * u_to[:, j]
        put_faces(to_x.at[:, 1], to_y.at[:, 1], next_x, next_x, next_y, next_y)
        for side, node in ((0, 0), (1, 7)):
            sp_x[field, side] = scale[node] * own_x[side]
            sp_y[field, side] = scale[:, node] * own_y[side]
        along_x = [jnp.sum(kx[:, n] * sp_y[field, s], axis=0) for s, n in ((0, 0), (1, 7))]
        along_y = [jnp.sum(ky[n] * sp_x[field, s], axis=0) for s, n in ((0, 0), (1, 7))]
        to_d[...] = -(
            jnp.where(ey == 0, along_x[0], along_x[1]) + jnp.where(low_x, along_y[0], along_y[1])
        )
        for copy in messages(
            (to_x, to_y, to_d),
            (xr.at[field, slot], yr.at[field, slot], dr.at[field, slot]),
            send.at[field, slot],
            recv.at[field, slot],
        ):
            copy.start()

    def complete(field, turn, u, v):
        slot = lax.rem(turn, 2)
        from_x, from_y, from_d = xr.at[field, slot], yr.at[field, slot], dr.at[field, slot]
        arrive(
            (xs.at[field, slot], ys.at[field, slot], ds.at[field, slot]),
            (from_x, from_y, from_d),
            send.at[field, slot],
            recv.at[field, slot],
        )
        for side, node in ((0, 0), (1, 7)):
            part = scale[node] * jnp.where(halo_x[side], unpack_x(side, from_x[side, 0]), 0.0)
            u[node] = u[node] - part
            v[node] = v[node] - part
        for side, node in ((0, 0), (1, 7)):
            part = scale[:, node] * jnp.where(halo_y[side], unpack_y(side, from_y[side, 0]), 0.0)
            u[:, node] = u[:, node] - part
            v[:, node] = v[:, node] - part
        return from_x, from_y, from_d

    def finish(field, arrived, source, gradient, v_from, u_to, v_to):
        from_x, from_y, from_d = arrived
        third(source, gradient)
        halos_x, halos_y = [], []
        for side in range(2):
            part = unpack_x(side, from_x[side, 1]) - kn_x[side] * sp_x[field, side]
            halos_x.append(jnp.where(halo_x[side], part, 0.0))
            part = unpack_y(side, from_y[side, 1]) - kn_y[side] * sp_y[field, side]
            halos_y.append(jnp.where(halo_y[side], part, 0.0))
        first_part(source, gradient, halos_x)
        for k, (ix, iy, _, turn) in enumerate(node_d):
            acc[ix, iy] = acc[ix, iy] + jnp.where(halo_d[k], roll_sub(from_d[k], turn), 0.0)
        second_part(source, gradient, halos_y, v_from, u_to, v_to)

    def begin_u(turn):
        n = 2 * turn + 1
        begin(0, turn, uf, gu.at[n], vf.at[n], uf, vf.at[n + 1])

    def begin_a(turn):
        n = 8 - 2 * turn
        begin(1, turn, aa.at[n], ga.at[n], va, aa.at[n - 1], va)

    def finish_u(turn):
        n = 2 * turn + 2
        arrived = complete(0, turn, uf, vf.at[n])
        finish(0, arrived, uf, gu.at[n], vf.at[n], uf, vf.at[n + 1])

    def finish_a(turn):
        n = 7 - 2 * turn
        arrived = complete(1, turn, aa.at[n], va)
        finish(1, arrived, aa.at[n], ga.at[n], va, aa.at[n - 1], va)

    begin_u(0)
    begin_a(0)
    arrive((xsk, ysk, None), (xrk, yrk, None), sendk, recvk)
    for side in range(2):
        kn_x[side] = unpack_x(side, xrk[side])
        kn_y[side] = unpack_y(side, yrk[side])

    def cycle(turn, carry):
        finish_u(turn)
        begin_u(turn + 1)
        finish_a(turn)
        begin_a(turn + 1)
        return carry

    lax.fori_loop(0, STEPS // 2 - 1, cycle, 0)

    def density_of(ns, ix):
        total = None
        for n in ns:
            for d in range(3):
                term = gu[n, d, ix] * ga[n, d, ix]
                total = term if total is None else total + term
        return total

    def moduli_of(ns, ix):
        modulus, impedance = None, None
        for n in ns:
            now, before, after = aa[n, ix], vf[n, ix], vf[n + 1, ix]
            a, b = now * (after - before), now * (after + before)
            modulus = a if modulus is None else modulus + a
            impedance = b if impedance is None else impedance + b
        return modulus, impedance

    for ix in range(8):
        sums[0, ix] = density_of(range(2, 8), ix)
        sums[1, ix], sums[2, ix] = moduli_of(range(2, 7), ix)

    last = STEPS // 2 - 1
    finish_u(last)
    complete(1, last, aa.at[1], va)
    source, gradient = aa.at[1], ga.at[1]
    high = source[...].reshape(512, LANES).astype(BF16)
    low = (source[...].reshape(512, LANES) - high.astype(F32)).astype(BF16)
    both = jnp.dot(jnp.concatenate([high, low], axis=1), table[0], preferred_element_type=F32)
    gradient[2] = (both[:, :LANES] + both[:, LANES:]).reshape(8, 8, 8, LANES)
    for c in range(0, 8, CHUNK):
        here = slice(c, c + CHUNK)
        slopes = apply_eight([source[j, here] for j in range(8)], FORWARD)
        for j in range(8):
            gradient[0, j, here] = slopes[j]
        slopes = apply_eight([source[here, j] for j in range(8)], FORWARD)
        for j in range(8):
            gradient[1, here, j] = slopes[j]

    for ix in range(8):
        density = sums[0, ix] + density_of((1, 8), ix)
        modulus, impedance = moduli_of((1, 7, 8), ix)
        modulus = sums[1, ix] + modulus
        impedance = (sums[2, ix] + impedance) * (1.0 - keep[ix])
        for iy in range(8):
            weight = wz * float(TIME_STEP * GLL_WEIGHTS[ix] * GLL_WEIGHTS[iy])
            rows = pl.ds(iy, 8, stride=8)
            nat[0, ix, rows, :] = weight * density[iy]
            nat[1, ix, rows, :] = modulus[iy]
            nat[2, ix, rows, :] = impedance[iy]
    stores = []
    for k, ref in enumerate((dens_ref, mod_ref, imp_ref)):
        for half in range(2):
            stores.append(
                pltpu.make_async_copy(
                    nat.at[k, :, pl.ds(32 * half, 32), :],
                    ref.at[pl.ds(8 * half, 8)],
                    out_sem.at[2 * k + half],
                )
            )
    for store in stores:
        store.start()
    for store in stores:
        store.wait()


def field(*lead):
    return pltpu.VMEM((*lead, 8, 8, 8, LANES), F32)


def per_device(shape_xy, *args):
    local = args[0].shape
    out = jax.ShapeDtypeStruct(local, F32)
    tables = jnp.asarray(third_tables())
    any_spec = pl.BlockSpec(memory_space=pl.ANY)
    vectors = lambda *lead: pltpu.VMEM((*lead, 8, LANES), F32)
    return pl.pallas_call(
        functools.partial(kernel, shape_xy),
        out_shape=(out, out, out),
        in_specs=[any_spec] * 8,
        out_specs=(any_spec,) * 3,
        scratch_shapes=[
            pltpu.VMEM((6, 8, 64, LANES), F32),
            pltpu.VMEM(args[6].shape, jnp.int32),
            pltpu.VMEM(tables.shape, BF16),
            field(),
            field(),
            field(),
            field(),
            field(),
            field(),
            field(),
            field(),
            field(10),
            field(9),
            field(),
            field(9, 3),
            field(9, 3),
            field(),
            vectors(2, 8),
            vectors(2, 8),
            vectors(2, 2, 8),
            vectors(2, 2, 8),
            vectors(2, 8),
            vectors(2, 8),
            field(3),
            vectors(2, 8, 4),
            vectors(2, 8, 2),
            vectors(7),
            vectors(2, 8, 4),
            vectors(2, 8, 2),
            vectors(4, 7),
            vectors(2, 4),
            vectors(2, 2),
            vectors(2, 2, 2, 2, 4),
            vectors(2, 2, 2, 2, 2),
            vectors(2, 2),
            vectors(2, 2, 2, 2, 4),
            vectors(2, 2, 2, 2, 2),
            vectors(2, 2, 4),
            pltpu.SemaphoreType.DMA((14,)),
            pltpu.SemaphoreType.DMA((6,)),
            pltpu.SemaphoreType.DMA((8,)),
            pltpu.SemaphoreType.DMA((8,)),
            pltpu.SemaphoreType.DMA((4,)),
            pltpu.SemaphoreType.DMA((4,)),
            pltpu.SemaphoreType.DMA((2, 2, 8)),
            pltpu.SemaphoreType.DMA((2, 2, 8)),
        ],
        compiler_params=pltpu.CompilerParams(
            collective_id=0, has_side_effects=True, vmem_limit_bytes=48 * 1024 * 1024
        ),
    )(*args, tables)


def solution(mesh):
    shape_xy = (mesh.shape["gx"], mesh.shape["gy"])
    in_specs = (P("gx", "gy", None),) * 6 + (P(None, "gx", "gy", None),)
    out_specs = (P("gx", "gy", None),) * 3
    return jax.shard_map(
        functools.partial(per_device, shape_xy),
        mesh=mesh,
        in_specs=in_specs,
        out_specs=out_specs,
        check_vma=False,
    )
```

```python
import functools

import jax
import jax.numpy as jnp
import numpy as np
from jax import lax
from jax.experimental import pallas as pl
from jax.experimental.pallas import tpu as pltpu
from jax.sharding import PartitionSpec as P

MESH = pl.DeviceIdType.MESH
F32 = jnp.float32
BF16 = jnp.bfloat16
NODES = 8
STEPS = 8
LANES = 128
CHUNK = 2

TIME_STEP = 0.01
GLL_POINTS = (
    -1.0,
    -0.8717401485096066,
    -0.5917001814331423,
    -0.2092992179024789,
    0.2092992179024789,
    0.5917001814331423,
    0.8717401485096066,
    1.0,
)
GLL_WEIGHTS = (
    0.03571428571428571,
    0.2107042271435061,
    0.3411226924835044,
    0.4124587946587038,
    0.4124587946587038,
    0.3411226924835044,
    0.2107042271435061,
    0.03571428571428571,
)


def gll_derivative():
    points = np.array(GLL_POINTS)
    previous_poly = np.ones(NODES)
    current_poly = points.copy()
    for degree in range(1, NODES - 1):
        next_poly = ((2 * degree + 1) * points * current_poly - degree * previous_poly) / (
            degree + 1
        )
        previous_poly, current_poly = (current_poly, next_poly)
    matrix = np.zeros((NODES, NODES))
    for row_index in range(NODES):
        for col_index in range(NODES):
            if row_index != col_index:
                matrix[row_index, col_index] = current_poly[row_index] / (
                    current_poly[col_index] * (points[row_index] - points[col_index])
                )
    matrix[0, 0] = -NODES * (NODES - 1) / 4.0
    matrix[NODES - 1, NODES - 1] = NODES * (NODES - 1) / 4.0
    return matrix


DERIVATIVE = gll_derivative()


def halves(matrix):
    near, far = matrix[:4, :4], matrix[:4, 7:3:-1]
    return (near - far) / 2, (near + far) / 2


FORWARD = halves(DERIVATIVE)
BACKWARD = halves(DERIVATIVE.T)


def apply_eight(values, blocks):
    odd, even = blocks
    sums = [values[j] + values[7 - j] for j in range(4)]
    diffs = [values[j] - values[7 - j] for j in range(4)]
    low, high = [], []
    for i in range(4):
        a = diffs[0] * float(odd[i, 0])
        b = sums[0] * float(even[i, 0])
        for j in range(1, 4):
            a = a + diffs[j] * float(odd[i, j])
            b = b + sums[j] * float(even[i, j])
        low.append(a + b)
        high.append(a - b)
    return low + high[::-1]


def roll_sub(values, shift):
    shift %= 8
    return values if shift == 0 else pltpu.roll(values, shift, values.ndim - 2)


def kernel(
    shape_xy,
    up_ref,
    uc_ref,
    an_ref,
    ac_ref,
    im_ref,
    id_ref,
    fm_ref,
    dens_ref,
    mod_ref,
    imp_ref,
    nat,
    mask,
    table,
    cx,
    cy,
    cz,
    scale,
    keep,
    kx,
    ky,
    uf,
    vf,
    aa,
    va,
    gu,
    ga,
    acc,
    sp_x,
    sp_y,
    kn_x,
    kn_y,
    sums,
    xs0,
    ys0,
    ds0,
    xs1,
    ys1,
    xr0,
    yr0,
    dr0,
    xr1,
    yr1,
    xrk,
    yrk,
    xs,
    ys,
    ds,
    xr,
    yr,
    dr,
    in_sem,
    send0,
    recv0,
    sendk,
    recvk,
    send,
    recv,
):
    count_x, count_y = shape_xy
    gx, gy = lax.axis_index("gx"), lax.axis_index("gy")

    in_x = {0: gx > 0, 1: gx < count_x - 1}
    in_y = {0: gy > 0, 1: gy < count_y - 1}
    other_x = gx + 1 - 2 * lax.rem(gx, 2)
    other_y = gy + 1 - 2 * lax.rem(gy, 2)

    def target_x(side):
        here = in_x[side]
        step = 2 * side - 1
        device = (jnp.where(here, gx + step, gx), jnp.where(here, gy, other_y))
        return device, jnp.where(here, 1 - side, side)

    def target_y(side):
        here = in_y[side]
        step = 2 * side - 1
        device = (jnp.where(here, gx, other_x), jnp.where(here, gy + step, gy))
        return device, jnp.where(here, 1 - side, side)

    def target_d(side_x, side_y):
        hx, hy = in_x[side_x], in_y[side_y]
        both_out = jnp.logical_not(jnp.logical_or(hx, hy))
        dx = jnp.where(both_out, count_x - 1 - gx, jnp.where(hx, gx + 2 * side_x - 1, gx))
        dy = jnp.where(hy, gy + 2 * side_y - 1, gy)
        slot_x = jnp.where(jnp.logical_or(hx, both_out), 1 - side_x, side_x)
        slot_y = jnp.where(hy, 1 - side_y, side_y)
        return (dx, dy), slot_x * 2 + slot_y

    targets_x = [target_x(0), target_x(1)]
    targets_y = [target_y(0), target_y(1)]
    targets_d = [target_d(0, 0), target_d(0, 1), target_d(1, 0), target_d(1, 1)]

    loads = []
    for k, ref in enumerate((id_ref, im_ref, uc_ref, up_ref, ac_ref, an_ref)):
        for half in range(2):
            loads.append(
                pltpu.make_async_copy(
                    ref.at[pl.ds(8 * half, 8)],
                    nat.at[k, :, pl.ds(32 * half, 32), :],
                    in_sem.at[2 * k + half],
                )
            )
    loads.append(pltpu.make_async_copy(fm_ref, mask, in_sem.at[12]))
    for load in loads:
        load.start()
    barrier = pltpu.get_barrier_semaphore()
    for device, _ in targets_x + targets_y + targets_d:
        pl.semaphore_signal(barrier, inc=1, device_id=device, device_id_type=MESH)

    sub = lax.broadcasted_iota(jnp.int32, (8, LANES), 0)
    lane = lax.broadcasted_iota(jnp.int32, (8, LANES), 1)
    ey = sub % 4
    low_x = sub < 4
    zplace = lane % 8
    z_low = jnp.logical_and(zplace == 0, lane > 0)
    z_high = jnp.logical_and(zplace == 7, lane < LANES - 1)
    zero = jnp.zeros((8, LANES), F32)
    wz = zero
    for j in range(NODES):
        wz = jnp.where(zplace == j, F32(GLL_WEIGHTS[j]), wz)

    def sum_third(values):
        before = pltpu.roll(values, 1, values.ndim - 1)
        after = pltpu.roll(values, LANES - 1, values.ndim - 1)
        return values + jnp.where(z_low, before, jnp.where(z_high, after, 0.0))

    tiles = [zero, zero]
    for i in range(8):
        for j in range(8):
            value = F32(DERIVATIVE[i, j])
            tiles[0] = jnp.where(jnp.logical_and(sub == j, zplace == i), value, tiles[0])
            tiles[1] = jnp.where(jnp.logical_and(sub == i, zplace == j), value, tiles[1])
    for which in range(2):
        rows = [jnp.where(lane // 8 == k, tiles[which], 0.0) for k in range(LANES // 8)]
        if which == 1:
            rows = [sum_third(row) for row in rows]
        block = jnp.concatenate(rows, axis=0)
        high = block.astype(BF16)
        low = (block - high.astype(F32)).astype(BF16)
        for half in range(2):
            here = slice(LANES * half, LANES * half + LANES)
            table[which, here, :LANES] = high
            table[which, here, LANES:] = low

    def one_if(flag):
        return jnp.where(flag, 1, 0)

    halo_x = [sub < 4 * one_if(in_x[0]), sub >= 8 - 4 * one_if(in_x[1])]
    halo_y = [ey < one_if(in_y[0]), ey >= 4 - one_if(in_y[1])]
    halo_d = [
        jnp.logical_and(halo_x[0], halo_y[0]),
        jnp.logical_and(halo_x[0], halo_y[1]),
        jnp.logical_and(halo_x[1], halo_y[0]),
        jnp.logical_and(halo_x[1], halo_y[1]),
    ]
    node_d = ((0, 0, 0, 1), (0, 7, 3, -1), (7, 0, 4, 1), (7, 7, 7, -1))

    def join_x(first, last):
        return (
            first + jnp.where(low_x, 0.0, roll_sub(last, 4)),
            last + jnp.where(low_x, roll_sub(first, 4), 0.0),
        )

    def join_y(first, last):
        return (
            first + jnp.where(ey == 0, 0.0, roll_sub(last, 1)),
            last + jnp.where(ey == 3, 0.0, roll_sub(first, 7)),
        )

    def pack_x(first, last):
        return (
            jnp.where(low_x, first[0:4], roll_sub(first[4:8], 4)),
            jnp.where(low_x, roll_sub(last[0:4], 4), last[4:8]),
        )

    def unpack_x(side, packed):
        turned = roll_sub(packed, 4)
        pair = [packed, turned] if side == 0 else [turned, packed]
        return jnp.concatenate(pair, axis=0)

    def pack_y(first, last):
        first = first.reshape(2, 4, 8, LANES)
        last = last.reshape(2, 4, 8, LANES)
        low, high = first[:, 0], roll_sub(last[:, 0], 5)
        for j in range(1, 4):
            low = jnp.where(ey == j, roll_sub(first[:, j], j), low)
            high = jnp.where(ey == j, roll_sub(last[:, j], 5 + j), high)
        return low, high

    def unpack_y(side, packed):
        rows = [roll_sub(packed, 3 * side - j) for j in range(4)]
        return jnp.stack(rows, axis=1).reshape(8, 8, LANES)

    def corner_lines(n00, n07, n70, n77):
        return jnp.where(low_x, jnp.where(ey == 0, n00, n07), jnp.where(ey == 0, n70, n77))

    def copies(src, dst, ssem, rsem, first):
        out = []
        for side in range(2):
            device, slot = targets_x[side]
            out.append((src[0].at[side], dst[0].at[slot], side, slot, device))
        for side in range(2):
            device, slot = targets_y[side]
            out.append((src[1].at[side], dst[1].at[slot], 2 + side, 2 + slot, device))
        if len(src) > 2:
            for k in range(4):
                device, slot = targets_d[k]
                out.append((src[2], dst[2].at[slot], 4 + k, 4 + slot, device))
        for a, b, i, j, device in out:
            pltpu.make_async_remote_copy(
                src_ref=a,
                dst_ref=b,
                send_sem=ssem.at[first + i],
                recv_sem=rsem.at[first + j],
                device_id=device,
                device_id_type=MESH,
            ).start()

    def arrive(src, dst, ssem, rsem, first, which=range(8)):
        pairs = [(src[0].at[side], dst[0].at[side]) for side in range(2)]
        pairs += [(src[1].at[side], dst[1].at[side]) for side in range(2)]
        if len(src) > 2:
            pairs += [(src[2], dst[2].at[k]) for k in range(4)]
        for i, (a, b) in enumerate(pairs):
            if i in which:
                copy = pltpu.make_async_remote_copy(
                    src_ref=a,
                    dst_ref=b,
                    send_sem=ssem.at[first + i],
                    recv_sem=rsem.at[first + i],
                    device_id=targets_x[0][0],
                    device_id_type=MESH,
                )
                copy.wait_recv()
                copy.wait_send()

    homes = (cz, scale, keep, uf, vf.at[1], aa.at[8], va)
    groups = ((0, 1, 2), (3, 4), (5, 6))

    def natural(k, ix, iy):
        return nat[k, ix, pl.ds(iy, 8, stride=8), :]

    half_x = [jnp.where(jnp.logical_or(halo_x[0], jnp.logical_not(low_x)), 0.5, 1.0), 1.0]
    half_x_high = jnp.where(jnp.logical_or(halo_x[1], low_x), 0.5, 1.0)
    half_y_low = jnp.where(jnp.logical_or(halo_y[0], ey != 0), 0.5, 1.0)
    half_y_high = jnp.where(jnp.logical_or(halo_y[1], ey != 3), 0.5, 1.0)
    half_z = jnp.where(jnp.logical_or(z_low, z_high), 0.5, 1.0)

    def share(ix, iy):
        value = half_z
        if ix == 0:
            value = value * half_x[0]
        if ix == 7:
            value = value * half_x_high
        if iy == 0:
            value = value * half_y_low
        if iy == 7:
            value = value * half_y_high
        return value

    for load in loads[0:2]:
        load.wait()
    for ix in range(8):
        for iy in range(8):
            raw = natural(0, ix, iy) * (wz * float(GLL_WEIGHTS[ix] * GLL_WEIGHTS[iy]))
            summed = sum_third(raw)
            cz[ix, iy] = raw
            cx[ix, iy] = summed
            cy[ix, iy] = summed
    for load in loads[2:4]:
        load.wait()
    for ix in range(8):
        for iy in range(8):
            raw = natural(1, ix, iy) * (wz * float(GLL_WEIGHTS[ix] * GLL_WEIGHTS[iy]))
            scale[ix, iy] = sum_third(raw)
    loads[12].wait()
    spread = jnp.where(
        lax.broadcasted_iota(jnp.int32, (16, LANES), 1) // 8
        == lax.broadcasted_iota(jnp.int32, (16, LANES), 0),
        1.0,
        0.0,
    ).astype(F32)
    faces = []
    for f in range(6):
        cells = jnp.concatenate([mask[f, 0], mask[f, 1]], axis=0).astype(F32)
        faces.append(jnp.dot(cells, spread, preferred_element_type=F32))
    third_face = sum_third(jnp.where(zplace == 0, faces[4], jnp.where(zplace == 7, faces[5], 0.0)))
    faces = [sum_third(wz * face) for face in faces[:4]]
    for ix in range(8):
        for iy in range(8):
            value = third_face * float(GLL_WEIGHTS[ix] * GLL_WEIGHTS[iy])
            if ix == 0:
                value = value + faces[0] * float(GLL_WEIGHTS[iy])
            if ix == 7:
                value = value + faces[1] * float(GLL_WEIGHTS[iy])
            if iy == 0:
                value = value + faces[2] * float(GLL_WEIGHTS[ix])
            if iy == 7:
                value = value + faces[3] * float(GLL_WEIGHTS[ix])
            keep[ix, iy] = value
    def join_first(home):
        first, last = join_x(home[0], home[7])
        home[0] = first
        home[7] = last

    def join_second(home):
        first, last = join_y(home[:, 0], home[:, 7])
        home[:, 0] = first
        home[:, 7] = last

    def pack_field(f):
        home = homes[f]
        join_first(home)
        join_second(home)
        xs0[0, f], xs0[1, f] = pack_x(home[0], home[7])
        ys0[0, f], ys0[1, f] = pack_y(home[:, 0], home[:, 7])
        ds0[f] = corner_lines(home[0, 0], home[0, 7], home[7, 0], home[7, 7])

    def group_refs(g):
        here = pl.ds(groups[g][0], len(groups[g]))
        src = (xs0.at[:, here], ys0.at[:, here], ds0.at[here])
        dst = (xr0.at[:, here], yr0.at[:, here], dr0.at[:, here])
        return src, dst, send0, recv0, 8 * g

    for f in groups[0]:
        pack_field(f)
    join_first(cy)
    join_second(cx)
    one_sided = ((xs1, ys1), (xr1, yr1), send0, recv0, 24)
    xs1[0], xs1[1] = pack_x(cy[0], cy[7])
    ys1[0], ys1[1] = pack_y(cx[:, 0], cx[:, 7])
    pl.semaphore_wait(barrier, 8)
    copies(*one_sided)
    copies(*group_refs(0))

    for g in (1, 2):
        for f in groups[g]:
            k = f - 1
            for load in loads[2 * k : 2 * k + 2]:
                load.wait()
            home = homes[f]
            for ix in range(8):
                for iy in range(8):
                    home[ix, iy] = sum_third(natural(k, ix, iy) * share(ix, iy))
            pack_field(f)
        copies(*group_refs(g))

    def add_x(home, received):
        for side, node in ((0, 0), (1, 7)):
            home[node] = home[node] + jnp.where(halo_x[side], unpack_x(side, received[side]), 0.0)

    def add_y(home, received):
        for side, node in ((0, 0), (1, 7)):
            part = jnp.where(halo_y[side], unpack_y(side, received[side]), 0.0)
            home[:, node] = home[:, node] + part

    def add_field(f):
        home = homes[f]
        add_x(home, xr0.at[:, f])
        add_y(home, yr0.at[:, f])
        for k, (ix, iy, _, turn) in enumerate(node_d):
            home[ix, iy] = home[ix, iy] + jnp.where(halo_d[k], roll_sub(dr0[k, f], turn), 0.0)

    arrive(*one_sided)
    add_x(cy, xr1)
    add_y(cx, yr1)

    end_x = [
        jnp.where(low_x, F32(DERIVATIVE[i, 0]), F32(DERIVATIVE[i, 7])) for i in range(8)
    ]
    end_y = [
        jnp.where(ey < 2, F32(DERIVATIVE[i, 0]), F32(DERIVATIVE[i, 7])) for i in range(8)
    ]
    for c in range(0, 8, CHUNK):
        here = slice(c, c + CHUNK)
        rows = apply_eight([end_x[i] * cx[i, here] for i in range(8)], BACKWARD)
        for j in range(8):
            kx[j, here] = rows[j]
        rows = apply_eight([end_y[i] * cy[here, i] for i in range(8)], BACKWARD)
        for j in range(8):
            ky[here, j] = rows[j]
    def put_faces(side_x, side_y, fx0, fx1, fy0, fy1):
        side_x[0], side_x[1] = pack_x(fx0, fx1)
        side_y[0], side_y[1] = pack_y(fy0, fy1)

    ends = ((xs1, ys1), (xrk, yrk), sendk, recvk, 0)
    put_faces(xs1, ys1, kx[0], kx[7], ky[:, 0], ky[:, 7])
    copies(*ends)
    arrive(*group_refs(0))
    for f in groups[0]:
        add_field(f)
    for ix in range(8):
        one_over = 1.0 / scale[ix]
        scale[ix] = (TIME_STEP * TIME_STEP) * one_over
        keep[ix] = 1.0 - TIME_STEP * keep[ix] * one_over
    arrive(*group_refs(1))
    for f in groups[1]:
        add_field(f)
    for ix in range(8):
        vf[1, ix] = uf[ix] - vf[1, ix]

    def times(values, which):
        high = values.astype(BF16)
        low = (values - high.astype(F32)).astype(BF16)
        both = jnp.dot(
            jnp.concatenate([high, low], axis=1), table[which], preferred_element_type=F32
        )
        return both[:, :LANES] + both[:, LANES:]

    def advance(source, gradient, v_from, u_to, v_to):
        slope = times(source[...].reshape(512, LANES), 0)
        gradient[2] = slope.reshape(8, 8, 8, LANES)
        acc[...] = times(cz[...].reshape(512, LANES) * slope, 1).reshape(8, 8, 8, LANES)
        for c in range(0, 8, CHUNK):
            here = slice(c, c + CHUNK)
            slopes = apply_eight([source[j, here] for j in range(8)], FORWARD)
            for j in range(8):
                gradient[0, j, here] = slopes[j]
            image = apply_eight([cx[j, here] * slopes[j] for j in range(8)], BACKWARD)
            image[0], image[7] = join_x(image[0], image[7])
            for j in range(8):
                acc[j, here] = acc[j, here] + image[j]
        for c in range(0, 8, CHUNK):
            here = slice(c, c + CHUNK)
            now = [source[here, j] for j in range(8)]
            slopes = apply_eight(now, FORWARD)
            for j in range(8):
                gradient[1, here, j] = slopes[j]
            image = apply_eight([cy[here, j] * slopes[j] for j in range(8)], BACKWARD)
            image[0], image[7] = join_y(image[0], image[7])
            for j in range(8):
                change = keep[here, j] * v_from[here, j] - scale[here, j] * (acc[here, j] + image[j])
                v_to[here, j] = change
                u_to[here, j] = now[j] + change

    def face_rows(u):
        along_x, along_y = kx[0] * u[0], ky[:, 0] * u[:, 0]
        for j in range(1, 8):
            along_x = along_x + kx[j] * u[j]
            along_y = along_y + ky[:, j] * u[:, j]
        return along_x, along_y

    def mail(kind, field, slot):
        src = [xs.at[kind, field, slot], ys.at[kind, field, slot]]
        dst = [xr.at[kind, field, slot], yr.at[kind, field, slot]]
        if kind == 0:
            src.append(ds.at[field, slot])
            dst.append(dr.at[field, slot])
        return src, dst, send.at[field, slot], recv.at[field, slot], 8 * kind

    def begin(field, turn, source, gradient, v_from, u_to, v_to):
        slot = lax.rem(turn, 2)
        first, second = mail(0, field, slot), mail(1, field, slot)
        own_x, own_y = face_rows(source)
        put_faces(first[0][0], first[0][1], own_x, own_x, own_y, own_y)
        for side, node in ((0, 0), (1, 7)):
            sp_x[field, side] = scale[node] * own_x
            sp_y[field, side] = scale[:, node] * own_y
        lines_x = [jnp.sum(kx[:, n] * sp_y[field, s], axis=0) for s, n in ((0, 0), (1, 7))]
        lines_y = [jnp.sum(ky[n] * sp_x[field, s], axis=0) for s, n in ((0, 0), (1, 7))]
        ds[field, slot] = -(
            jnp.where(ey == 0, lines_x[0], lines_x[1]) + jnp.where(low_x, lines_y[0], lines_y[1])
        )
        copies(*first)
        advance(source, gradient, v_from, u_to, v_to)
        next_x, next_y = face_rows(u_to)
        put_faces(second[0][0], second[0][1], next_x, next_x, next_y, next_y)
        copies(*second)

    def mend(u, v, parts_x, parts_y):
        for node, part in zip((0, 7), parts_x):
            part = scale[node] * part
            u[node] = u[node] - part
            v[node] = v[node] - part
        for node, part in zip((0, 7), parts_y):
            part = scale[:, node] * part
            u[:, node] = u[:, node] - part
            v[:, node] = v[:, node] - part

    def complete(field, turn, u, v):
        letter = mail(0, field, lax.rem(turn, 2))
        arrive(*letter, range(4))
        from_x, from_y = letter[1][:2]
        mend(
            u,
            v,
            [jnp.where(halo_x[s], unpack_x(s, from_x[s]), 0.0) for s in range(2)],
            [jnp.where(halo_y[s], unpack_y(s, from_y[s]), 0.0) for s in range(2)],
        )

    def finish(field, turn, source, gradient, v_from, u_to, v_to):
        slot = lax.rem(turn, 2)
        advance(source, gradient, v_from, u_to, v_to)
        first, second = mail(0, field, slot), mail(1, field, slot)
        arrive(*second)
        from_x, from_y = second[1]
        parts_x, parts_y = [], []
        for s in range(2):
            part = unpack_x(s, from_x[s]) - kn_x[s] * sp_x[field, s]
            parts_x.append(jnp.where(halo_x[s], part, 0.0))
            part = unpack_y(s, from_y[s]) - kn_y[s] * sp_y[field, s]
            parts_y.append(jnp.where(halo_y[s], part, 0.0))
        mend(u_to, v_to, parts_x, parts_y)
        arrive(*first, range(4, 8))
        from_d = first[1][2]
        for k, (ix, iy, _, turn_by) in enumerate(node_d):
            line = jnp.where(halo_d[k], roll_sub(from_d[k], turn_by), 0.0)
            part = scale[ix, iy] * line
            u_to[ix, iy] = u_to[ix, iy] - part
            v_to[ix, iy] = v_to[ix, iy] - part

    def begin_u(turn):
        n = 2 * turn + 1
        begin(0, turn, uf, gu.at[n], vf.at[n], uf, vf.at[n + 1])

    def begin_a(turn):
        n = 8 - 2 * turn
        begin(1, turn, aa.at[n], ga.at[n], va, aa.at[n - 1], va)

    def finish_u(turn):
        n = 2 * turn + 2
        complete(0, turn, uf, vf.at[n])
        finish(0, turn, uf, gu.at[n], vf.at[n], uf, vf.at[n + 1])

    def finish_a(turn):
        n = 7 - 2 * turn
        complete(1, turn, aa.at[n], va)
        finish(1, turn, aa.at[n], ga.at[n], va, aa.at[n - 1], va)

    begin_u(0)
    arrive(*group_refs(2))
    for f in groups[2]:
        add_field(f)
    for ix in range(8):
        va[ix] = aa[8, ix] - va[ix]
    begin_a(0)
    arrive(*ends)
    for side in range(2):
        kn_x[side] = unpack_x(side, xrk[side])
        kn_y[side] = unpack_y(side, yrk[side])

    def cycle(turn, carry):
        finish_u(turn)
        begin_u(turn + 1)
        finish_a(turn)
        begin_a(turn + 1)
        return carry

    lax.fori_loop(0, STEPS // 2 - 1, cycle, 0)

    def density_of(ns, ix):
        total = None
        for n in ns:
            for d in range(3):
                term = gu[n, d, ix] * ga[n, d, ix]
                total = term if total is None else total + term
        return total

    def moduli_of(ns, ix):
        modulus, impedance = None, None
        for n in ns:
            now, before, after = aa[n, ix], vf[n, ix], vf[n + 1, ix]
            a, b = now * (after - before), now * (after + before)
            modulus = a if modulus is None else modulus + a
            impedance = b if impedance is None else impedance + b
        return modulus, impedance

    for ix in range(8):
        sums[0, ix] = density_of(range(2, 8), ix)
        sums[1, ix], sums[2, ix] = moduli_of(range(2, 7), ix)

    last = STEPS // 2 - 1
    finish_u(last)
    complete(1, last, aa.at[1], va)
    arrive(*mail(0, 1, last % 2), range(4, 8))
    arrive(*mail(1, 1, last % 2))
    source, gradient = aa.at[1], ga.at[1]
    gradient[2] = times(source[...].reshape(512, LANES), 0).reshape(8, 8, 8, LANES)
    for c in range(0, 8, CHUNK):
        here = slice(c, c + CHUNK)
        slopes = apply_eight([source[j, here] for j in range(8)], FORWARD)
        for j in range(8):
            gradient[0, j, here] = slopes[j]
        slopes = apply_eight([source[here, j] for j in range(8)], FORWARD)
        for j in range(8):
            gradient[1, here, j] = slopes[j]

    for ix in range(8):
        density = sums[0, ix] + density_of((1, 8), ix)
        modulus, impedance = moduli_of((1, 7, 8), ix)
        modulus = sums[1, ix] + modulus
        impedance = (sums[2, ix] + impedance) * (1.0 - keep[ix])
        for iy in range(8):
            weight = wz * float(TIME_STEP * GLL_WEIGHTS[ix] * GLL_WEIGHTS[iy])
            rows = pl.ds(iy, 8, stride=8)
            dens_ref[ix, rows, :] = weight * density[iy]
            mod_ref[ix, rows, :] = modulus[iy]
            imp_ref[ix, rows, :] = impedance[iy]


def deliver(*refs):
    parts, outs, sem = refs[:3], refs[3:6], refs[6]
    stores = [
        pltpu.make_async_copy(
            parts[k].at[:, pl.ds(32 * half, 32), :],
            outs[k].at[pl.ds(8 * half, 8)],
            sem.at[2 * k + half],
        )
        for k in range(3)
        for half in range(2)
    ]
    for store in stores:
        store.start()
    for store in stores:
        store.wait()


def field(*lead):
    return pltpu.VMEM((*lead, 8, 8, 8, LANES), F32)


def per_device(shape_xy, *args):
    vectors = lambda *lead: pltpu.VMEM((*lead, 8, LANES), F32)
    hbm = pl.BlockSpec(memory_space=pltpu.HBM)
    vmem = pl.BlockSpec(memory_space=pltpu.VMEM)
    operands = [pltpu.with_memory_space_constraint(a, pltpu.HBM) for a in args]
    parts = pl.pallas_call(
        functools.partial(kernel, shape_xy),
        out_shape=(pltpu.VMEM((8, 64, LANES), F32),) * 3,
        in_specs=[hbm] * 7,
        out_specs=(vmem,) * 3,
        scratch_shapes=[
            pltpu.VMEM((6, 8, 64, LANES), F32),
            pltpu.VMEM(args[6].shape, jnp.int32),
            pltpu.VMEM((2, 2 * LANES, 2 * LANES), BF16),
            field(),
            field(),
            field(),
            field(),
            field(),
            field(),
            field(),
            field(),
            field(10),
            field(9),
            field(),
            field(9, 3),
            field(9, 3),
            field(),
            vectors(2, 2, 8),
            vectors(2, 2, 8),
            vectors(2, 8),
            vectors(2, 8),
            field(3),
            vectors(2, 7, 4),
            vectors(2, 7, 2),
            vectors(7),
            vectors(2, 4),
            vectors(2, 2),
            vectors(2, 7, 4),
            vectors(2, 7, 2),
            vectors(4, 7),
            vectors(2, 4),
            vectors(2, 2),
            vectors(2, 4),
            vectors(2, 2),
            vectors(2, 2, 2, 2, 4),
            vectors(2, 2, 2, 2, 2),
            vectors(2, 2),
            vectors(2, 2, 2, 2, 4),
            vectors(2, 2, 2, 2, 2),
            vectors(2, 2, 4),
            pltpu.SemaphoreType.DMA((13,)),
            pltpu.SemaphoreType.DMA((28,)),
            pltpu.SemaphoreType.DMA((28,)),
            pltpu.SemaphoreType.DMA((4,)),
            pltpu.SemaphoreType.DMA((4,)),
            pltpu.SemaphoreType.DMA((2, 2, 12)),
            pltpu.SemaphoreType.DMA((2, 2, 12)),
        ],
        compiler_params=pltpu.CompilerParams(
            collective_id=0, has_side_effects=True, vmem_limit_bytes=48 * 1024 * 1024
        ),
    )(*operands)
    return pl.pallas_call(
        deliver,
        out_shape=(pltpu.HBM(args[0].shape, F32),) * 3,
        in_specs=[pl.BlockSpec(memory_space=pl.ANY)] * 3,
        out_specs=(hbm,) * 3,
        scratch_shapes=[pltpu.SemaphoreType.DMA((6,))],
    )(*[pltpu.with_memory_space_constraint(part, pltpu.VMEM) for part in parts])


def solution(mesh):
    shape_xy = (mesh.shape["gx"], mesh.shape["gy"])
    in_specs = (P("gx", "gy", None),) * 6 + (P(None, "gx", "gy", None),)
    out_specs = (P("gx", "gy", None),) * 3
    return jax.shard_map(
        functools.partial(per_device, shape_xy),
        mesh=mesh,
        in_specs=in_specs,
        out_specs=out_specs,
        check_vma=False,
    )
```

```python
import functools

import jax
import jax.numpy as jnp
import numpy as np
from jax import lax
from jax.experimental import pallas as pl
from jax.experimental.pallas import tpu as pltpu
from jax.sharding import PartitionSpec as P

MESH = pl.DeviceIdType.MESH
F32 = jnp.float32
BF16 = jnp.bfloat16
NODES = 8
STEPS = 8
LANES = 128
CHUNK = 2

TIME_STEP = 0.01
GLL_POINTS = (
    -1.0,
    -0.8717401485096066,
    -0.5917001814331423,
    -0.2092992179024789,
    0.2092992179024789,
    0.5917001814331423,
    0.8717401485096066,
    1.0,
)
GLL_WEIGHTS = (
    0.03571428571428571,
    0.2107042271435061,
    0.3411226924835044,
    0.4124587946587038,
    0.4124587946587038,
    0.3411226924835044,
    0.2107042271435061,
    0.03571428571428571,
)


def gll_derivative():
    points = np.array(GLL_POINTS)
    previous_poly = np.ones(NODES)
    current_poly = points.copy()
    for degree in range(1, NODES - 1):
        next_poly = ((2 * degree + 1) * points * current_poly - degree * previous_poly) / (
            degree + 1
        )
        previous_poly, current_poly = (current_poly, next_poly)
    matrix = np.zeros((NODES, NODES))
    for row_index in range(NODES):
        for col_index in range(NODES):
            if row_index != col_index:
                matrix[row_index, col_index] = current_poly[row_index] / (
                    current_poly[col_index] * (points[row_index] - points[col_index])
                )
    matrix[0, 0] = -NODES * (NODES - 1) / 4.0
    matrix[NODES - 1, NODES - 1] = NODES * (NODES - 1) / 4.0
    return matrix


DERIVATIVE = gll_derivative()


def halves(matrix):
    near, far = matrix[:4, :4], matrix[:4, 7:3:-1]
    return (near - far) / 2, (near + far) / 2


FORWARD = halves(DERIVATIVE)
BACKWARD = halves(DERIVATIVE.T)


def apply_eight(values, blocks):
    odd, even = blocks
    sums = [values[j] + values[7 - j] for j in range(4)]
    diffs = [values[j] - values[7 - j] for j in range(4)]
    low, high = [], []
    for i in range(4):
        a = diffs[0] * float(odd[i, 0])
        b = sums[0] * float(even[i, 0])
        for j in range(1, 4):
            a = a + diffs[j] * float(odd[i, j])
            b = b + sums[j] * float(even[i, j])
        low.append(a + b)
        high.append(a - b)
    return low + high[::-1]


def roll_sub(values, shift):
    shift %= 8
    return values if shift == 0 else pltpu.roll(values, shift, values.ndim - 2)


def kernel(
    shape_xy,
    up_ref,
    uc_ref,
    an_ref,
    ac_ref,
    im_ref,
    id_ref,
    fm_ref,
    dens_ref,
    mod_ref,
    imp_ref,
    nat,
    mask,
    table,
    cx,
    cy,
    cz,
    scale,
    keep,
    kx,
    ky,
    uf,
    vf,
    aa,
    va,
    gu,
    ga,
    acc,
    sp_x,
    sp_y,
    kn_x,
    kn_y,
    sums,
    xs0,
    ys0,
    ds0,
    xs1,
    ys1,
    xr0,
    yr0,
    dr0,
    xrk,
    yrk,
    xs,
    ys,
    ds,
    xr,
    yr,
    dr,
    in_sem,
    send0,
    recv0,
    sendk,
    recvk,
    send,
    recv,
):
    count_x, count_y = shape_xy
    gx, gy = lax.axis_index("gx"), lax.axis_index("gy")

    in_x = {0: gx > 0, 1: gx < count_x - 1}
    in_y = {0: gy > 0, 1: gy < count_y - 1}
    other_x = gx + 1 - 2 * lax.rem(gx, 2)
    other_y = gy + 1 - 2 * lax.rem(gy, 2)

    def target_x(side):
        here = in_x[side]
        step = 2 * side - 1
        device = (jnp.where(here, gx + step, gx), jnp.where(here, gy, other_y))
        return device, jnp.where(here, 1 - side, side)

    def target_y(side):
        here = in_y[side]
        step = 2 * side - 1
        device = (jnp.where(here, gx, other_x), jnp.where(here, gy + step, gy))
        return device, jnp.where(here, 1 - side, side)

    def target_d(side_x, side_y):
        hx, hy = in_x[side_x], in_y[side_y]
        both_out = jnp.logical_not(jnp.logical_or(hx, hy))
        dx = jnp.where(both_out, count_x - 1 - gx, jnp.where(hx, gx + 2 * side_x - 1, gx))
        dy = jnp.where(hy, gy + 2 * side_y - 1, gy)
        slot_x = jnp.where(jnp.logical_or(hx, both_out), 1 - side_x, side_x)
        slot_y = jnp.where(hy, 1 - side_y, side_y)
        return (dx, dy), slot_x * 2 + slot_y

    targets_x = [target_x(0), target_x(1)]
    targets_y = [target_y(0), target_y(1)]
    targets_d = [target_d(0, 0), target_d(0, 1), target_d(1, 0), target_d(1, 1)]

    barrier = pltpu.get_barrier_semaphore()
    for device, _ in targets_x + targets_y + targets_d:
        pl.semaphore_signal(barrier, inc=1, device_id=device, device_id_type=MESH)

    loads = []
    for k, ref in enumerate((id_ref, uc_ref, im_ref, up_ref, ac_ref, an_ref)):
        for half in range(2):
            loads.append(
                pltpu.make_async_copy(
                    ref.at[pl.ds(8 * half, 8)],
                    nat.at[k, :, pl.ds(32 * half, 32), :],
                    in_sem.at[2 * k + half],
                )
            )
    loads.append(pltpu.make_async_copy(fm_ref, mask, in_sem.at[12]))
    for load in loads:
        load.start()

    sub = lax.broadcasted_iota(jnp.int32, (8, LANES), 0)
    lane = lax.broadcasted_iota(jnp.int32, (8, LANES), 1)
    ey = sub % 4
    low_x = sub < 4
    zplace = lane % 8
    z_low = jnp.logical_and(zplace == 0, lane > 0)
    z_high = jnp.logical_and(zplace == 7, lane < LANES - 1)
    zero = jnp.zeros((8, LANES), F32)
    wz = zero
    for j in range(NODES):
        wz = jnp.where(zplace == j, F32(GLL_WEIGHTS[j]), wz)

    def sum_third(values):
        before = pltpu.roll(values, 1, values.ndim - 1)
        after = pltpu.roll(values, LANES - 1, values.ndim - 1)
        return values + jnp.where(z_low, before, jnp.where(z_high, after, 0.0))

    def one_if(flag):
        return jnp.where(flag, 1, 0)

    halo_x = [sub < 4 * one_if(in_x[0]), sub >= 8 - 4 * one_if(in_x[1])]
    halo_y = [ey < one_if(in_y[0]), ey >= 4 - one_if(in_y[1])]
    halo_d = [
        jnp.logical_and(halo_x[0], halo_y[0]),
        jnp.logical_and(halo_x[0], halo_y[1]),
        jnp.logical_and(halo_x[1], halo_y[0]),
        jnp.logical_and(halo_x[1], halo_y[1]),
    ]
    node_d = ((0, 0, 0, 1), (0, 7, 3, -1), (7, 0, 4, 1), (7, 7, 7, -1))

    def join_x(first, last):
        return (
            first + jnp.where(low_x, 0.0, roll_sub(last, 4)),
            last + jnp.where(low_x, roll_sub(first, 4), 0.0),
        )

    def join_y(first, last):
        return (
            first + jnp.where(ey == 0, 0.0, roll_sub(last, 1)),
            last + jnp.where(ey == 3, 0.0, roll_sub(first, 7)),
        )

    def pack_x(first, last):
        return (
            jnp.where(low_x, first[0:4], roll_sub(first[4:8], 4)),
            jnp.where(low_x, roll_sub(last[0:4], 4), last[4:8]),
        )

    def unpack_x(side, packed):
        turned = roll_sub(packed, 4)
        pair = [packed, turned] if side == 0 else [turned, packed]
        return jnp.concatenate(pair, axis=0)

    def pack_y(first, last):
        first = first.reshape(2, 4, 8, LANES)
        last = last.reshape(2, 4, 8, LANES)
        low, high = first[:, 0], roll_sub(last[:, 0], 5)
        for j in range(1, 4):
            low = jnp.where(ey == j, roll_sub(first[:, j], j), low)
            high = jnp.where(ey == j, roll_sub(last[:, j], 5 + j), high)
        return low, high

    def unpack_y(side, packed):
        rows = [roll_sub(packed, 3 * side - j) for j in range(4)]
        return jnp.stack(rows, axis=1).reshape(8, 8, LANES)

    def corner_lines(n00, n07, n70, n77):
        return jnp.where(low_x, jnp.where(ey == 0, n00, n07), jnp.where(ey == 0, n70, n77))

    def copies(src, dst, ssem, rsem, first):
        out = []
        for kind, targets in ((2, targets_d), (1, targets_y), (0, targets_x)):
            if src[kind] is not None:
                for k, (device, slot) in enumerate(targets):
                    a = src[kind] if kind == 2 else src[kind].at[k]
                    out.append((a, dst[kind].at[slot], 2 * kind + k, 2 * kind + slot, device))
        for a, b, i, j, device in out:
            pltpu.make_async_remote_copy(
                src_ref=a,
                dst_ref=b,
                send_sem=ssem.at[first + i],
                recv_sem=rsem.at[first + j],
                device_id=device,
                device_id_type=MESH,
            ).start()

    def arrive(src, dst, ssem, rsem, first):
        for kind in range(3):
            if src[kind] is not None:
                for k in range(4 if kind == 2 else 2):
                    copy = pltpu.make_async_remote_copy(
                        src_ref=src[kind] if kind == 2 else src[kind].at[k],
                        dst_ref=dst[kind].at[k],
                        send_sem=ssem.at[first + 2 * kind + k],
                        recv_sem=rsem.at[first + 2 * kind + k],
                        device_id=targets_x[0][0],
                        device_id_type=MESH,
                    )
                    copy.wait_recv()
                    copy.wait_send()

    homes = (cz, uf, scale, keep, vf.at[1], aa.at[8], va)
    places = (0, 1, 2, None, 3, 4, 5)
    groups = ((0, 1), (2, 3, 4), (5, 6))

    def natural(k, ix, iy):
        return nat[k, ix, pl.ds(iy, 8, stride=8), :]

    half_x = [jnp.where(jnp.logical_or(halo_x[0], jnp.logical_not(low_x)), 0.5, 1.0), 1.0]
    half_x_high = jnp.where(jnp.logical_or(halo_x[1], low_x), 0.5, 1.0)
    half_y_low = jnp.where(jnp.logical_or(halo_y[0], ey != 0), 0.5, 1.0)
    half_y_high = jnp.where(jnp.logical_or(halo_y[1], ey != 3), 0.5, 1.0)
    half_z = jnp.where(jnp.logical_or(z_low, z_high), 0.5, 1.0)

    def share(ix, iy):
        value = half_z
        if ix == 0:
            value = value * half_x[0]
        if ix == 7:
            value = value * half_x_high
        if iy == 0:
            value = value * half_y_low
        if iy == 7:
            value = value * half_y_high
        return value

    def fill_tables():
        tiles = [zero, zero]
        for i in range(8):
            for j in range(8):
                value = F32(DERIVATIVE[i, j])
                tiles[0] = jnp.where(jnp.logical_and(sub == j, zplace == i), value, tiles[0])
                tiles[1] = jnp.where(jnp.logical_and(sub == i, zplace == j), value, tiles[1])
        for which in range(2):
            rows = [jnp.where(lane // 8 == k, tiles[which], 0.0) for k in range(LANES // 8)]
            if which == 1:
                rows = [sum_third(row) for row in rows]
            block = jnp.concatenate(rows, axis=0)
            high = block.astype(BF16)
            low = (block - high.astype(F32)).astype(BF16)
            for half in range(2):
                here = slice(LANES * half, LANES * half + LANES)
                table[which, here, :LANES] = high
                table[which, here, LANES:] = low

    faces_at = [(ix, iy) for ix in range(8) for iy in range(8) if ix in (0, 7) or iy in (0, 7)]
    inside_at = [(ix, iy) for ix in range(1, 7) for iy in range(1, 7)]
    face_parts = ((0,), (7,), (slice(1, 7), 0), (slice(1, 7), 7))
    inside = (slice(1, 7), slice(1, 7))

    def arrived_here(f):
        for load in loads[2 * places[f] : 2 * places[f] + 2]:
            load.wait()

    def fill(f, nodes):
        for ix, iy in nodes:
            weight = float(GLL_WEIGHTS[ix] * GLL_WEIGHTS[iy])
            if f == 0:
                raw = natural(0, ix, iy) * (wz * weight)
                summed = sum_third(raw)
                cz[ix, iy] = raw
                cx[ix, iy] = summed
                cy[ix, iy] = summed
            elif f == 2:
                scale[ix, iy] = sum_third(natural(2, ix, iy) * (wz * weight))
            elif f == 3:
                value = third_face * weight
                if ix == 0:
                    value = value + faces[0] * float(GLL_WEIGHTS[iy])
                if ix == 7:
                    value = value + faces[1] * float(GLL_WEIGHTS[iy])
                if iy == 0:
                    value = value + faces[2] * float(GLL_WEIGHTS[ix])
                if iy == 7:
                    value = value + faces[3] * float(GLL_WEIGHTS[ix])
                keep[ix, iy] = value
            else:
                homes[f][ix, iy] = sum_third(natural(places[f], ix, iy) * share(ix, iy))

    def damping_faces():
        spread = jnp.where(
            lax.broadcasted_iota(jnp.int32, (16, LANES), 1) // 8
            == lax.broadcasted_iota(jnp.int32, (16, LANES), 0),
            1.0,
            0.0,
        ).astype(F32)
        cells = [
            jnp.dot(
                jnp.concatenate([mask[f, 0], mask[f, 1]], axis=0).astype(F32),
                spread,
                preferred_element_type=F32,
            )
            for f in range(6)
        ]
        ends = jnp.where(zplace == 0, cells[4], jnp.where(zplace == 7, cells[5], 0.0))
        return [sum_third(wz * cell) for cell in cells[:4]], sum_third(ends)

    def join_first(home):
        first, last = join_x(home[0], home[7])
        home[0] = first
        home[7] = last

    def join_second(home):
        first, last = join_y(home[:, 0], home[:, 7])
        home[:, 0] = first
        home[:, 7] = last

    def pack_field(f):
        home = homes[f]
        if f > 0:
            join_first(home)
            join_second(home)
        xs0[0, f], xs0[1, f] = pack_x(home[0], home[7])
        ys0[0, f], ys0[1, f] = pack_y(home[:, 0], home[:, 7])
        ds0[f] = corner_lines(home[0, 0], home[0, 7], home[7, 0], home[7, 7])

    def group_refs(g):
        here = pl.ds(groups[g][0], len(groups[g]))
        src = (xs0.at[:, here], ys0.at[:, here], ds0.at[here])
        dst = (xr0.at[:, here], yr0.at[:, here], dr0.at[:, here])
        return src, dst, send0, recv0, 8 * g

    for f in groups[0]:
        arrived_here(f)
        fill(f, faces_at)
        pack_field(f)
    loads[12].wait()
    faces, third_face = damping_faces()
    for f in groups[1]:
        if f != 3:
            arrived_here(f)
        fill(f, faces_at)
        pack_field(f)
    pl.semaphore_wait(barrier, 8)
    copies(*group_refs(0))
    copies(*group_refs(1))
    for home, joins in ((cz, (join_first, join_second)), (cy, (join_first,)), (cx, (join_second,))):
        for join in joins:
            join(home)

    def rates(here):
        one_over = 1.0 / scale[here]
        scale[here] = (TIME_STEP * TIME_STEP) * one_over
        keep[here] = 1.0 - TIME_STEP * keep[here] * one_over

    end_x = [jnp.where(low_x, F32(DERIVATIVE[i, 0]), F32(DERIVATIVE[i, 7])) for i in range(8)]
    end_y = [jnp.where(ey < 2, F32(DERIVATIVE[i, 0]), F32(DERIVATIVE[i, 7])) for i in range(8)]

    def fill_rows(here):
        rows = apply_eight([end_x[i] * cx[i, here] for i in range(8)], BACKWARD)
        for j in range(8):
            kx[j, here] = rows[j]
        rows = apply_eight([end_y[i] * cy[here, i] for i in range(8)], BACKWARD)
        for j in range(8):
            ky[here, j] = rows[j]

    for f in range(5):
        fill(f, inside_at)
    fill_tables()
    rates(inside)
    vf[1, 1:7, 1:7] = uf[inside] - vf[1, 1:7, 1:7]
    for c in range(1, 7, CHUNK):
        fill_rows(slice(c, c + CHUNK))

    for f in groups[2]:
        arrived_here(f)
        fill(f, faces_at)
        pack_field(f)
    copies(*group_refs(2))
    for f in groups[2]:
        fill(f, inside_at)
    va[inside] = aa[8, 1:7, 1:7] - va[inside]

    def from_sides(f):
        parts_x = [jnp.where(halo_x[s], unpack_x(s, xr0[s, f]), 0.0) for s in range(2)]
        parts_y = [jnp.where(halo_y[s], unpack_y(s, yr0[s, f]), 0.0) for s in range(2)]
        return parts_x, parts_y

    def add_x(home, parts):
        for node, part in zip((0, 7), parts):
            home[node] = home[node] + part

    def add_y(home, parts):
        for node, part in zip((0, 7), parts):
            home[:, node] = home[:, node] + part

    def add_field(f):
        home = homes[f]
        parts_x, parts_y = from_sides(f)
        add_x(home, parts_x)
        add_y(home, parts_y)
        if f == 0:
            add_x(cy, [sum_third(part) for part in parts_x])
            add_y(cx, [sum_third(part) for part in parts_y])
            for node, part in zip((0, 7), parts_x):
                first, last = join_y(part[0], part[7])
                cz[node, 0] = cz[node, 0] + (first - part[0])
                cz[node, 7] = cz[node, 7] + (last - part[7])
            for node, part in zip((0, 7), parts_y):
                first, last = join_x(part[0], part[7])
                cz[0, node] = cz[0, node] + (first - part[0])
                cz[7, node] = cz[7, node] + (last - part[7])
        for k, (ix, iy, _, turn) in enumerate(node_d):
            home[ix, iy] = home[ix, iy] + jnp.where(halo_d[k], roll_sub(dr0[k, f], turn), 0.0)

    arrive(*group_refs(0))
    add_field(0)
    for c in (0, 7):
        fill_rows(slice(c, c + 1))

    def put_faces(side_x, side_y, fx0, fx1, fy0, fy1):
        side_x[0], side_x[1] = pack_x(fx0, fx1)
        side_y[0], side_y[1] = pack_y(fy0, fy1)

    ends = ((xs1, ys1, None), (xrk, yrk, None), sendk, recvk, 0)
    put_faces(xs1, ys1, kx[0], kx[7], ky[:, 0], ky[:, 7])
    copies(*ends)
    add_field(1)

    def rest_of_setup():
        arrive(*group_refs(1))
        for f in groups[1]:
            add_field(f)
        for here in face_parts:
            rates(here)
            vf[(1, *here)] = uf[here] - vf[(1, *here)]

    def times(values, which):
        high = values.astype(BF16)
        low = (values - high.astype(F32)).astype(BF16)
        both = jnp.dot(
            jnp.concatenate([high, low], axis=1), table[which], preferred_element_type=F32
        )
        return both[:, :LANES] + both[:, LANES:]

    def advance(source, gradient, v_from, u_to, v_to, between=None):
        slope = times(source[...].reshape(512, LANES), 0)
        gradient[2] = slope.reshape(8, 8, 8, LANES)
        acc[...] = times(cz[...].reshape(512, LANES) * slope, 1).reshape(8, 8, 8, LANES)
        for c in range(0, 8, CHUNK):
            here = slice(c, c + CHUNK)
            slopes = apply_eight([source[j, here] for j in range(8)], FORWARD)
            for j in range(8):
                gradient[0, j, here] = slopes[j]
            image = apply_eight([cx[j, here] * slopes[j] for j in range(8)], BACKWARD)
            image[0], image[7] = join_x(image[0], image[7])
            for j in range(8):
                acc[j, here] = acc[j, here] + image[j]
        if between is not None:
            between()
        for c in range(0, 8, CHUNK):
            here = slice(c, c + CHUNK)
            now = [source[here, j] for j in range(8)]
            slopes = apply_eight(now, FORWARD)
            for j in range(8):
                gradient[1, here, j] = slopes[j]
            image = apply_eight([cy[here, j] * slopes[j] for j in range(8)], BACKWARD)
            image[0], image[7] = join_y(image[0], image[7])
            for j in range(8):
                change = keep[here, j] * v_from[here, j] - scale[here, j] * (acc[here, j] + image[j])
                v_to[here, j] = change
                u_to[here, j] = now[j] + change

    def face_rows(u):
        along_x, along_y = kx[0] * u[0], ky[:, 0] * u[:, 0]
        for j in range(1, 8):
            along_x = along_x + kx[j] * u[j]
            along_y = along_y + ky[:, j] * u[:, j]
        return along_x, along_y

    def mail(kind, field, slot):
        if kind < 2:
            src = (xs.at[kind, field, slot], ys.at[kind, field, slot], None)
            dst = (xr.at[kind, field, slot], yr.at[kind, field, slot], None)
        else:
            src = (None, None, ds.at[field, slot])
            dst = (None, None, dr.at[field, slot])
        return src, dst, send.at[field, slot], recv.at[field, slot], (0, 8, 0)[kind]

    def begin(field, turn, source, gradient, v_from, u_to, v_to, between=None):
        slot = lax.rem(turn, 2)
        first, second = mail(0, field, slot), mail(1, field, slot)
        corners = mail(2, field, slot)
        own_x, own_y = face_rows(source)
        put_faces(first[0][0], first[0][1], own_x, own_x, own_y, own_y)
        copies(*first)

        def send_corners():
            for side, node in ((0, 0), (1, 7)):
                sp_x[field, side] = scale[node] * own_x
                sp_y[field, side] = scale[:, node] * own_y
            lines_x = [jnp.sum(kx[:, n] * sp_y[field, s], axis=0) for s, n in ((0, 0), (1, 7))]
            lines_y = [jnp.sum(ky[n] * sp_x[field, s], axis=0) for s, n in ((0, 0), (1, 7))]
            ds[field, slot] = -(
                jnp.where(ey == 0, lines_x[0], lines_x[1])
                + jnp.where(low_x, lines_y[0], lines_y[1])
            )
            copies(*corners)

        if between is None:
            send_corners()
            advance(source, gradient, v_from, u_to, v_to)
        else:

            def both():
                between()
                send_corners()

            advance(source, gradient, v_from, u_to, v_to, both)
        next_x, next_y = face_rows(u_to)
        put_faces(second[0][0], second[0][1], next_x, next_x, next_y, next_y)
        copies(*second)

    def mend(u, v, parts_x, parts_y):
        for node, part in zip((0, 7), parts_x):
            part = scale[node] * part
            u[node] = u[node] - part
            v[node] = v[node] - part
        for node, part in zip((0, 7), parts_y):
            part = scale[:, node] * part
            u[:, node] = u[:, node] - part
            v[:, node] = v[:, node] - part

    def complete(field, turn, u, v):
        letter = mail(0, field, lax.rem(turn, 2))
        arrive(*letter)
        from_x, from_y = letter[1][:2]
        mend(
            u,
            v,
            [jnp.where(halo_x[s], unpack_x(s, from_x[s]), 0.0) for s in range(2)],
            [jnp.where(halo_y[s], unpack_y(s, from_y[s]), 0.0) for s in range(2)],
        )

    def finish(field, turn, source, gradient, v_from, u_to, v_to):
        slot = lax.rem(turn, 2)
        advance(source, gradient, v_from, u_to, v_to)
        second, corners = mail(1, field, slot), mail(2, field, slot)
        arrive(*second)
        from_x, from_y = second[1][:2]
        parts_x, parts_y = [], []
        for s in range(2):
            part = unpack_x(s, from_x[s]) - kn_x[s] * sp_x[field, s]
            parts_x.append(jnp.where(halo_x[s], part, 0.0))
            part = unpack_y(s, from_y[s]) - kn_y[s] * sp_y[field, s]
            parts_y.append(jnp.where(halo_y[s], part, 0.0))
        mend(u_to, v_to, parts_x, parts_y)
        arrive(*corners)
        from_d = corners[1][2]
        for k, (ix, iy, _, turn_by) in enumerate(node_d):
            line = jnp.where(halo_d[k], roll_sub(from_d[k], turn_by), 0.0)
            part = scale[ix, iy] * line
            u_to[ix, iy] = u_to[ix, iy] - part
            v_to[ix, iy] = v_to[ix, iy] - part

    def begin_u(turn, between=None):
        n = 2 * turn + 1
        begin(0, turn, uf, gu.at[n], vf.at[n], uf, vf.at[n + 1], between)

    def begin_a(turn):
        n = 8 - 2 * turn
        begin(1, turn, aa.at[n], ga.at[n], va, aa.at[n - 1], va)

    def finish_u(turn):
        n = 2 * turn + 2
        complete(0, turn, uf, vf.at[n])
        finish(0, turn, uf, gu.at[n], vf.at[n], uf, vf.at[n + 1])

    def finish_a(turn):
        n = 7 - 2 * turn
        complete(1, turn, aa.at[n], va)
        finish(1, turn, aa.at[n], ga.at[n], va, aa.at[n - 1], va)

    begin_u(0, rest_of_setup)
    arrive(*group_refs(2))
    for f in groups[2]:
        add_field(f)
    for here in face_parts:
        va[here] = aa[(8, *here)] - va[here]
    begin_a(0)
    arrive(*ends)
    for side in range(2):
        kn_x[side] = unpack_x(side, xrk[side])
        kn_y[side] = unpack_y(side, yrk[side])

    def cycle(turn, carry):
        finish_u(turn)
        begin_u(turn + 1)
        finish_a(turn)
        begin_a(turn + 1)
        return carry

    lax.fori_loop(0, STEPS // 2 - 1, cycle, 0)

    def density_of(ns, ix):
        total = None
        for n in ns:
            for d in range(3):
                term = gu[n, d, ix] * ga[n, d, ix]
                total = term if total is None else total + term
        return total

    def moduli_of(ns, ix):
        modulus, impedance = None, None
        for n in ns:
            now, before, after = aa[n, ix], vf[n, ix], vf[n + 1, ix]
            a, b = now * (after - before), now * (after + before)
            modulus = a if modulus is None else modulus + a
            impedance = b if impedance is None else impedance + b
        return modulus, impedance

    for ix in range(8):
        sums[0, ix] = density_of(range(2, 8), ix)
        sums[1, ix], sums[2, ix] = moduli_of(range(2, 7), ix)

    last = STEPS // 2 - 1
    finish_u(last)
    for ix in range(8):
        sums[0, ix] = sums[0, ix] + density_of((8,), ix)
        modulus, impedance = moduli_of((7, 8), ix)
        sums[1, ix] = sums[1, ix] + modulus
        sums[2, ix] = sums[2, ix] + impedance
    complete(1, last, aa.at[1], va)
    source, gradient = aa.at[1], ga.at[1]
    gradient[2] = times(source[...].reshape(512, LANES), 0).reshape(8, 8, 8, LANES)
    for c in range(0, 8, CHUNK):
        here = slice(c, c + CHUNK)
        slopes = apply_eight([source[j, here] for j in range(8)], FORWARD)
        for j in range(8):
            gradient[0, j, here] = slopes[j]
        slopes = apply_eight([source[here, j] for j in range(8)], FORWARD)
        for j in range(8):
            gradient[1, here, j] = slopes[j]

    for ix in range(8):
        density = sums[0, ix] + density_of((1,), ix)
        modulus, impedance = moduli_of((1,), ix)
        modulus = sums[1, ix] + modulus
        impedance = (sums[2, ix] + impedance) * (1.0 - keep[ix])
        for iy in range(8):
            weight = wz * float(TIME_STEP * GLL_WEIGHTS[ix] * GLL_WEIGHTS[iy])
            rows = pl.ds(iy, 8, stride=8)
            dens_ref[ix, rows, :] = weight * density[iy]
            mod_ref[ix, rows, :] = modulus[iy]
            imp_ref[ix, rows, :] = impedance[iy]
    arrive(*mail(2, 1, last % 2))
    arrive(*mail(1, 1, last % 2))


def deliver(*refs):
    parts, outs, sem = refs[:3], refs[3:6], refs[6]
    stores = [
        pltpu.make_async_copy(
            parts[k].at[:, pl.ds(32 * half, 32), :],
            outs[k].at[pl.ds(8 * half, 8)],
            sem.at[2 * k + half],
        )
        for k in range(3)
        for half in range(2)
    ]
    for store in stores:
        store.start()
    for store in stores:
        store.wait()


def field(*lead):
    return pltpu.VMEM((*lead, 8, 8, 8, LANES), F32)


def per_device(shape_xy, *args):
    vectors = lambda *lead: pltpu.VMEM((*lead, 8, LANES), F32)
    hbm = pl.BlockSpec(memory_space=pltpu.HBM)
    vmem = pl.BlockSpec(memory_space=pltpu.VMEM)
    operands = [pltpu.with_memory_space_constraint(a, pltpu.HBM) for a in args]
    parts = pl.pallas_call(
        functools.partial(kernel, shape_xy),
        out_shape=(pltpu.VMEM((8, 64, LANES), F32),) * 3,
        in_specs=[hbm] * 7,
        out_specs=(vmem,) * 3,
        scratch_shapes=[
            pltpu.VMEM((6, 8, 64, LANES), F32),
            pltpu.VMEM(args[6].shape, jnp.int32),
            pltpu.VMEM((2, 2 * LANES, 2 * LANES), BF16),
            field(),
            field(),
            field(),
            field(),
            field(),
            field(),
            field(),
            field(),
            field(10),
            field(9),
            field(),
            field(9, 3),
            field(9, 3),
            field(),
            vectors(2, 2, 8),
            vectors(2, 2, 8),
            vectors(2, 8),
            vectors(2, 8),
            field(3),
            vectors(2, 7, 4),
            vectors(2, 7, 2),
            vectors(7),
            vectors(2, 4),
            vectors(2, 2),
            vectors(2, 7, 4),
            vectors(2, 7, 2),
            vectors(4, 7),
            vectors(2, 4),
            vectors(2, 2),
            vectors(2, 2, 2, 2, 4),
            vectors(2, 2, 2, 2, 2),
            vectors(2, 2),
            vectors(2, 2, 2, 2, 4),
            vectors(2, 2, 2, 2, 2),
            vectors(2, 2, 4),
            pltpu.SemaphoreType.DMA((13,)),
            pltpu.SemaphoreType.DMA((24,)),
            pltpu.SemaphoreType.DMA((24,)),
            pltpu.SemaphoreType.DMA((4,)),
            pltpu.SemaphoreType.DMA((4,)),
            pltpu.SemaphoreType.DMA((2, 2, 12)),
            pltpu.SemaphoreType.DMA((2, 2, 12)),
        ],
        compiler_params=pltpu.CompilerParams(
            collective_id=0, has_side_effects=True, vmem_limit_bytes=48 * 1024 * 1024
        ),
    )(*operands)
    return pl.pallas_call(
        deliver,
        out_shape=(pltpu.HBM(args[0].shape, F32),) * 3,
        in_specs=[pl.BlockSpec(memory_space=pl.ANY)] * 3,
        out_specs=(hbm,) * 3,
        scratch_shapes=[pltpu.SemaphoreType.DMA((6,))],
    )(*[pltpu.with_memory_space_constraint(part, pltpu.VMEM) for part in parts])


def solution(mesh):
    shape_xy = (mesh.shape["gx"], mesh.shape["gy"])
    in_specs = (P("gx", "gy", None),) * 6 + (P(None, "gx", "gy", None),)
    out_specs = (P("gx", "gy", None),) * 3
    return jax.shard_map(
        functools.partial(per_device, shape_xy),
        mesh=mesh,
        in_specs=in_specs,
        out_specs=out_specs,
        check_vma=False,
    )
```

```python
import functools

import jax
import jax.numpy as jnp
import numpy as np
from jax import lax
from jax.experimental import pallas as pl
from jax.experimental.pallas import tpu as pltpu
from jax.sharding import PartitionSpec as P

MESH = pl.DeviceIdType.MESH
F32 = jnp.float32
BF16 = jnp.bfloat16
NODES = 8
STEPS = 8
LANES = 128
CHUNK = 2

TIME_STEP = 0.01
GLL_POINTS = (
    -1.0,
    -0.8717401485096066,
    -0.5917001814331423,
    -0.2092992179024789,
    0.2092992179024789,
    0.5917001814331423,
    0.8717401485096066,
    1.0,
)
GLL_WEIGHTS = (
    0.03571428571428571,
    0.2107042271435061,
    0.3411226924835044,
    0.4124587946587038,
    0.4124587946587038,
    0.3411226924835044,
    0.2107042271435061,
    0.03571428571428571,
)


def gll_derivative():
    points = np.array(GLL_POINTS)
    previous_poly = np.ones(NODES)
    current_poly = points.copy()
    for degree in range(1, NODES - 1):
        next_poly = ((2 * degree + 1) * points * current_poly - degree * previous_poly) / (
            degree + 1
        )
        previous_poly, current_poly = (current_poly, next_poly)
    matrix = np.zeros((NODES, NODES))
    for row_index in range(NODES):
        for col_index in range(NODES):
            if row_index != col_index:
                matrix[row_index, col_index] = current_poly[row_index] / (
                    current_poly[col_index] * (points[row_index] - points[col_index])
                )
    matrix[0, 0] = -NODES * (NODES - 1) / 4.0
    matrix[NODES - 1, NODES - 1] = NODES * (NODES - 1) / 4.0
    return matrix


DERIVATIVE = gll_derivative()


def halves(matrix):
    near, far = matrix[:4, :4], matrix[:4, 7:3:-1]
    return (near - far) / 2, (near + far) / 2


FORWARD = halves(DERIVATIVE)
BACKWARD = halves(DERIVATIVE.T)


def apply_eight(values, blocks):
    odd, even = blocks
    sums = [values[j] + values[7 - j] for j in range(4)]
    diffs = [values[j] - values[7 - j] for j in range(4)]
    low, high = [], []
    for i in range(4):
        a = diffs[0] * float(odd[i, 0])
        b = sums[0] * float(even[i, 0])
        for j in range(1, 4):
            a = a + diffs[j] * float(odd[i, j])
            b = b + sums[j] * float(even[i, j])
        low.append(a + b)
        high.append(a - b)
    return low + high[::-1]


def roll_sub(values, shift):
    shift %= 8
    return values if shift == 0 else pltpu.roll(values, shift, values.ndim - 2)


def kernel(
    shape_xy,
    up_ref,
    uc_ref,
    an_ref,
    ac_ref,
    im_ref,
    id_ref,
    fm_ref,
    dens_ref,
    mod_ref,
    imp_ref,
    nat,
    mask,
    table,
    cx,
    cy,
    cz,
    scale,
    keep,
    kx,
    ky,
    uf,
    vf,
    aa,
    va,
    gu,
    ga,
    acc,
    sp_x,
    sp_y,
    kn_x,
    kn_y,
    sums,
    outs0,
    lines0,
    ins0,
    ends_out,
    ends_in,
    outs,
    lines,
    ins,
    in_sem,
    send0,
    recv0,
    send,
    recv,
):
    count_x, count_y = shape_xy
    gx, gy = lax.axis_index("gx"), lax.axis_index("gy")

    in_x = {0: gx > 0, 1: gx < count_x - 1}
    in_y = {0: gy > 0, 1: gy < count_y - 1}
    other_x = gx + 1 - 2 * lax.rem(gx, 2)
    other_y = gy + 1 - 2 * lax.rem(gy, 2)

    def target_x(side):
        here = in_x[side]
        step = 2 * side - 1
        device = (jnp.where(here, gx + step, gx), jnp.where(here, gy, other_y))
        return device, jnp.where(here, 1 - side, side)

    def target_y(side):
        here = in_y[side]
        step = 2 * side - 1
        device = (jnp.where(here, gx, other_x), jnp.where(here, gy + step, gy))
        return device, jnp.where(here, 1 - side, side)

    def target_d(side_x, side_y):
        hx, hy = in_x[side_x], in_y[side_y]
        both_out = jnp.logical_not(jnp.logical_or(hx, hy))
        dx = jnp.where(both_out, count_x - 1 - gx, jnp.where(hx, gx + 2 * side_x - 1, gx))
        dy = jnp.where(hy, gy + 2 * side_y - 1, gy)
        slot_x = jnp.where(jnp.logical_or(hx, both_out), 1 - side_x, side_x)
        slot_y = jnp.where(hy, 1 - side_y, side_y)
        return (dx, dy), slot_x * 2 + slot_y

    targets_x = [target_x(0), target_x(1)]
    targets_y = [target_y(0), target_y(1)]
    targets_d = [target_d(0, 0), target_d(0, 1), target_d(1, 0), target_d(1, 1)]

    barrier = pltpu.get_barrier_semaphore()
    for device, _ in targets_d + targets_y + targets_x:
        pl.semaphore_signal(barrier, inc=1, device_id=device, device_id_type=MESH)

    loads = []
    for k, ref in enumerate((id_ref, uc_ref, im_ref, up_ref, ac_ref, an_ref)):
        for half in range(2):
            loads.append(
                pltpu.make_async_copy(
                    ref.at[pl.ds(8 * half, 8)],
                    nat.at[k, :, pl.ds(32 * half, 32), :],
                    in_sem.at[2 * k + half],
                )
            )
    loads.append(pltpu.make_async_copy(fm_ref, mask, in_sem.at[12]))
    for load in loads:
        load.start()

    sub = lax.broadcasted_iota(jnp.int32, (8, LANES), 0)
    lane = lax.broadcasted_iota(jnp.int32, (8, LANES), 1)
    ey = sub % 4
    low_x = sub < 4
    zplace = lane % 8
    z_low = jnp.logical_and(zplace == 0, lane > 0)
    z_high = jnp.logical_and(zplace == 7, lane < LANES - 1)
    zero = jnp.zeros((8, LANES), F32)
    wz = zero
    for j in range(NODES):
        wz = jnp.where(zplace == j, F32(GLL_WEIGHTS[j]), wz)

    def sum_third(values):
        before = pltpu.roll(values, 1, values.ndim - 1)
        after = pltpu.roll(values, LANES - 1, values.ndim - 1)
        return values + jnp.where(z_low, before, jnp.where(z_high, after, 0.0))

    def one_if(flag):
        return jnp.where(flag, 1, 0)

    halo_x = [sub < 4 * one_if(in_x[0]), sub >= 8 - 4 * one_if(in_x[1])]
    halo_y = [ey < one_if(in_y[0]), ey >= 4 - one_if(in_y[1])]
    halo_d = [
        jnp.logical_and(halo_x[0], halo_y[0]),
        jnp.logical_and(halo_x[0], halo_y[1]),
        jnp.logical_and(halo_x[1], halo_y[0]),
        jnp.logical_and(halo_x[1], halo_y[1]),
    ]
    node_d = ((0, 0, 1), (0, 7, -1), (7, 0, 1), (7, 7, -1))

    def join_x(first, last):
        return (
            first + jnp.where(low_x, 0.0, roll_sub(last, 4)),
            last + jnp.where(low_x, roll_sub(first, 4), 0.0),
        )

    def join_y(first, last):
        return (
            first + jnp.where(ey == 0, 0.0, roll_sub(last, 1)),
            last + jnp.where(ey == 3, 0.0, roll_sub(first, 7)),
        )

    def pack_x(first, last):
        return (
            jnp.where(low_x, first[0:4], roll_sub(first[4:8], 4)),
            jnp.where(low_x, roll_sub(last[0:4], 4), last[4:8]),
        )

    def unpack_x(side, packed):
        turned = roll_sub(packed, 4)
        pair = [packed, turned] if side == 0 else [turned, packed]
        return jnp.concatenate(pair, axis=0)

    def pack_y(first, last):
        first = first.reshape(2, 4, 8, LANES)
        last = last.reshape(2, 4, 8, LANES)
        low, high = first[:, 0], roll_sub(last[:, 0], 5)
        for j in range(1, 4):
            low = jnp.where(ey == j, roll_sub(first[:, j], j), low)
            high = jnp.where(ey == j, roll_sub(last[:, j], 5 + j), high)
        return low, high

    def unpack_y(side, packed):
        rows = [roll_sub(packed, 3 * side - j) for j in range(4)]
        return jnp.stack(rows, axis=1).reshape(8, 8, LANES)

    def corner_lines(n00, n07, n70, n77):
        return jnp.where(low_x, jnp.where(ey == 0, n00, n07), jnp.where(ey == 0, n70, n77))

    def copy(src, dst, ssem, rsem, device):
        return pltpu.make_async_remote_copy(
            src_ref=src,
            dst_ref=dst,
            send_sem=ssem,
            recv_sem=rsem,
            device_id=device,
            device_id_type=MESH,
        )

    def post_faces(out, into, ssem, rsem, lead=()):
        for side, (device, slot) in enumerate(targets_y):
            src, dst = out.at[(*lead, pl.ds(8 + 2 * side, 2))], into.at[(*lead, pl.ds(8 + 2 * slot, 2))]
            copy(src, dst, ssem, rsem, device).start()
        for side, (device, slot) in enumerate(targets_x):
            src, dst = out.at[(*lead, pl.ds(4 * side, 4))], into.at[(*lead, pl.ds(4 * slot, 4))]
            copy(src, dst, ssem, rsem, device).start()

    def post_lines(line, into, ssem, rsem, lead=()):
        for device, slot in targets_d:
            copy(line, into.at[(*lead, 12 + slot)], ssem, rsem, device).start()

    def received(into, rsem):
        copy(into, into, rsem, rsem, targets_x[0][0]).wait_recv()

    def sent(out, ssem):
        copy(out, out, ssem, ssem, targets_x[0][0]).wait_send()

    def put_faces(out, fx0, fx1, fy0, fy1):
        out[0:4], out[4:8] = pack_x(fx0, fx1)
        out[8:10], out[10:12] = pack_y(fy0, fy1)

    def read_x(into, side):
        return jnp.where(halo_x[side], unpack_x(side, into[4 * side : 4 * side + 4]), 0.0)

    def read_y(into, side):
        return jnp.where(halo_y[side], unpack_y(side, into[8 + 2 * side : 10 + 2 * side]), 0.0)

    def read_line(into, k):
        return jnp.where(halo_d[k], roll_sub(into[12 + k], node_d[k][2]), 0.0)

    homes = (cz, uf, scale, keep, vf.at[1], aa.at[8], va)
    places = (0, 1, 2, None, 3, 4, 5)
    groups = ((0, 1), (2, 3, 4), (5, 6))

    def natural(k, ix, iy):
        return nat[k, ix, pl.ds(iy, 8, stride=8), :]

    half_x = [jnp.where(jnp.logical_or(halo_x[0], jnp.logical_not(low_x)), 0.5, 1.0), 1.0]
    half_x_high = jnp.where(jnp.logical_or(halo_x[1], low_x), 0.5, 1.0)
    half_y_low = jnp.where(jnp.logical_or(halo_y[0], ey != 0), 0.5, 1.0)
    half_y_high = jnp.where(jnp.logical_or(halo_y[1], ey != 3), 0.5, 1.0)
    half_z = jnp.where(jnp.logical_or(z_low, z_high), 0.5, 1.0)

    def share(ix, iy):
        value = half_z
        if ix == 0:
            value = value * half_x[0]
        if ix == 7:
            value = value * half_x_high
        if iy == 0:
            value = value * half_y_low
        if iy == 7:
            value = value * half_y_high
        return value

    def fill_tables():
        tiles = [zero, zero]
        for i in range(8):
            for j in range(8):
                value = F32(DERIVATIVE[i, j])
                tiles[0] = jnp.where(jnp.logical_and(sub == j, zplace == i), value, tiles[0])
                tiles[1] = jnp.where(jnp.logical_and(sub == i, zplace == j), value, tiles[1])
        for which in range(2):
            rows = [jnp.where(lane // 8 == k, tiles[which], 0.0) for k in range(LANES // 8)]
            if which == 1:
                rows = [sum_third(row) for row in rows]
            block = jnp.concatenate(rows, axis=0)
            high = block.astype(BF16)
            low = (block - high.astype(F32)).astype(BF16)
            for half in range(2):
                here = slice(LANES * half, LANES * half + LANES)
                table[which, here, :LANES] = high
                table[which, here, LANES:] = low

    faces_at = [(ix, iy) for ix in range(8) for iy in range(8) if ix in (0, 7) or iy in (0, 7)]
    inside_at = [(ix, iy) for ix in range(1, 7) for iy in range(1, 7)]
    face_parts = ((0,), (7,), (slice(1, 7), 0), (slice(1, 7), 7))
    inside = (slice(1, 7), slice(1, 7))

    def arrived_here(f):
        for load in loads[2 * places[f] : 2 * places[f] + 2]:
            load.wait()

    def fill(f, nodes):
        for ix, iy in nodes:
            weight = float(GLL_WEIGHTS[ix] * GLL_WEIGHTS[iy])
            if f == 0:
                raw = natural(0, ix, iy) * (wz * weight)
                summed = sum_third(raw)
                cz[ix, iy] = raw
                cx[ix, iy] = summed
                cy[ix, iy] = summed
            elif f == 2:
                scale[ix, iy] = sum_third(natural(2, ix, iy) * (wz * weight))
            elif f == 3:
                value = third_face * weight
                if ix == 0:
                    value = value + faces[0] * float(GLL_WEIGHTS[iy])
                if ix == 7:
                    value = value + faces[1] * float(GLL_WEIGHTS[iy])
                if iy == 0:
                    value = value + faces[2] * float(GLL_WEIGHTS[ix])
                if iy == 7:
                    value = value + faces[3] * float(GLL_WEIGHTS[ix])
                keep[ix, iy] = value
            else:
                homes[f][ix, iy] = sum_third(natural(places[f], ix, iy) * share(ix, iy))

    def damping_faces():
        spread = jnp.where(
            lax.broadcasted_iota(jnp.int32, (16, LANES), 1) // 8
            == lax.broadcasted_iota(jnp.int32, (16, LANES), 0),
            1.0,
            0.0,
        ).astype(F32)
        cells = [
            jnp.dot(
                jnp.concatenate([mask[f, 0], mask[f, 1]], axis=0).astype(F32),
                spread,
                preferred_element_type=F32,
            )
            for f in range(6)
        ]
        ends = jnp.where(zplace == 0, cells[4], jnp.where(zplace == 7, cells[5], 0.0))
        return [sum_third(wz * cell) for cell in cells[:4]], sum_third(ends)

    def join_first(home):
        first, last = join_x(home[0], home[7])
        home[0] = first
        home[7] = last

    def join_second(home):
        first, last = join_y(home[:, 0], home[:, 7])
        home[:, 0] = first
        home[:, 7] = last

    def pack_field(f):
        home = homes[f]
        if f > 0:
            join_first(home)
            join_second(home)
        put_faces(outs0.at[f], home[0], home[7], home[:, 0], home[:, 7])
        lines0[f] = corner_lines(home[0, 0], home[0, 7], home[7, 0], home[7, 7])

    def post_group(g):
        here = pl.ds(groups[g][0], len(groups[g]))
        every = (pl.ds(0, len(groups[g])),)
        out, into = outs0.at[here], ins0.at[here]
        post_lines(lines0.at[here], into, send0.at[g], recv0.at[g], every)
        post_faces(out, into, send0.at[g], recv0.at[g], every)

    def receive_group(g):
        received(ins0.at[pl.ds(groups[g][0], len(groups[g]))], recv0.at[g])

    for f in groups[0]:
        arrived_here(f)
        fill(f, faces_at)
        pack_field(f)
    loads[12].wait()
    faces, third_face = damping_faces()
    for f in groups[1]:
        if f != 3:
            arrived_here(f)
        fill(f, faces_at)
        pack_field(f)
    pl.semaphore_wait(barrier, 8)
    post_group(0)
    post_group(1)
    for home, joins in ((cz, (join_first, join_second)), (cy, (join_first,)), (cx, (join_second,))):
        for join in joins:
            join(home)

    def rates(here):
        one_over = 1.0 / scale[here]
        scale[here] = (TIME_STEP * TIME_STEP) * one_over
        keep[here] = 1.0 - TIME_STEP * keep[here] * one_over

    end_x = [jnp.where(low_x, F32(DERIVATIVE[i, 0]), F32(DERIVATIVE[i, 7])) for i in range(8)]
    end_y = [jnp.where(ey < 2, F32(DERIVATIVE[i, 0]), F32(DERIVATIVE[i, 7])) for i in range(8)]

    def fill_rows(here):
        rows = apply_eight([end_x[i] * cx[i, here] for i in range(8)], BACKWARD)
        for j in range(8):
            kx[j, here] = rows[j]
        rows = apply_eight([end_y[i] * cy[here, i] for i in range(8)], BACKWARD)
        for j in range(8):
            ky[here, j] = rows[j]

    for f in range(5):
        fill(f, inside_at)
    fill_tables()
    rates(inside)
    vf[1, 1:7, 1:7] = uf[inside] - vf[1, 1:7, 1:7]
    for c in range(1, 7, CHUNK):
        fill_rows(slice(c, c + CHUNK))

    for f in groups[2]:
        arrived_here(f)
        fill(f, faces_at)
        pack_field(f)
    post_group(2)
    for f in groups[2]:
        fill(f, inside_at)
    va[inside] = aa[8, 1:7, 1:7] - va[inside]

    def add_x(home, parts):
        for node, part in zip((0, 7), parts):
            home[node] = home[node] + part

    def add_y(home, parts):
        for node, part in zip((0, 7), parts):
            home[:, node] = home[:, node] + part

    def add_field(f):
        home = homes[f]
        parts_x = [read_x(ins0.at[f], side) for side in range(2)]
        parts_y = [read_y(ins0.at[f], side) for side in range(2)]
        add_x(home, parts_x)
        add_y(home, parts_y)
        if f == 0:
            add_x(cy, [sum_third(part) for part in parts_x])
            add_y(cx, [sum_third(part) for part in parts_y])
            for node, part in zip((0, 7), parts_x):
                first, last = join_y(part[0], part[7])
                cz[node, 0] = cz[node, 0] + (first - part[0])
                cz[node, 7] = cz[node, 7] + (last - part[7])
            for node, part in zip((0, 7), parts_y):
                first, last = join_x(part[0], part[7])
                cz[0, node] = cz[0, node] + (first - part[0])
                cz[7, node] = cz[7, node] + (last - part[7])
        for k, (ix, iy, _) in enumerate(node_d):
            home[ix, iy] = home[ix, iy] + read_line(ins0.at[f], k)

    receive_group(0)
    add_field(0)
    for c in (0, 7):
        fill_rows(slice(c, c + 1))

    put_faces(ends_out, kx[0], kx[7], ky[:, 0], ky[:, 7])
    post_faces(ends_out, ends_in, send0.at[3], recv0.at[3])
    add_field(1)

    def rest_of_setup():
        receive_group(1)
        for f in groups[1]:
            add_field(f)
        for here in face_parts:
            rates(here)
            vf[(1, *here)] = uf[here] - vf[(1, *here)]

    def times(values, which):
        high = values.astype(BF16)
        low = (values - high.astype(F32)).astype(BF16)
        both = jnp.dot(
            jnp.concatenate([high, low], axis=1), table[which], preferred_element_type=F32
        )
        return both[:, :LANES] + both[:, LANES:]

    def advance(source, gradient, v_from, u_to, v_to, between=None):
        slope = times(source[...].reshape(512, LANES), 0)
        gradient[2] = slope.reshape(8, 8, 8, LANES)
        acc[...] = times(cz[...].reshape(512, LANES) * slope, 1).reshape(8, 8, 8, LANES)
        for c in range(0, 8, CHUNK):
            here = slice(c, c + CHUNK)
            slopes = apply_eight([source[j, here] for j in range(8)], FORWARD)
            for j in range(8):
                gradient[0, j, here] = slopes[j]
            image = apply_eight([cx[j, here] * slopes[j] for j in range(8)], BACKWARD)
            image[0], image[7] = join_x(image[0], image[7])
            for j in range(8):
                acc[j, here] = acc[j, here] + image[j]
        if between is not None:
            between()
        for c in range(0, 8, CHUNK):
            here = slice(c, c + CHUNK)
            now = [source[here, j] for j in range(8)]
            slopes = apply_eight(now, FORWARD)
            for j in range(8):
                gradient[1, here, j] = slopes[j]
            image = apply_eight([cy[here, j] * slopes[j] for j in range(8)], BACKWARD)
            image[0], image[7] = join_y(image[0], image[7])
            for j in range(8):
                change = keep[here, j] * v_from[here, j] - scale[here, j] * (acc[here, j] + image[j])
                v_to[here, j] = change
                u_to[here, j] = now[j] + change

    def face_rows(u):
        along_x, along_y = kx[0] * u[0], ky[:, 0] * u[:, 0]
        for j in range(1, 8):
            along_x = along_x + kx[j] * u[j]
            along_y = along_y + ky[:, j] * u[:, j]
        return along_x, along_y

    def begin(field, turn, source, gradient, v_from, u_to, v_to, between=None):
        slot = lax.rem(turn, 2)
        out, into = outs.at[field, slot], ins.at[field, slot]
        ssem, rsem = send.at[field, slot], recv.at[field, slot]
        own_x, own_y = face_rows(source)
        put_faces(out.at[0], own_x, own_x, own_y, own_y)
        post_faces(out.at[0], into.at[0], ssem.at[0], rsem.at[0])

        def send_corners():
            for side, node in ((0, 0), (1, 7)):
                sp_x[field, side] = scale[node] * own_x
                sp_y[field, side] = scale[:, node] * own_y
            lines_x = [jnp.sum(kx[:, n] * sp_y[field, s], axis=0) for s, n in ((0, 0), (1, 7))]
            lines_y = [jnp.sum(ky[n] * sp_x[field, s], axis=0) for s, n in ((0, 0), (1, 7))]
            lines[field, slot] = -(
                jnp.where(ey == 0, lines_x[0], lines_x[1])
                + jnp.where(low_x, lines_y[0], lines_y[1])
            )
            post_lines(lines.at[field, slot], into.at[1], ssem.at[2], rsem.at[1])

        if between is None:
            send_corners()
            advance(source, gradient, v_from, u_to, v_to)
        else:

            def both():
                between()
                send_corners()

            advance(source, gradient, v_from, u_to, v_to, both)
        next_x, next_y = face_rows(u_to)
        put_faces(out.at[1], next_x, next_x, next_y, next_y)
        post_faces(out.at[1], into.at[1], ssem.at[1], rsem.at[1])

    def mend(u, v, parts_x, parts_y):
        for node, part in zip((0, 7), parts_x):
            part = scale[node] * part
            u[node] = u[node] - part
            v[node] = v[node] - part
        for node, part in zip((0, 7), parts_y):
            part = scale[:, node] * part
            u[:, node] = u[:, node] - part
            v[:, node] = v[:, node] - part

    def complete(field, turn, u, v):
        slot = lax.rem(turn, 2)
        out, into = outs.at[field, slot], ins.at[field, slot]
        sent(out.at[0], send.at[field, slot, 0])
        sent(out.at[1], send.at[field, slot, 1])
        sent(out.at[0, pl.ds(0, 4)], send.at[field, slot, 2])
        received(into.at[0, pl.ds(0, 12)], recv.at[field, slot, 0])
        parts_x = [read_x(into.at[0], side) for side in range(2)]
        mend(u, v, parts_x, [read_y(into.at[0], side) for side in range(2)])

    def finish(field, turn, source, gradient, v_from, u_to, v_to):
        slot = lax.rem(turn, 2)
        into = ins.at[field, slot, 1]
        advance(source, gradient, v_from, u_to, v_to)
        received(into, recv.at[field, slot, 1])
        parts_x, parts_y = [], []
        for s in range(2):
            part = read_x(into, s) - kn_x[s] * sp_x[field, s]
            parts_x.append(part)
            part = read_y(into, s) - kn_y[s] * sp_y[field, s]
            parts_y.append(part)
        mend(u_to, v_to, parts_x, parts_y)
        for k, (ix, iy, _) in enumerate(node_d):
            part = scale[ix, iy] * read_line(into, k)
            u_to[ix, iy] = u_to[ix, iy] - part
            v_to[ix, iy] = v_to[ix, iy] - part

    def begin_u(turn, between=None):
        n = 2 * turn + 1
        begin(0, turn, uf, gu.at[n], vf.at[n], uf, vf.at[n + 1], between)

    def begin_a(turn):
        n = 8 - 2 * turn
        begin(1, turn, aa.at[n], ga.at[n], va, aa.at[n - 1], va)

    def finish_u(turn):
        n = 2 * turn + 2
        complete(0, turn, uf, vf.at[n])
        finish(0, turn, uf, gu.at[n], vf.at[n], uf, vf.at[n + 1])

    def finish_a(turn):
        n = 7 - 2 * turn
        complete(1, turn, aa.at[n], va)
        finish(1, turn, aa.at[n], ga.at[n], va, aa.at[n - 1], va)

    begin_u(0, rest_of_setup)
    receive_group(2)
    for f in groups[2]:
        add_field(f)
    for here in face_parts:
        va[here] = aa[(8, *here)] - va[here]
    begin_a(0)
    received(ends_in, recv0.at[3])
    for side in range(2):
        kn_x[side] = read_x(ends_in, side)
        kn_y[side] = read_y(ends_in, side)
    sent(ends_out, send0.at[3])
    for g, group in enumerate(groups):
        sent(ins0.at[pl.ds(group[0], len(group))], send0.at[g])

    def cycle(turn, carry):
        finish_u(turn)
        begin_u(turn + 1)
        finish_a(turn)
        begin_a(turn + 1)
        return carry

    lax.fori_loop(0, STEPS // 2 - 1, cycle, 0)

    def density_of(ns, ix):
        total = None
        for n in ns:
            for d in range(3):
                term = gu[n, d, ix] * ga[n, d, ix]
                total = term if total is None else total + term
        return total

    def moduli_of(ns, ix):
        modulus, impedance = None, None
        for n in ns:
            now, before, after = aa[n, ix], vf[n, ix], vf[n + 1, ix]
            a, b = now * (after - before), now * (after + before)
            modulus = a if modulus is None else modulus + a
            impedance = b if impedance is None else impedance + b
        return modulus, impedance

    for ix in range(8):
        sums[0, ix] = density_of(range(2, 8), ix)
        sums[1, ix], sums[2, ix] = moduli_of(range(2, 7), ix)

    last = STEPS // 2 - 1
    finish_u(last)
    for ix in range(8):
        sums[0, ix] = sums[0, ix] + density_of((8,), ix)
        modulus, impedance = moduli_of((7, 8), ix)
        sums[1, ix] = sums[1, ix] + modulus
        sums[2, ix] = sums[2, ix] + impedance
    complete(1, last, aa.at[1], va)
    source, gradient = aa.at[1], ga.at[1]
    gradient[2] = times(source[...].reshape(512, LANES), 0).reshape(8, 8, 8, LANES)
    for c in range(0, 8, CHUNK):
        here = slice(c, c + CHUNK)
        slopes = apply_eight([source[j, here] for j in range(8)], FORWARD)
        for j in range(8):
            gradient[0, j, here] = slopes[j]
        slopes = apply_eight([source[here, j] for j in range(8)], FORWARD)
        for j in range(8):
            gradient[1, here, j] = slopes[j]

    for ix in range(8):
        density = sums[0, ix] + density_of((1,), ix)
        modulus, impedance = moduli_of((1,), ix)
        modulus = sums[1, ix] + modulus
        impedance = (sums[2, ix] + impedance) * (1.0 - keep[ix])
        for iy in range(8):
            weight = wz * float(TIME_STEP * GLL_WEIGHTS[ix] * GLL_WEIGHTS[iy])
            rows = pl.ds(iy, 8, stride=8)
            dens_ref[ix, rows, :] = weight * density[iy]
            mod_ref[ix, rows, :] = modulus[iy]
            imp_ref[ix, rows, :] = impedance[iy]
    received(ins.at[1, last % 2, 1], recv.at[1, last % 2, 1])


def deliver(*refs):
    parts, outs, sem = refs[:3], refs[3:6], refs[6]
    stores = [
        pltpu.make_async_copy(
            parts[k].at[:, pl.ds(32 * half, 32), :],
            outs[k].at[pl.ds(8 * half, 8)],
            sem.at[2 * k + half],
        )
        for k in range(3)
        for half in range(2)
    ]
    for store in stores:
        store.start()
    for store in stores:
        store.wait()


def field(*lead):
    return pltpu.VMEM((*lead, 8, 8, 8, LANES), F32)


def per_device(shape_xy, *args):
    vectors = lambda *lead: pltpu.VMEM((*lead, 8, LANES), F32)
    hbm = pl.BlockSpec(memory_space=pltpu.HBM)
    vmem = pl.BlockSpec(memory_space=pltpu.VMEM)
    operands = [pltpu.with_memory_space_constraint(a, pltpu.HBM) for a in args]
    parts = pl.pallas_call(
        functools.partial(kernel, shape_xy),
        out_shape=(pltpu.VMEM((8, 64, LANES), F32),) * 3,
        in_specs=[hbm] * 7,
        out_specs=(vmem,) * 3,
        scratch_shapes=[
            pltpu.VMEM((6, 8, 64, LANES), F32),
            pltpu.VMEM(args[6].shape, jnp.int32),
            pltpu.VMEM((2, 2 * LANES, 2 * LANES), BF16),
            field(),
            field(),
            field(),
            field(),
            field(),
            field(),
            field(),
            field(),
            field(10),
            field(9),
            field(),
            field(9, 3),
            field(9, 3),
            field(),
            vectors(2, 2, 8),
            vectors(2, 2, 8),
            vectors(2, 8),
            vectors(2, 8),
            field(3),
            vectors(7, 12),
            vectors(7),
            vectors(7, 16),
            vectors(12),
            vectors(12),
            vectors(2, 2, 2, 12),
            vectors(2, 2),
            vectors(2, 2, 2, 16),
            pltpu.SemaphoreType.DMA((13,)),
            pltpu.SemaphoreType.DMA((4,)),
            pltpu.SemaphoreType.DMA((4,)),
            pltpu.SemaphoreType.DMA((2, 2, 3)),
            pltpu.SemaphoreType.DMA((2, 2, 2)),
        ],
        compiler_params=pltpu.CompilerParams(
            collective_id=0, has_side_effects=True, vmem_limit_bytes=48 * 1024 * 1024
        ),
    )(*operands)
    return pl.pallas_call(
        deliver,
        out_shape=(pltpu.HBM(args[0].shape, F32),) * 3,
        in_specs=[pl.BlockSpec(memory_space=pl.ANY)] * 3,
        out_specs=(hbm,) * 3,
        scratch_shapes=[pltpu.SemaphoreType.DMA((6,))],
    )(*[pltpu.with_memory_space_constraint(part, pltpu.VMEM) for part in parts])


def solution(mesh):
    shape_xy = (mesh.shape["gx"], mesh.shape["gy"])
    in_specs = (P("gx", "gy", None),) * 6 + (P(None, "gx", "gy", None),)
    out_specs = (P("gx", "gy", None),) * 3
    return jax.shard_map(
        functools.partial(per_device, shape_xy),
        mesh=mesh,
        in_specs=in_specs,
        out_specs=out_specs,
        check_vma=False,
    )
```

```python
import functools

import jax
import jax.numpy as jnp
import numpy as np
from jax import lax
from jax.experimental import pallas as pl
from jax.experimental.pallas import tpu as pltpu
from jax.sharding import PartitionSpec as P

MESH = pl.DeviceIdType.MESH
F32 = jnp.float32
BF16 = jnp.bfloat16
NODES = 8
STEPS = 8
LANES = 128
CHUNK = 2

TIME_STEP = 0.01
GLL_POINTS = (
    -1.0,
    -0.8717401485096066,
    -0.5917001814331423,
    -0.2092992179024789,
    0.2092992179024789,
    0.5917001814331423,
    0.8717401485096066,
    1.0,
)
GLL_WEIGHTS = (
    0.03571428571428571,
    0.2107042271435061,
    0.3411226924835044,
    0.4124587946587038,
    0.4124587946587038,
    0.3411226924835044,
    0.2107042271435061,
    0.03571428571428571,
)


def gll_derivative():
    points = np.array(GLL_POINTS)
    previous_poly = np.ones(NODES)
    current_poly = points.copy()
    for degree in range(1, NODES - 1):
        next_poly = ((2 * degree + 1) * points * current_poly - degree * previous_poly) / (
            degree + 1
        )
        previous_poly, current_poly = (current_poly, next_poly)
    matrix = np.zeros((NODES, NODES))
    for row_index in range(NODES):
        for col_index in range(NODES):
            if row_index != col_index:
                matrix[row_index, col_index] = current_poly[row_index] / (
                    current_poly[col_index] * (points[row_index] - points[col_index])
                )
    matrix[0, 0] = -NODES * (NODES - 1) / 4.0
    matrix[NODES - 1, NODES - 1] = NODES * (NODES - 1) / 4.0
    return matrix


DERIVATIVE = gll_derivative()


def halves(matrix):
    near, far = matrix[:4, :4], matrix[:4, 7:3:-1]
    return (near - far) / 2, (near + far) / 2


FORWARD = halves(DERIVATIVE)
BACKWARD = halves(DERIVATIVE.T)


def apply_eight(values, blocks):
    odd, even = blocks
    sums = [values[j] + values[7 - j] for j in range(4)]
    diffs = [values[j] - values[7 - j] for j in range(4)]
    low, high = [], []
    for i in range(4):
        a = diffs[0] * float(odd[i, 0])
        b = sums[0] * float(even[i, 0])
        for j in range(1, 4):
            a = a + diffs[j] * float(odd[i, j])
            b = b + sums[j] * float(even[i, j])
        low.append(a + b)
        high.append(a - b)
    return low + high[::-1]


def roll_sub(values, shift):
    shift %= 8
    return values if shift == 0 else pltpu.roll(values, shift, values.ndim - 2)


def kernel(
    shape_xy,
    up_ref,
    uc_ref,
    an_ref,
    ac_ref,
    im_ref,
    id_ref,
    fm_ref,
    dens_ref,
    mod_ref,
    imp_ref,
    nat,
    mask,
    table,
    cx,
    cy,
    cz,
    scale,
    keep,
    kx,
    ky,
    uf,
    vf,
    aa,
    va,
    gu,
    ga,
    acc,
    sp_x,
    sp_y,
    kn_x,
    kn_y,
    sums,
    outs0,
    lines0,
    ins0,
    ends_out,
    ends_in,
    outs,
    lines,
    ins,
    in_sem,
    send0,
    recv0,
    send,
    recv,
):
    count_x, count_y = shape_xy
    gx, gy = lax.axis_index("gx"), lax.axis_index("gy")

    in_x = {0: gx > 0, 1: gx < count_x - 1}
    in_y = {0: gy > 0, 1: gy < count_y - 1}
    other_x = gx + 1 - 2 * lax.rem(gx, 2)
    other_y = gy + 1 - 2 * lax.rem(gy, 2)

    def target_x(side):
        here = in_x[side]
        step = 2 * side - 1
        device = (jnp.where(here, gx + step, gx), jnp.where(here, gy, other_y))
        return device, jnp.where(here, 1 - side, side)

    def target_y(side):
        here = in_y[side]
        step = 2 * side - 1
        device = (jnp.where(here, gx, other_x), jnp.where(here, gy + step, gy))
        return device, jnp.where(here, 1 - side, side)

    def target_d(side_x, side_y):
        hx, hy = in_x[side_x], in_y[side_y]
        both_out = jnp.logical_not(jnp.logical_or(hx, hy))
        dx = jnp.where(both_out, count_x - 1 - gx, jnp.where(hx, gx + 2 * side_x - 1, gx))
        dy = jnp.where(hy, gy + 2 * side_y - 1, gy)
        slot_x = jnp.where(jnp.logical_or(hx, both_out), 1 - side_x, side_x)
        slot_y = jnp.where(hy, 1 - side_y, side_y)
        return (dx, dy), slot_x * 2 + slot_y

    targets_x = [target_x(0), target_x(1)]
    targets_y = [target_y(0), target_y(1)]
    targets_d = [target_d(0, 0), target_d(0, 1), target_d(1, 0), target_d(1, 1)]

    barrier = pltpu.get_barrier_semaphore()
    for device, _ in targets_d + targets_y + targets_x:
        pl.semaphore_signal(barrier, inc=1, device_id=device, device_id_type=MESH)

    loads = []
    for k, ref in enumerate((id_ref, uc_ref, im_ref, up_ref, ac_ref, an_ref)):
        for half in range(2):
            loads.append(
                pltpu.make_async_copy(
                    ref.at[pl.ds(8 * half, 8)],
                    nat.at[k, :, pl.ds(32 * half, 32), :],
                    in_sem.at[2 * k + half],
                )
            )
    loads.append(pltpu.make_async_copy(fm_ref, mask, in_sem.at[12]))
    for load in loads:
        load.start()

    sub = lax.broadcasted_iota(jnp.int32, (8, LANES), 0)
    lane = lax.broadcasted_iota(jnp.int32, (8, LANES), 1)
    ey = sub % 4
    low_x = sub < 4
    zplace = lane % 8
    z_low = jnp.logical_and(zplace == 0, lane > 0)
    z_high = jnp.logical_and(zplace == 7, lane < LANES - 1)
    zero = jnp.zeros((8, LANES), F32)
    wz = zero
    for j in range(NODES):
        wz = jnp.where(zplace == j, F32(GLL_WEIGHTS[j]), wz)

    def sum_third(values):
        before = pltpu.roll(values, 1, values.ndim - 1)
        after = pltpu.roll(values, LANES - 1, values.ndim - 1)
        return values + jnp.where(z_low, before, jnp.where(z_high, after, 0.0))

    def one_if(flag):
        return jnp.where(flag, 1, 0)

    halo_x = [sub < 4 * one_if(in_x[0]), sub >= 8 - 4 * one_if(in_x[1])]
    halo_y = [ey < one_if(in_y[0]), ey >= 4 - one_if(in_y[1])]
    halo_d = [
        jnp.logical_and(halo_x[0], halo_y[0]),
        jnp.logical_and(halo_x[0], halo_y[1]),
        jnp.logical_and(halo_x[1], halo_y[0]),
        jnp.logical_and(halo_x[1], halo_y[1]),
    ]
    node_d = ((0, 0, 1), (0, 7, -1), (7, 0, 1), (7, 7, -1))

    def join_x(first, last):
        return (
            first + jnp.where(low_x, 0.0, roll_sub(last, 4)),
            last + jnp.where(low_x, roll_sub(first, 4), 0.0),
        )

    def join_y(first, last):
        return (
            first + jnp.where(ey == 0, 0.0, roll_sub(last, 1)),
            last + jnp.where(ey == 3, 0.0, roll_sub(first, 7)),
        )

    def pack_x(first, last):
        return (
            jnp.where(low_x, first[0:4], roll_sub(first[4:8], 4)),
            jnp.where(low_x, roll_sub(last[0:4], 4), last[4:8]),
        )

    def unpack_x(side, packed):
        turned = roll_sub(packed, 4)
        pair = [packed, turned] if side == 0 else [turned, packed]
        return jnp.concatenate(pair, axis=0)

    def pack_y(first, last):
        first = first.reshape(2, 4, 8, LANES)
        last = last.reshape(2, 4, 8, LANES)
        low, high = first[:, 0], roll_sub(last[:, 0], 5)
        for j in range(1, 4):
            low = jnp.where(ey == j, roll_sub(first[:, j], j), low)
            high = jnp.where(ey == j, roll_sub(last[:, j], 5 + j), high)
        return low, high

    def unpack_y(side, packed):
        rows = [roll_sub(packed, 3 * side - j) for j in range(4)]
        return jnp.stack(rows, axis=1).reshape(8, 8, LANES)

    def corner_lines(n00, n07, n70, n77):
        return jnp.where(low_x, jnp.where(ey == 0, n00, n07), jnp.where(ey == 0, n70, n77))

    def copy(src, dst, ssem, rsem, device):
        return pltpu.make_async_remote_copy(
            src_ref=src,
            dst_ref=dst,
            send_sem=ssem,
            recv_sem=rsem,
            device_id=device,
            device_id_type=MESH,
        )

    def post_faces(out, into, ssem, rsem, lead=()):
        for side, (device, slot) in enumerate(targets_y):
            src, dst = out.at[(*lead, pl.ds(8 + 2 * side, 2))], into.at[(*lead, pl.ds(8 + 2 * slot, 2))]
            copy(src, dst, ssem, rsem, device).start()
        for side, (device, slot) in enumerate(targets_x):
            src, dst = out.at[(*lead, pl.ds(4 * side, 4))], into.at[(*lead, pl.ds(4 * slot, 4))]
            copy(src, dst, ssem, rsem, device).start()

    def post_lines(line, into, ssem, rsem, lead=()):
        for device, slot in targets_d:
            copy(line, into.at[(*lead, 12 + slot)], ssem, rsem, device).start()

    def received(into, rsem):
        copy(into, into, rsem, rsem, targets_x[0][0]).wait_recv()

    def sent(out, ssem):
        copy(out, out, ssem, ssem, targets_x[0][0]).wait_send()

    def put_faces(out, fx0, fx1, fy0, fy1):
        out[0:4], out[4:8] = pack_x(fx0, fx1)
        out[8:10], out[10:12] = pack_y(fy0, fy1)

    def read_x(into, side):
        return jnp.where(halo_x[side], unpack_x(side, into[4 * side : 4 * side + 4]), 0.0)

    def read_y(into, side):
        return jnp.where(halo_y[side], unpack_y(side, into[8 + 2 * side : 10 + 2 * side]), 0.0)

    def read_line(into, k):
        return jnp.where(halo_d[k], roll_sub(into[12 + k], node_d[k][2]), 0.0)

    homes = (cz, uf, scale, keep, vf.at[1], aa.at[8], va)
    places = (0, 1, 2, None, 3, 4, 5)
    groups = ((0, 1), (2, 3, 4), (5, 6))

    def natural(k, ix, iy):
        return nat[k, ix, pl.ds(iy, 8, stride=8), :]

    half_x = [jnp.where(jnp.logical_or(halo_x[0], jnp.logical_not(low_x)), 0.5, 1.0), 1.0]
    half_x_high = jnp.where(jnp.logical_or(halo_x[1], low_x), 0.5, 1.0)
    half_y_low = jnp.where(jnp.logical_or(halo_y[0], ey != 0), 0.5, 1.0)
    half_y_high = jnp.where(jnp.logical_or(halo_y[1], ey != 3), 0.5, 1.0)
    half_z = jnp.where(jnp.logical_or(z_low, z_high), 0.5, 1.0)

    def share(ix, iy):
        value = half_z
        if ix == 0:
            value = value * half_x[0]
        if ix == 7:
            value = value * half_x_high
        if iy == 0:
            value = value * half_y_low
        if iy == 7:
            value = value * half_y_high
        return value

    def fill_tables():
        tiles = [zero, zero]
        for i in range(8):
            for j in range(8):
                value = F32(DERIVATIVE[i, j])
                tiles[0] = jnp.where(jnp.logical_and(sub == j, zplace == i), value, tiles[0])
                tiles[1] = jnp.where(jnp.logical_and(sub == i, zplace == j), value, tiles[1])
        for which in range(2):
            rows = [jnp.where(lane // 8 == k, tiles[which], 0.0) for k in range(LANES // 8)]
            if which == 1:
                rows = [sum_third(row) for row in rows]
            block = jnp.concatenate(rows, axis=0)
            high = block.astype(BF16)
            low = (block - high.astype(F32)).astype(BF16)
            for half in range(2):
                here = slice(LANES * half, LANES * half + LANES)
                table[which, here, :LANES] = high
                table[which, here, LANES:] = low

    faces_at = [(ix, iy) for ix in range(8) for iy in range(8) if ix in (0, 7) or iy in (0, 7)]
    inside_at = [(ix, iy) for ix in range(1, 7) for iy in range(1, 7)]
    face_parts = ((0,), (7,), (slice(1, 7), 0), (slice(1, 7), 7))
    inside = (slice(1, 7), slice(1, 7))

    def arrived_here(f):
        for load in loads[2 * places[f] : 2 * places[f] + 2]:
            load.wait()

    def fill(f, nodes):
        for ix, iy in nodes:
            weight = float(GLL_WEIGHTS[ix] * GLL_WEIGHTS[iy])
            if f == 0:
                raw = natural(0, ix, iy) * (wz * weight)
                summed = sum_third(raw)
                cz[ix, iy] = raw
                cx[ix, iy] = summed
                cy[ix, iy] = summed
            elif f == 2:
                scale[ix, iy] = sum_third(natural(2, ix, iy) * (wz * weight))
            elif f == 3:
                value = third_face * weight
                if ix == 0:
                    value = value + faces[0] * float(GLL_WEIGHTS[iy])
                if ix == 7:
                    value = value + faces[1] * float(GLL_WEIGHTS[iy])
                if iy == 0:
                    value = value + faces[2] * float(GLL_WEIGHTS[ix])
                if iy == 7:
                    value = value + faces[3] * float(GLL_WEIGHTS[ix])
                keep[ix, iy] = value
            else:
                homes[f][ix, iy] = sum_third(natural(places[f], ix, iy) * share(ix, iy))

    def damping_faces():
        spread = jnp.where(
            lax.broadcasted_iota(jnp.int32, (16, LANES), 1) // 8
            == lax.broadcasted_iota(jnp.int32, (16, LANES), 0),
            1.0,
            0.0,
        ).astype(F32)
        cells = [
            jnp.dot(
                jnp.concatenate([mask[f, 0], mask[f, 1]], axis=0).astype(F32),
                spread,
                preferred_element_type=F32,
            )
            for f in range(6)
        ]
        ends = jnp.where(zplace == 0, cells[4], jnp.where(zplace == 7, cells[5], 0.0))
        return [sum_third(wz * cell) for cell in cells[:4]], sum_third(ends)

    def join_first(home):
        first, last = join_x(home[0], home[7])
        home[0] = first
        home[7] = last

    def join_second(home):
        first, last = join_y(home[:, 0], home[:, 7])
        home[:, 0] = first
        home[:, 7] = last

    def pack_field(f):
        home = homes[f]
        if f > 0:
            join_first(home)
            join_second(home)
        put_faces(outs0.at[f], home[0], home[7], home[:, 0], home[:, 7])
        lines0[f] = corner_lines(home[0, 0], home[0, 7], home[7, 0], home[7, 7])

    def post_group(g):
        here = pl.ds(groups[g][0], len(groups[g]))
        every = (pl.ds(0, len(groups[g])),)
        out, into = outs0.at[here], ins0.at[here]
        post_lines(lines0.at[here], into, send0.at[g], recv0.at[g], every)
        post_faces(out, into, send0.at[g], recv0.at[g], every)

    def receive_group(g):
        received(ins0.at[pl.ds(groups[g][0], len(groups[g]))], recv0.at[g])

    for f in groups[0]:
        arrived_here(f)
        fill(f, faces_at)
        pack_field(f)
    loads[12].wait()
    faces, third_face = damping_faces()
    for f in groups[1]:
        if f != 3:
            arrived_here(f)
        fill(f, faces_at)
        pack_field(f)
    pl.semaphore_wait(barrier, 8)
    post_group(0)
    post_group(1)
    for home, joins in ((cz, (join_first, join_second)), (cy, (join_first,)), (cx, (join_second,))):
        for join in joins:
            join(home)

    def rates(here):
        one_over = 1.0 / scale[here]
        scale[here] = (TIME_STEP * TIME_STEP) * one_over
        keep[here] = 1.0 - TIME_STEP * keep[here] * one_over

    end_x = [jnp.where(low_x, F32(DERIVATIVE[i, 0]), F32(DERIVATIVE[i, 7])) for i in range(8)]
    end_y = [jnp.where(ey < 2, F32(DERIVATIVE[i, 0]), F32(DERIVATIVE[i, 7])) for i in range(8)]

    def fill_rows(here):
        rows = apply_eight([end_x[i] * cx[i, here] for i in range(8)], BACKWARD)
        for j in range(8):
            kx[j, here] = rows[j]
        rows = apply_eight([end_y[i] * cy[here, i] for i in range(8)], BACKWARD)
        for j in range(8):
            ky[here, j] = rows[j]

    for f in range(5):
        fill(f, inside_at)
    fill_tables()
    rates(inside)
    vf[1, 1:7, 1:7] = uf[inside] - vf[1, 1:7, 1:7]
    for c in range(1, 7, CHUNK):
        fill_rows(slice(c, c + CHUNK))

    for f in groups[2]:
        arrived_here(f)
        fill(f, faces_at)
        pack_field(f)
    post_group(2)
    for f in groups[2]:
        fill(f, inside_at)
    va[inside] = aa[8, 1:7, 1:7] - va[inside]

    def add_x(home, parts):
        for node, part in zip((0, 7), parts):
            home[node] = home[node] + part

    def add_y(home, parts):
        for node, part in zip((0, 7), parts):
            home[:, node] = home[:, node] + part

    def add_field(f):
        home = homes[f]
        parts_x = [read_x(ins0.at[f], side) for side in range(2)]
        parts_y = [read_y(ins0.at[f], side) for side in range(2)]
        add_x(home, parts_x)
        add_y(home, parts_y)
        if f == 0:
            add_x(cy, [sum_third(part) for part in parts_x])
            add_y(cx, [sum_third(part) for part in parts_y])
            for node, part in zip((0, 7), parts_x):
                first, last = join_y(part[0], part[7])
                cz[node, 0] = cz[node, 0] + (first - part[0])
                cz[node, 7] = cz[node, 7] + (last - part[7])
            for node, part in zip((0, 7), parts_y):
                first, last = join_x(part[0], part[7])
                cz[0, node] = cz[0, node] + (first - part[0])
                cz[7, node] = cz[7, node] + (last - part[7])
        for k, (ix, iy, _) in enumerate(node_d):
            home[ix, iy] = home[ix, iy] + read_line(ins0.at[f], k)

    receive_group(0)
    add_field(0)
    for c in (0, 7):
        fill_rows(slice(c, c + 1))

    put_faces(ends_out, kx[0], kx[7], ky[:, 0], ky[:, 7])
    post_faces(ends_out, ends_in, send0.at[3], recv0.at[3])
    add_field(1)

    def rest_of_setup():
        receive_group(1)
        for f in groups[1]:
            add_field(f)
        for here in face_parts:
            rates(here)
            vf[(1, *here)] = uf[here] - vf[(1, *here)]

    def times(values, which):
        high = values.astype(BF16)
        low = (values - high.astype(F32)).astype(BF16)
        both = jnp.dot(
            jnp.concatenate([high, low], axis=1), table[which], preferred_element_type=F32
        )
        return both[:, :LANES] + both[:, LANES:]

    def advance(source, gradient, v_from, u_to, v_to, between=None):
        slope = times(source[...].reshape(512, LANES), 0)
        gradient[2] = slope.reshape(8, 8, 8, LANES)
        acc[...] = times(cz[...].reshape(512, LANES) * slope, 1).reshape(8, 8, 8, LANES)
        for c in range(0, 8, CHUNK):
            here = slice(c, c + CHUNK)
            slopes = apply_eight([source[j, here] for j in range(8)], FORWARD)
            for j in range(8):
                gradient[0, j, here] = slopes[j]
            image = apply_eight([cx[j, here] * slopes[j] for j in range(8)], BACKWARD)
            image[0], image[7] = join_x(image[0], image[7])
            for j in range(8):
                acc[j, here] = acc[j, here] + image[j]
        if between is not None:
            between()
        for c in range(0, 8, CHUNK):
            here = slice(c, c + CHUNK)
            now = [source[here, j] for j in range(8)]
            slopes = apply_eight(now, FORWARD)
            for j in range(8):
                gradient[1, here, j] = slopes[j]
            image = apply_eight([cy[here, j] * slopes[j] for j in range(8)], BACKWARD)
            image[0], image[7] = join_y(image[0], image[7])
            for j in range(8):
                change = keep[here, j] * v_from[here, j] - scale[here, j] * (acc[here, j] + image[j])
                v_to[here, j] = change
                u_to[here, j] = now[j] + change

    def face_rows(u):
        along_x, along_y = kx[0] * u[0], ky[:, 0] * u[:, 0]
        for j in range(1, 8):
            along_x = along_x + kx[j] * u[j]
            along_y = along_y + ky[:, j] * u[:, j]
        return along_x, along_y

    def begin(field, turn, source, gradient, v_from, u_to, v_to, between=None):
        slot = lax.rem(turn, 2)
        out, into = outs.at[field, slot], ins.at[field, slot]
        ssem, rsem = send.at[field, slot], recv.at[field, slot]

        def if_needed(post):
            if field == 0 or isinstance(turn, int):
                post()
            else:
                pl.when(turn < STEPS // 2 - 1)(post)

        own_x, own_y = face_rows(source)
        put_faces(out.at[0], own_x, own_x, own_y, own_y)
        post_faces(out.at[0], into.at[0], ssem.at[0], rsem.at[0])

        def send_corners():
            for side, node in ((0, 0), (1, 7)):
                sp_x[field, side] = scale[node] * own_x
                sp_y[field, side] = scale[:, node] * own_y
            lines_x = [jnp.sum(kx[:, n] * sp_y[field, s], axis=0) for s, n in ((0, 0), (1, 7))]
            lines_y = [jnp.sum(ky[n] * sp_x[field, s], axis=0) for s, n in ((0, 0), (1, 7))]
            lines[field, slot] = -(
                jnp.where(ey == 0, lines_x[0], lines_x[1])
                + jnp.where(low_x, lines_y[0], lines_y[1])
            )

            @if_needed
            def _():
                post_lines(lines.at[field, slot], into.at[1], ssem.at[2], rsem.at[1])

        if between is None:
            send_corners()
            advance(source, gradient, v_from, u_to, v_to)
        else:

            def both():
                between()
                send_corners()

            advance(source, gradient, v_from, u_to, v_to, both)

        @if_needed
        def _():
            next_x, next_y = face_rows(u_to)
            put_faces(out.at[1], next_x, next_x, next_y, next_y)
            post_faces(out.at[1], into.at[1], ssem.at[1], rsem.at[1])

    def mend(u, v, parts_x, parts_y):
        for node, part in zip((0, 7), parts_x):
            part = scale[node] * part
            u[node] = u[node] - part
            v[node] = v[node] - part
        for node, part in zip((0, 7), parts_y):
            part = scale[:, node] * part
            u[:, node] = u[:, node] - part
            v[:, node] = v[:, node] - part

    def complete(field, turn, u, v, second=True):
        slot = lax.rem(turn, 2)
        out, into = outs.at[field, slot], ins.at[field, slot]
        sent(out.at[0], send.at[field, slot, 0])
        if second:
            sent(out.at[1], send.at[field, slot, 1])
            sent(out.at[0, pl.ds(0, 4)], send.at[field, slot, 2])
        received(into.at[0, pl.ds(0, 12)], recv.at[field, slot, 0])
        parts_x = [read_x(into.at[0], side) for side in range(2)]
        mend(u, v, parts_x, [read_y(into.at[0], side) for side in range(2)])

    def finish(field, turn, source, gradient, v_from, u_to, v_to):
        slot = lax.rem(turn, 2)
        into = ins.at[field, slot, 1]
        advance(source, gradient, v_from, u_to, v_to)
        received(into, recv.at[field, slot, 1])
        parts_x, parts_y = [], []
        for s in range(2):
            part = read_x(into, s) - kn_x[s] * sp_x[field, s]
            parts_x.append(part)
            part = read_y(into, s) - kn_y[s] * sp_y[field, s]
            parts_y.append(part)
        mend(u_to, v_to, parts_x, parts_y)
        for k, (ix, iy, _) in enumerate(node_d):
            part = scale[ix, iy] * read_line(into, k)
            u_to[ix, iy] = u_to[ix, iy] - part
            v_to[ix, iy] = v_to[ix, iy] - part

    def begin_u(turn, between=None):
        n = 2 * turn + 1
        begin(0, turn, uf, gu.at[n], vf.at[n], uf, vf.at[n + 1], between)

    def begin_a(turn):
        n = 8 - 2 * turn
        begin(1, turn, aa.at[n], ga.at[n], va, aa.at[n - 1], va)

    def finish_u(turn):
        n = 2 * turn + 2
        complete(0, turn, uf, vf.at[n])
        finish(0, turn, uf, gu.at[n], vf.at[n], uf, vf.at[n + 1])

    def finish_a(turn):
        n = 7 - 2 * turn
        complete(1, turn, aa.at[n], va)
        finish(1, turn, aa.at[n], ga.at[n], va, aa.at[n - 1], va)

    begin_u(0, rest_of_setup)
    receive_group(2)
    for f in groups[2]:
        add_field(f)
    for here in face_parts:
        va[here] = aa[(8, *here)] - va[here]
    begin_a(0)
    received(ends_in, recv0.at[3])
    for side in range(2):
        kn_x[side] = read_x(ends_in, side)
        kn_y[side] = read_y(ends_in, side)
    sent(ends_out, send0.at[3])
    for g, group in enumerate(groups):
        sent(ins0.at[pl.ds(group[0], len(group))], send0.at[g])

    def cycle(turn, carry):
        finish_u(turn)
        begin_u(turn + 1)
        finish_a(turn)
        begin_a(turn + 1)
        return carry

    lax.fori_loop(0, STEPS // 2 - 1, cycle, 0)

    def density_of(ns, ix):
        total = None
        for n in ns:
            for d in range(3):
                term = gu[n, d, ix] * ga[n, d, ix]
                total = term if total is None else total + term
        return total

    def moduli_of(ns, ix):
        modulus, impedance = None, None
        for n in ns:
            now, before, after = aa[n, ix], vf[n, ix], vf[n + 1, ix]
            a, b = now * (after - before), now * (after + before)
            modulus = a if modulus is None else modulus + a
            impedance = b if impedance is None else impedance + b
        return modulus, impedance

    for ix in range(8):
        sums[0, ix] = density_of(range(2, 8), ix)
        sums[1, ix], sums[2, ix] = moduli_of(range(2, 7), ix)

    last = STEPS // 2 - 1
    finish_u(last)
    for ix in range(8):
        sums[0, ix] = sums[0, ix] + density_of((8,), ix)
        modulus, impedance = moduli_of((7, 8), ix)
        sums[1, ix] = sums[1, ix] + modulus
        sums[2, ix] = sums[2, ix] + impedance
    complete(1, last, aa.at[1], va, second=False)
    source, gradient = aa.at[1], ga.at[1]
    gradient[2] = times(source[...].reshape(512, LANES), 0).reshape(8, 8, 8, LANES)
    for c in range(0, 8, CHUNK):
        here = slice(c, c + CHUNK)
        slopes = apply_eight([source[j, here] for j in range(8)], FORWARD)
        for j in range(8):
            gradient[0, j, here] = slopes[j]
        slopes = apply_eight([source[here, j] for j in range(8)], FORWARD)
        for j in range(8):
            gradient[1, here, j] = slopes[j]

    for ix in range(8):
        density = sums[0, ix] + density_of((1,), ix)
        modulus, impedance = moduli_of((1,), ix)
        modulus = sums[1, ix] + modulus
        impedance = (sums[2, ix] + impedance) * (1.0 - keep[ix])
        for iy in range(8):
            weight = wz * float(TIME_STEP * GLL_WEIGHTS[ix] * GLL_WEIGHTS[iy])
            rows = pl.ds(iy, 8, stride=8)
            dens_ref[ix, rows, :] = weight * density[iy]
            mod_ref[ix, rows, :] = modulus[iy]
            imp_ref[ix, rows, :] = impedance[iy]


def deliver(*refs):
    parts, outs, sem = refs[:3], refs[3:6], refs[6]
    stores = [
        pltpu.make_async_copy(
            parts[k].at[:, pl.ds(32 * half, 32), :],
            outs[k].at[pl.ds(8 * half, 8)],
            sem.at[2 * k + half],
        )
        for k in range(3)
        for half in range(2)
    ]
    for store in stores:
        store.start()
    for store in stores:
        store.wait()


def field(*lead):
    return pltpu.VMEM((*lead, 8, 8, 8, LANES), F32)


def per_device(shape_xy, *args):
    vectors = lambda *lead: pltpu.VMEM((*lead, 8, LANES), F32)
    hbm = pl.BlockSpec(memory_space=pltpu.HBM)
    vmem = pl.BlockSpec(memory_space=pltpu.VMEM)
    operands = [pltpu.with_memory_space_constraint(a, pltpu.HBM) for a in args]
    parts = pl.pallas_call(
        functools.partial(kernel, shape_xy),
        out_shape=(pltpu.VMEM((8, 64, LANES), F32),) * 3,
        in_specs=[hbm] * 7,
        out_specs=(vmem,) * 3,
        scratch_shapes=[
            pltpu.VMEM((6, 8, 64, LANES), F32),
            pltpu.VMEM(args[6].shape, jnp.int32),
            pltpu.VMEM((2, 2 * LANES, 2 * LANES), BF16),
            field(),
            field(),
            field(),
            field(),
            field(),
            field(),
            field(),
            field(),
            field(10),
            field(9),
            field(),
            field(9, 3),
            field(9, 3),
            field(),
            vectors(2, 2, 8),
            vectors(2, 2, 8),
            vectors(2, 8),
            vectors(2, 8),
            field(3),
            vectors(7, 12),
            vectors(7),
            vectors(7, 16),
            vectors(12),
            vectors(12),
            vectors(2, 2, 2, 12),
            vectors(2, 2),
            vectors(2, 2, 2, 16),
            pltpu.SemaphoreType.DMA((13,)),
            pltpu.SemaphoreType.DMA((4,)),
            pltpu.SemaphoreType.DMA((4,)),
            pltpu.SemaphoreType.DMA((2, 2, 3)),
            pltpu.SemaphoreType.DMA((2, 2, 2)),
        ],
        compiler_params=pltpu.CompilerParams(
            collective_id=0, has_side_effects=True, vmem_limit_bytes=48 * 1024 * 1024
        ),
    )(*operands)
    return pl.pallas_call(
        deliver,
        out_shape=(pltpu.HBM(args[0].shape, F32),) * 3,
        in_specs=[pl.BlockSpec(memory_space=pl.ANY)] * 3,
        out_specs=(hbm,) * 3,
        scratch_shapes=[pltpu.SemaphoreType.DMA((6,))],
    )(*[pltpu.with_memory_space_constraint(part, pltpu.VMEM) for part in parts])


def solution(mesh):
    shape_xy = (mesh.shape["gx"], mesh.shape["gy"])
    in_specs = (P("gx", "gy", None),) * 6 + (P(None, "gx", "gy", None),)
    out_specs = (P("gx", "gy", None),) * 3
    return jax.shard_map(
        functools.partial(per_device, shape_xy),
        mesh=mesh,
        in_specs=in_specs,
        out_specs=out_specs,
        check_vma=False,
    )
```

```python
import functools

import jax
import jax.numpy as jnp
import numpy as np
from jax import lax
from jax.experimental import pallas as pl
from jax.experimental.pallas import tpu as pltpu
from jax.sharding import PartitionSpec as P

MESH = pl.DeviceIdType.MESH
F32 = jnp.float32
BF16 = jnp.bfloat16
NODES = 8
STEPS = 8
LANES = 128
CHUNK = 2

TIME_STEP = 0.01
GLL_POINTS = (
    -1.0,
    -0.8717401485096066,
    -0.5917001814331423,
    -0.2092992179024789,
    0.2092992179024789,
    0.5917001814331423,
    0.8717401485096066,
    1.0,
)
GLL_WEIGHTS = (
    0.03571428571428571,
    0.2107042271435061,
    0.3411226924835044,
    0.4124587946587038,
    0.4124587946587038,
    0.3411226924835044,
    0.2107042271435061,
    0.03571428571428571,
)


def gll_derivative():
    points = np.array(GLL_POINTS)
    previous_poly = np.ones(NODES)
    current_poly = points.copy()
    for degree in range(1, NODES - 1):
        next_poly = ((2 * degree + 1) * points * current_poly - degree * previous_poly) / (
            degree + 1
        )
        previous_poly, current_poly = (current_poly, next_poly)
    matrix = np.zeros((NODES, NODES))
    for row_index in range(NODES):
        for col_index in range(NODES):
            if row_index != col_index:
                matrix[row_index, col_index] = current_poly[row_index] / (
                    current_poly[col_index] * (points[row_index] - points[col_index])
                )
    matrix[0, 0] = -NODES * (NODES - 1) / 4.0
    matrix[NODES - 1, NODES - 1] = NODES * (NODES - 1) / 4.0
    return matrix


DERIVATIVE = gll_derivative()


def halves(matrix):
    near, far = matrix[:4, :4], matrix[:4, 7:3:-1]
    return (near - far) / 2, (near + far) / 2


FORWARD = halves(DERIVATIVE)
BACKWARD = halves(DERIVATIVE.T)


def apply_eight(values, blocks):
    odd, even = blocks
    sums = [values[j] + values[7 - j] for j in range(4)]
    diffs = [values[j] - values[7 - j] for j in range(4)]
    low, high = [], []
    for i in range(4):
        a = diffs[0] * float(odd[i, 0])
        b = sums[0] * float(even[i, 0])
        for j in range(1, 4):
            a = a + diffs[j] * float(odd[i, j])
            b = b + sums[j] * float(even[i, j])
        low.append(a + b)
        high.append(a - b)
    return low + high[::-1]


def roll_sub(values, shift):
    shift %= 8
    return values if shift == 0 else pltpu.roll(values, shift, values.ndim - 2)


def kernel(
    shape_xy,
    up_ref,
    uc_ref,
    an_ref,
    ac_ref,
    im_ref,
    id_ref,
    fm_ref,
    dens_ref,
    mod_ref,
    imp_ref,
    nat,
    mask,
    table,
    cx,
    cy,
    cz,
    scale,
    keep,
    kx,
    ky,
    uf,
    vf,
    aa,
    va,
    gu,
    ga,
    acc,
    sp_x,
    sp_y,
    kn_x,
    kn_y,
    sums,
    outs0,
    lines0,
    ins0,
    ends_out,
    ends_in,
    outs,
    lines,
    ins,
    in_sem,
    send0,
    recv0,
    send,
    recv,
):
    count_x, count_y = shape_xy
    gx, gy = lax.axis_index("gx"), lax.axis_index("gy")

    in_x = {0: gx > 0, 1: gx < count_x - 1}
    in_y = {0: gy > 0, 1: gy < count_y - 1}
    other_x = gx + 1 - 2 * lax.rem(gx, 2)
    other_y = gy + 1 - 2 * lax.rem(gy, 2)

    def target_x(side):
        here = in_x[side]
        step = 2 * side - 1
        device = (jnp.where(here, gx + step, gx), jnp.where(here, gy, other_y))
        return device, jnp.where(here, 1 - side, side)

    def target_y(side):
        here = in_y[side]
        step = 2 * side - 1
        device = (jnp.where(here, gx, other_x), jnp.where(here, gy + step, gy))
        return device, jnp.where(here, 1 - side, side)

    def target_d(side_x, side_y):
        hx, hy = in_x[side_x], in_y[side_y]
        both_out = jnp.logical_not(jnp.logical_or(hx, hy))
        dx = jnp.where(both_out, count_x - 1 - gx, jnp.where(hx, gx + 2 * side_x - 1, gx))
        dy = jnp.where(hy, gy + 2 * side_y - 1, gy)
        slot_x = jnp.where(jnp.logical_or(hx, both_out), 1 - side_x, side_x)
        slot_y = jnp.where(hy, 1 - side_y, side_y)
        return (dx, dy), slot_x * 2 + slot_y

    targets_x = [target_x(0), target_x(1)]
    targets_y = [target_y(0), target_y(1)]
    targets_d = [target_d(0, 0), target_d(0, 1), target_d(1, 0), target_d(1, 1)]

    barrier = pltpu.get_barrier_semaphore()
    for device, _ in targets_d + targets_y + targets_x:
        pl.semaphore_signal(barrier, inc=1, device_id=device, device_id_type=MESH)

    loads = []
    for k, ref in enumerate((id_ref, uc_ref, im_ref, up_ref, ac_ref, an_ref)):
        for half in range(2):
            loads.append(
                pltpu.make_async_copy(
                    ref.at[pl.ds(8 * half, 8)],
                    nat.at[k, :, pl.ds(32 * half, 32), :],
                    in_sem.at[2 * k + half],
                )
            )
    loads.append(pltpu.make_async_copy(fm_ref, mask, in_sem.at[12]))
    for load in loads:
        load.start()

    sub = lax.broadcasted_iota(jnp.int32, (8, LANES), 0)
    lane = lax.broadcasted_iota(jnp.int32, (8, LANES), 1)
    ey = sub % 4
    low_x = sub < 4
    zplace = lane % 8
    z_low = jnp.logical_and(zplace == 0, lane > 0)
    z_high = jnp.logical_and(zplace == 7, lane < LANES - 1)
    zero = jnp.zeros((8, LANES), F32)
    wz = zero
    for j in range(NODES):
        wz = jnp.where(zplace == j, F32(GLL_WEIGHTS[j]), wz)

    def sum_third(values):
        before = pltpu.roll(values, 1, values.ndim - 1)
        after = pltpu.roll(values, LANES - 1, values.ndim - 1)
        return values + jnp.where(z_low, before, jnp.where(z_high, after, 0.0))

    def one_if(flag):
        return jnp.where(flag, 1, 0)

    halo_x = [sub < 4 * one_if(in_x[0]), sub >= 8 - 4 * one_if(in_x[1])]
    halo_y = [ey < one_if(in_y[0]), ey >= 4 - one_if(in_y[1])]
    halo_d = [
        jnp.logical_and(halo_x[0], halo_y[0]),
        jnp.logical_and(halo_x[0], halo_y[1]),
        jnp.logical_and(halo_x[1], halo_y[0]),
        jnp.logical_and(halo_x[1], halo_y[1]),
    ]
    node_d = ((0, 0, 1), (0, 7, -1), (7, 0, 1), (7, 7, -1))

    def join_x(first, last):
        return (
            first + jnp.where(low_x, 0.0, roll_sub(last, 4)),
            last + jnp.where(low_x, roll_sub(first, 4), 0.0),
        )

    def join_y(first, last):
        return (
            first + jnp.where(ey == 0, 0.0, roll_sub(last, 1)),
            last + jnp.where(ey == 3, 0.0, roll_sub(first, 7)),
        )

    def pack_x(first, last):
        return (
            jnp.where(low_x, first[0:4], roll_sub(first[4:8], 4)),
            jnp.where(low_x, roll_sub(last[0:4], 4), last[4:8]),
        )

    def unpack_x(side, packed):
        turned = roll_sub(packed, 4)
        pair = [packed, turned] if side == 0 else [turned, packed]
        return jnp.concatenate(pair, axis=0)

    def pack_y(first, last):
        first = first.reshape(2, 4, 8, LANES)
        last = last.reshape(2, 4, 8, LANES)
        low, high = first[:, 0], roll_sub(last[:, 0], 5)
        for j in range(1, 4):
            low = jnp.where(ey == j, roll_sub(first[:, j], j), low)
            high = jnp.where(ey == j, roll_sub(last[:, j], 5 + j), high)
        return low, high

    def unpack_y(side, packed):
        rows = [roll_sub(packed, 3 * side - j) for j in range(4)]
        return jnp.stack(rows, axis=1).reshape(8, 8, LANES)

    def corner_lines(n00, n07, n70, n77):
        return jnp.where(low_x, jnp.where(ey == 0, n00, n07), jnp.where(ey == 0, n70, n77))

    def copy(src, dst, ssem, rsem, device):
        return pltpu.make_async_remote_copy(
            src_ref=src,
            dst_ref=dst,
            send_sem=ssem,
            recv_sem=rsem,
            device_id=device,
            device_id_type=MESH,
        )

    def post_faces(out, into, ssem, rsem, lead=()):
        for side, (device, slot) in enumerate(targets_y):
            src, dst = out.at[(*lead, pl.ds(8 + 2 * side, 2))], into.at[(*lead, pl.ds(8 + 2 * slot, 2))]
            copy(src, dst, ssem, rsem, device).start()
        for side, (device, slot) in enumerate(targets_x):
            src, dst = out.at[(*lead, pl.ds(4 * side, 4))], into.at[(*lead, pl.ds(4 * slot, 4))]
            copy(src, dst, ssem, rsem, device).start()

    def post_lines(line, into, ssem, rsem, lead=()):
        for row, (device, slot) in zip((0, 3, 4, 7), targets_d):
            src = line.at[(*lead, pl.ds(row, 1))]
            dst = into.at[(*lead, 12 + slot, pl.ds(row, 1))]
            copy(src, dst, ssem, rsem, device).start()

    def received(into, rsem):
        copy(into, into, rsem, rsem, targets_x[0][0]).wait_recv()

    def sent(out, ssem):
        copy(out, out, ssem, ssem, targets_x[0][0]).wait_send()

    def put_faces(out, fx0, fx1, fy0, fy1):
        out[0:4], out[4:8] = pack_x(fx0, fx1)
        out[8:10], out[10:12] = pack_y(fy0, fy1)

    def read_x(into, side):
        return jnp.where(halo_x[side], unpack_x(side, into[4 * side : 4 * side + 4]), 0.0)

    def read_y(into, side):
        return jnp.where(halo_y[side], unpack_y(side, into[8 + 2 * side : 10 + 2 * side]), 0.0)

    def read_line(into, k):
        return jnp.where(halo_d[k], roll_sub(into[12 + k], node_d[k][2]), 0.0)

    homes = (cz, uf, scale, keep, vf.at[1], aa.at[8], va)
    places = (0, 1, 2, None, 3, 4, 5)
    groups = ((0, 1), (2, 3, 4), (5, 6))

    def natural(k, ix, iy):
        return nat[k, ix, pl.ds(iy, 8, stride=8), :]

    half_x = [jnp.where(jnp.logical_or(halo_x[0], jnp.logical_not(low_x)), 0.5, 1.0), 1.0]
    half_x_high = jnp.where(jnp.logical_or(halo_x[1], low_x), 0.5, 1.0)
    half_y_low = jnp.where(jnp.logical_or(halo_y[0], ey != 0), 0.5, 1.0)
    half_y_high = jnp.where(jnp.logical_or(halo_y[1], ey != 3), 0.5, 1.0)
    half_z = jnp.where(jnp.logical_or(z_low, z_high), 0.5, 1.0)

    def share(ix, iy):
        value = half_z
        if ix == 0:
            value = value * half_x[0]
        if ix == 7:
            value = value * half_x_high
        if iy == 0:
            value = value * half_y_low
        if iy == 7:
            value = value * half_y_high
        return value

    def fill_tables():
        tiles = [zero, zero]
        for i in range(8):
            for j in range(8):
                value = F32(DERIVATIVE[i, j])
                tiles[0] = jnp.where(jnp.logical_and(sub == j, zplace == i), value, tiles[0])
                tiles[1] = jnp.where(jnp.logical_and(sub == i, zplace == j), value, tiles[1])
        for which in range(2):
            rows = [jnp.where(lane // 8 == k, tiles[which], 0.0) for k in range(LANES // 8)]
            if which == 1:
                rows = [sum_third(row) for row in rows]
            block = jnp.concatenate(rows, axis=0)
            high = block.astype(BF16)
            low = (block - high.astype(F32)).astype(BF16)
            for half in range(2):
                here = slice(LANES * half, LANES * half + LANES)
                table[which, here, :LANES] = high
                table[which, here, LANES:] = low

    faces_at = [(ix, iy) for ix in range(8) for iy in range(8) if ix in (0, 7) or iy in (0, 7)]
    inside_at = [(ix, iy) for ix in range(1, 7) for iy in range(1, 7)]
    face_parts = ((0,), (7,), (slice(1, 7), 0), (slice(1, 7), 7))
    inside = (slice(1, 7), slice(1, 7))

    def arrived_here(f):
        for load in loads[2 * places[f] : 2 * places[f] + 2]:
            load.wait()

    def fill(f, nodes):
        for ix, iy in nodes:
            weight = float(GLL_WEIGHTS[ix] * GLL_WEIGHTS[iy])
            if f == 0:
                raw = natural(0, ix, iy) * (wz * weight)
                summed = sum_third(raw)
                cz[ix, iy] = raw
                cx[ix, iy] = summed
                cy[ix, iy] = summed
            elif f == 2:
                scale[ix, iy] = sum_third(natural(2, ix, iy) * (wz * weight))
            elif f == 3:
                value = third_face * weight
                if ix == 0:
                    value = value + faces[0] * float(GLL_WEIGHTS[iy])
                if ix == 7:
                    value = value + faces[1] * float(GLL_WEIGHTS[iy])
                if iy == 0:
                    value = value + faces[2] * float(GLL_WEIGHTS[ix])
                if iy == 7:
                    value = value + faces[3] * float(GLL_WEIGHTS[ix])
                keep[ix, iy] = value
            else:
                homes[f][ix, iy] = sum_third(natural(places[f], ix, iy) * share(ix, iy))

    def damping_faces():
        spread = jnp.where(
            lax.broadcasted_iota(jnp.int32, (16, LANES), 1) // 8
            == lax.broadcasted_iota(jnp.int32, (16, LANES), 0),
            1.0,
            0.0,
        ).astype(F32)
        cells = [
            jnp.dot(
                jnp.concatenate([mask[f, 0], mask[f, 1]], axis=0).astype(F32),
                spread,
                preferred_element_type=F32,
            )
            for f in range(6)
        ]
        ends = jnp.where(zplace == 0, cells[4], jnp.where(zplace == 7, cells[5], 0.0))
        return [sum_third(wz * cell) for cell in cells[:4]], sum_third(ends)

    def join_first(home):
        first, last = join_x(home[0], home[7])
        home[0] = first
        home[7] = last

    def join_second(home):
        first, last = join_y(home[:, 0], home[:, 7])
        home[:, 0] = first
        home[:, 7] = last

    def pack_field(f):
        home = homes[f]
        if f > 0:
            join_first(home)
            join_second(home)
        put_faces(outs0.at[f], home[0], home[7], home[:, 0], home[:, 7])
        lines0[f] = corner_lines(home[0, 0], home[0, 7], home[7, 0], home[7, 7])

    def post_group(g):
        here = pl.ds(groups[g][0], len(groups[g]))
        every = (pl.ds(0, len(groups[g])),)
        out, into = outs0.at[here], ins0.at[here]
        post_lines(lines0.at[here], into, send0.at[4 + g], recv0.at[4 + g], every)
        post_faces(out, into, send0.at[g], recv0.at[g], every)

    def receive_group(g):
        here = pl.ds(groups[g][0], len(groups[g]))
        received(ins0.at[here, pl.ds(0, 12)], recv0.at[g])
        received(lines0.at[here, pl.ds(0, 4)], recv0.at[4 + g])

    for f in groups[0]:
        arrived_here(f)
        fill(f, faces_at)
        pack_field(f)
    pl.semaphore_wait(barrier, 8)
    post_group(0)
    loads[12].wait()
    faces, third_face = damping_faces()
    for f in groups[1]:
        if f != 3:
            arrived_here(f)
        fill(f, faces_at)
        pack_field(f)
    post_group(1)
    for home, joins in ((cz, (join_first, join_second)), (cy, (join_first,)), (cx, (join_second,))):
        for join in joins:
            join(home)

    def rates(here):
        one_over = 1.0 / scale[here]
        scale[here] = (TIME_STEP * TIME_STEP) * one_over
        keep[here] = 1.0 - TIME_STEP * keep[here] * one_over

    end_x = [jnp.where(low_x, F32(DERIVATIVE[i, 0]), F32(DERIVATIVE[i, 7])) for i in range(8)]
    end_y = [jnp.where(ey < 2, F32(DERIVATIVE[i, 0]), F32(DERIVATIVE[i, 7])) for i in range(8)]

    def fill_rows(here):
        rows = apply_eight([end_x[i] * cx[i, here] for i in range(8)], BACKWARD)
        for j in range(8):
            kx[j, here] = rows[j]
        rows = apply_eight([end_y[i] * cy[here, i] for i in range(8)], BACKWARD)
        for j in range(8):
            ky[here, j] = rows[j]

    for f in range(5):
        fill(f, inside_at)
    fill_tables()
    rates(inside)
    vf[1, 1:7, 1:7] = uf[inside] - vf[1, 1:7, 1:7]
    for c in range(1, 7, CHUNK):
        fill_rows(slice(c, c + CHUNK))

    for f in groups[2]:
        arrived_here(f)
        fill(f, faces_at)
        pack_field(f)
    post_group(2)
    for f in groups[2]:
        fill(f, inside_at)
    va[inside] = aa[8, 1:7, 1:7] - va[inside]

    def add_x(home, parts):
        for node, part in zip((0, 7), parts):
            home[node] = home[node] + part

    def add_y(home, parts):
        for node, part in zip((0, 7), parts):
            home[:, node] = home[:, node] + part

    def add_field(f):
        home = homes[f]
        parts_x = [read_x(ins0.at[f], side) for side in range(2)]
        parts_y = [read_y(ins0.at[f], side) for side in range(2)]
        add_x(home, parts_x)
        add_y(home, parts_y)
        if f == 0:
            add_x(cy, [sum_third(part) for part in parts_x])
            add_y(cx, [sum_third(part) for part in parts_y])
            for node, part in zip((0, 7), parts_x):
                first, last = join_y(part[0], part[7])
                cz[node, 0] = cz[node, 0] + (first - part[0])
                cz[node, 7] = cz[node, 7] + (last - part[7])
            for node, part in zip((0, 7), parts_y):
                first, last = join_x(part[0], part[7])
                cz[0, node] = cz[0, node] + (first - part[0])
                cz[7, node] = cz[7, node] + (last - part[7])
        for k, (ix, iy, _) in enumerate(node_d):
            home[ix, iy] = home[ix, iy] + read_line(ins0.at[f], k)

    receive_group(0)
    add_field(0)
    for c in (0, 7):
        fill_rows(slice(c, c + 1))

    add_field(1)

    def rest_of_setup():
        put_faces(ends_out, kx[0], kx[7], ky[:, 0], ky[:, 7])
        post_faces(ends_out, ends_in, send0.at[3], recv0.at[3])
        receive_group(1)
        for f in groups[1]:
            add_field(f)
        for here in face_parts:
            rates(here)
            vf[(1, *here)] = uf[here] - vf[(1, *here)]

    def times(values, which):
        high = values.astype(BF16)
        low = (values - high.astype(F32)).astype(BF16)
        both = jnp.dot(
            jnp.concatenate([high, low], axis=1), table[which], preferred_element_type=F32
        )
        return both[:, :LANES] + both[:, LANES:]

    def advance(source, gradient, v_from, u_to, v_to, between=None):
        slope = times(source[...].reshape(512, LANES), 0)
        gradient[2] = slope.reshape(8, 8, 8, LANES)
        acc[...] = times(cz[...].reshape(512, LANES) * slope, 1).reshape(8, 8, 8, LANES)
        for c in range(0, 8, CHUNK):
            here = slice(c, c + CHUNK)
            slopes = apply_eight([source[j, here] for j in range(8)], FORWARD)
            for j in range(8):
                gradient[0, j, here] = slopes[j]
            image = apply_eight([cx[j, here] * slopes[j] for j in range(8)], BACKWARD)
            image[0], image[7] = join_x(image[0], image[7])
            for j in range(8):
                acc[j, here] = acc[j, here] + image[j]
        if between is not None:
            between()
        for c in range(0, 8, CHUNK):
            here = slice(c, c + CHUNK)
            now = [source[here, j] for j in range(8)]
            slopes = apply_eight(now, FORWARD)
            for j in range(8):
                gradient[1, here, j] = slopes[j]
            image = apply_eight([cy[here, j] * slopes[j] for j in range(8)], BACKWARD)
            image[0], image[7] = join_y(image[0], image[7])
            for j in range(8):
                change = keep[here, j] * v_from[here, j] - scale[here, j] * (acc[here, j] + image[j])
                v_to[here, j] = change
                u_to[here, j] = now[j] + change

    def face_rows(u):
        along_x, along_y = kx[0] * u[0], ky[:, 0] * u[:, 0]
        for j in range(1, 8):
            along_x = along_x + kx[j] * u[j]
            along_y = along_y + ky[:, j] * u[:, j]
        return along_x, along_y

    def begin(field, turn, source, gradient, v_from, u_to, v_to, between=None):
        slot = lax.rem(turn, 2)
        out, into = outs.at[field, slot], ins.at[field, slot]
        ssem, rsem = send.at[field, slot], recv.at[field, slot]

        def if_needed(post):
            if field == 0 or isinstance(turn, int):
                post()
            else:
                pl.when(turn < STEPS // 2 - 1)(post)

        own_x, own_y = face_rows(source)
        put_faces(out.at[0], own_x, own_x, own_y, own_y)
        post_faces(out.at[0], into.at[0], ssem.at[0], rsem.at[0])

        def send_corners():
            for side, node in ((0, 0), (1, 7)):
                sp_x[field, side] = scale[node] * own_x
                sp_y[field, side] = scale[:, node] * own_y
            lines_x = [jnp.sum(kx[:, n] * sp_y[field, s], axis=0) for s, n in ((0, 0), (1, 7))]
            lines_y = [jnp.sum(ky[n] * sp_x[field, s], axis=0) for s, n in ((0, 0), (1, 7))]
            lines[field, slot] = -(
                jnp.where(ey == 0, lines_x[0], lines_x[1])
                + jnp.where(low_x, lines_y[0], lines_y[1])
            )

            @if_needed
            def _():
                post_lines(lines.at[field, slot], into.at[1], ssem.at[2], rsem.at[2])

        if between is None:
            send_corners()
            advance(source, gradient, v_from, u_to, v_to)
        else:

            def both():
                between()
                send_corners()

            advance(source, gradient, v_from, u_to, v_to, both)

        @if_needed
        def _():
            next_x, next_y = face_rows(u_to)
            put_faces(out.at[1], next_x, next_x, next_y, next_y)
            post_faces(out.at[1], into.at[1], ssem.at[1], rsem.at[1])

    def mend(u, v, parts_x, parts_y):
        for node, part in zip((0, 7), parts_x):
            part = scale[node] * part
            u[node] = u[node] - part
            v[node] = v[node] - part
        for node, part in zip((0, 7), parts_y):
            part = scale[:, node] * part
            u[:, node] = u[:, node] - part
            v[:, node] = v[:, node] - part

    def complete(field, turn, u, v, second=True):
        slot = lax.rem(turn, 2)
        out, into = outs.at[field, slot], ins.at[field, slot]
        sent(out.at[0], send.at[field, slot, 0])
        if second:
            sent(out.at[1], send.at[field, slot, 1])
            sent(lines.at[field, slot, pl.ds(0, 4)], send.at[field, slot, 2])
        received(into.at[0, pl.ds(0, 12)], recv.at[field, slot, 0])
        parts_x = [read_x(into.at[0], side) for side in range(2)]
        mend(u, v, parts_x, [read_y(into.at[0], side) for side in range(2)])

    def finish(field, turn, source, gradient, v_from, u_to, v_to):
        slot = lax.rem(turn, 2)
        into = ins.at[field, slot, 1]
        advance(source, gradient, v_from, u_to, v_to)
        received(into.at[pl.ds(0, 12)], recv.at[field, slot, 1])
        parts_x, parts_y = [], []
        for s in range(2):
            part = read_x(into, s) - kn_x[s] * sp_x[field, s]
            parts_x.append(part)
            part = read_y(into, s) - kn_y[s] * sp_y[field, s]
            parts_y.append(part)
        mend(u_to, v_to, parts_x, parts_y)
        received(lines.at[field, slot, pl.ds(0, 4)], recv.at[field, slot, 2])
        for k, (ix, iy, _) in enumerate(node_d):
            part = scale[ix, iy] * read_line(into, k)
            u_to[ix, iy] = u_to[ix, iy] - part
            v_to[ix, iy] = v_to[ix, iy] - part

    def begin_u(turn, between=None):
        n = 2 * turn + 1
        begin(0, turn, uf, gu.at[n], vf.at[n], uf, vf.at[n + 1], between)

    def begin_a(turn):
        n = 8 - 2 * turn
        begin(1, turn, aa.at[n], ga.at[n], va, aa.at[n - 1], va)

    def finish_u(turn):
        n = 2 * turn + 2
        complete(0, turn, uf, vf.at[n])
        finish(0, turn, uf, gu.at[n], vf.at[n], uf, vf.at[n + 1])

    def finish_a(turn):
        n = 7 - 2 * turn
        complete(1, turn, aa.at[n], va)
        finish(1, turn, aa.at[n], ga.at[n], va, aa.at[n - 1], va)

    begin_u(0, rest_of_setup)
    receive_group(2)
    for f in groups[2]:
        add_field(f)
    for here in face_parts:
        va[here] = aa[(8, *here)] - va[here]
    begin_a(0)
    received(ends_in, recv0.at[3])
    for side in range(2):
        kn_x[side] = read_x(ends_in, side)
        kn_y[side] = read_y(ends_in, side)
    sent(ends_out, send0.at[3])
    for g, group in enumerate(groups):
        here = pl.ds(group[0], len(group))
        sent(outs0.at[here], send0.at[g])
        sent(lines0.at[here, pl.ds(0, 4)], send0.at[4 + g])

    def cycle(turn, carry):
        finish_u(turn)
        begin_u(turn + 1)
        finish_a(turn)
        begin_a(turn + 1)
        return carry

    lax.fori_loop(0, STEPS // 2 - 1, cycle, 0)

    def density_of(ns, ix):
        total = None
        for n in ns:
            for d in range(3):
                term = gu[n, d, ix] * ga[n, d, ix]
                total = term if total is None else total + term
        return total

    def moduli_of(ns, ix):
        modulus, impedance = None, None
        for n in ns:
            now, before, after = aa[n, ix], vf[n, ix], vf[n + 1, ix]
            a, b = now * (after - before), now * (after + before)
            modulus = a if modulus is None else modulus + a
            impedance = b if impedance is None else impedance + b
        return modulus, impedance

    for ix in range(8):
        sums[0, ix] = density_of(range(2, 8), ix)
        sums[1, ix], sums[2, ix] = moduli_of(range(2, 7), ix)

    last = STEPS // 2 - 1
    finish_u(last)
    for ix in range(8):
        sums[0, ix] = sums[0, ix] + density_of((8,), ix)
        modulus, impedance = moduli_of((7, 8), ix)
        sums[1, ix] = sums[1, ix] + modulus
        sums[2, ix] = sums[2, ix] + impedance
    complete(1, last, aa.at[1], va, second=False)
    source, gradient = aa.at[1], ga.at[1]
    gradient[2] = times(source[...].reshape(512, LANES), 0).reshape(8, 8, 8, LANES)
    for c in range(0, 8, CHUNK):
        here = slice(c, c + CHUNK)
        slopes = apply_eight([source[j, here] for j in range(8)], FORWARD)
        for j in range(8):
            gradient[0, j, here] = slopes[j]
        slopes = apply_eight([source[here, j] for j in range(8)], FORWARD)
        for j in range(8):
            gradient[1, here, j] = slopes[j]

    for ix in range(8):
        density = sums[0, ix] + density_of((1,), ix)
        modulus, impedance = moduli_of((1,), ix)
        modulus = sums[1, ix] + modulus
        impedance = (sums[2, ix] + impedance) * (1.0 - keep[ix])
        for iy in range(8):
            weight = wz * float(TIME_STEP * GLL_WEIGHTS[ix] * GLL_WEIGHTS[iy])
            rows = pl.ds(iy, 8, stride=8)
            dens_ref[ix, rows, :] = weight * density[iy]
            mod_ref[ix, rows, :] = modulus[iy]
            imp_ref[ix, rows, :] = impedance[iy]


def deliver(*refs):
    parts, outs, sem = refs[:3], refs[3:6], refs[6]
    stores = [
        pltpu.make_async_copy(
            parts[k].at[:, pl.ds(32 * half, 32), :],
            outs[k].at[pl.ds(8 * half, 8)],
            sem.at[2 * k + half],
        )
        for k in range(3)
        for half in range(2)
    ]
    for store in stores:
        store.start()
    for store in stores:
        store.wait()


def field(*lead):
    return pltpu.VMEM((*lead, 8, 8, 8, LANES), F32)


def per_device(shape_xy, *args):
    vectors = lambda *lead: pltpu.VMEM((*lead, 8, LANES), F32)
    hbm = pl.BlockSpec(memory_space=pltpu.HBM)
    vmem = pl.BlockSpec(memory_space=pltpu.VMEM)
    operands = [pltpu.with_memory_space_constraint(a, pltpu.HBM) for a in args]
    parts = pl.pallas_call(
        functools.partial(kernel, shape_xy),
        out_shape=(pltpu.VMEM((8, 64, LANES), F32),) * 3,
        in_specs=[hbm] * 7,
        out_specs=(vmem,) * 3,
        scratch_shapes=[
            pltpu.VMEM((6, 8, 64, LANES), F32),
            pltpu.VMEM(args[6].shape, jnp.int32),
            pltpu.VMEM((2, 2 * LANES, 2 * LANES), BF16),
            field(),
            field(),
            field(),
            field(),
            field(),
            field(),
            field(),
            field(),
            field(10),
            field(9),
            field(),
            field(9, 3),
            field(9, 3),
            field(),
            vectors(2, 2, 8),
            vectors(2, 2, 8),
            vectors(2, 8),
            vectors(2, 8),
            field(3),
            vectors(7, 12),
            vectors(7),
            vectors(7, 16),
            vectors(12),
            vectors(12),
            vectors(2, 2, 2, 12),
            vectors(2, 2),
            vectors(2, 2, 2, 16),
            pltpu.SemaphoreType.DMA((13,)),
            pltpu.SemaphoreType.DMA((7,)),
            pltpu.SemaphoreType.DMA((7,)),
            pltpu.SemaphoreType.DMA((2, 2, 3)),
            pltpu.SemaphoreType.DMA((2, 2, 3)),
        ],
        compiler_params=pltpu.CompilerParams(
            collective_id=0, has_side_effects=True, vmem_limit_bytes=48 * 1024 * 1024
        ),
    )(*operands)
    return pl.pallas_call(
        deliver,
        out_shape=(pltpu.HBM(args[0].shape, F32),) * 3,
        in_specs=[pl.BlockSpec(memory_space=pl.ANY)] * 3,
        out_specs=(hbm,) * 3,
        scratch_shapes=[pltpu.SemaphoreType.DMA((6,))],
    )(*[pltpu.with_memory_space_constraint(part, pltpu.VMEM) for part in parts])


def solution(mesh):
    shape_xy = (mesh.shape["gx"], mesh.shape["gy"])
    in_specs = (P("gx", "gy", None),) * 6 + (P(None, "gx", "gy", None),)
    out_specs = (P("gx", "gy", None),) * 3
    return jax.shard_map(
        functools.partial(per_device, shape_xy),
        mesh=mesh,
        in_specs=in_specs,
        out_specs=out_specs,
        check_vma=False,
    )
```

```python
import functools

import jax
import jax.numpy as jnp
import numpy as np
from jax import lax
from jax.experimental import pallas as pl
from jax.experimental.pallas import tpu as pltpu
from jax.sharding import PartitionSpec as P

MESH = pl.DeviceIdType.MESH
F32 = jnp.float32
BF16 = jnp.bfloat16
NODES = 8
STEPS = 8
LANES = 128
CHUNK = 2

TIME_STEP = 0.01
GLL_POINTS = (
    -1.0,
    -0.8717401485096066,
    -0.5917001814331423,
    -0.2092992179024789,
    0.2092992179024789,
    0.5917001814331423,
    0.8717401485096066,
    1.0,
)
GLL_WEIGHTS = (
    0.03571428571428571,
    0.2107042271435061,
    0.3411226924835044,
    0.4124587946587038,
    0.4124587946587038,
    0.3411226924835044,
    0.2107042271435061,
    0.03571428571428571,
)


def gll_derivative():
    points = np.array(GLL_POINTS)
    previous_poly = np.ones(NODES)
    current_poly = points.copy()
    for degree in range(1, NODES - 1):
        next_poly = ((2 * degree + 1) * points * current_poly - degree * previous_poly) / (
            degree + 1
        )
        previous_poly, current_poly = (current_poly, next_poly)
    matrix = np.zeros((NODES, NODES))
    for row_index in range(NODES):
        for col_index in range(NODES):
            if row_index != col_index:
                matrix[row_index, col_index] = current_poly[row_index] / (
                    current_poly[col_index] * (points[row_index] - points[col_index])
                )
    matrix[0, 0] = -NODES * (NODES - 1) / 4.0
    matrix[NODES - 1, NODES - 1] = NODES * (NODES - 1) / 4.0
    return matrix


DERIVATIVE = gll_derivative()


def halves(matrix):
    near, far = matrix[:4, :4], matrix[:4, 7:3:-1]
    return (near - far) / 2, (near + far) / 2


FORWARD = halves(DERIVATIVE)
BACKWARD = halves(DERIVATIVE.T)


def apply_eight(values, blocks):
    odd, even = blocks
    sums = [values[j] + values[7 - j] for j in range(4)]
    diffs = [values[j] - values[7 - j] for j in range(4)]
    low, high = [], []
    for i in range(4):
        a = diffs[0] * float(odd[i, 0])
        b = sums[0] * float(even[i, 0])
        for j in range(1, 4):
            a = a + diffs[j] * float(odd[i, j])
            b = b + sums[j] * float(even[i, j])
        low.append(a + b)
        high.append(a - b)
    return low + high[::-1]


def roll_sub(values, shift):
    shift %= 8
    return values if shift == 0 else pltpu.roll(values, shift, values.ndim - 2)


def kernel(
    shape_xy,
    up_ref,
    uc_ref,
    an_ref,
    ac_ref,
    im_ref,
    id_ref,
    fm_ref,
    dens_ref,
    mod_ref,
    imp_ref,
    nat,
    mask,
    table,
    cx,
    cy,
    cz,
    scale,
    keep,
    kx,
    ky,
    uf,
    vf,
    aa,
    va,
    gu,
    ga,
    acc,
    sp_x,
    sp_y,
    kn_x,
    kn_y,
    sums,
    outs0,
    lines0,
    ins0,
    ends_out,
    ends_in,
    outs,
    lines,
    ins,
    in_sem,
    send0,
    recv0,
    send,
    recv,
):
    count_x, count_y = shape_xy
    gx, gy = lax.axis_index("gx"), lax.axis_index("gy")

    in_x = {0: gx > 0, 1: gx < count_x - 1}
    in_y = {0: gy > 0, 1: gy < count_y - 1}
    other_x = gx + 1 - 2 * lax.rem(gx, 2)
    other_y = gy + 1 - 2 * lax.rem(gy, 2)

    def target_x(side):
        here = in_x[side]
        step = 2 * side - 1
        device = (jnp.where(here, gx + step, gx), jnp.where(here, gy, other_y))
        return device, jnp.where(here, 1 - side, side)

    def target_y(side):
        here = in_y[side]
        step = 2 * side - 1
        device = (jnp.where(here, gx, other_x), jnp.where(here, gy + step, gy))
        return device, jnp.where(here, 1 - side, side)

    def target_d(side_x, side_y):
        hx, hy = in_x[side_x], in_y[side_y]
        both_out = jnp.logical_not(jnp.logical_or(hx, hy))
        dx = jnp.where(both_out, count_x - 1 - gx, jnp.where(hx, gx + 2 * side_x - 1, gx))
        dy = jnp.where(hy, gy + 2 * side_y - 1, gy)
        slot_x = jnp.where(jnp.logical_or(hx, both_out), 1 - side_x, side_x)
        slot_y = jnp.where(hy, 1 - side_y, side_y)
        return (dx, dy), slot_x * 2 + slot_y

    targets_x = [target_x(0), target_x(1)]
    targets_y = [target_y(0), target_y(1)]
    targets_d = [target_d(0, 0), target_d(0, 1), target_d(1, 0), target_d(1, 1)]

    barrier = pltpu.get_barrier_semaphore()
    for device, _ in targets_d + targets_y + targets_x:
        pl.semaphore_signal(barrier, inc=1, device_id=device, device_id_type=MESH)

    loads = []
    for k, ref in enumerate((id_ref, uc_ref, im_ref, up_ref, ac_ref, an_ref)):
        for half in range(2):
            loads.append(
                pltpu.make_async_copy(
                    ref.at[pl.ds(8 * half, 8)],
                    nat.at[k, :, pl.ds(32 * half, 32), :],
                    in_sem.at[2 * k + half],
                )
            )
    loads.append(pltpu.make_async_copy(fm_ref, mask, in_sem.at[12]))
    for load in loads:
        load.start()

    sub = lax.broadcasted_iota(jnp.int32, (8, LANES), 0)
    lane = lax.broadcasted_iota(jnp.int32, (8, LANES), 1)
    ey = sub % 4
    low_x = sub < 4
    zplace = lane % 8
    z_low = jnp.logical_and(zplace == 0, lane > 0)
    z_high = jnp.logical_and(zplace == 7, lane < LANES - 1)
    zero = jnp.zeros((8, LANES), F32)
    wz = zero
    for j in range(NODES):
        wz = jnp.where(zplace == j, F32(GLL_WEIGHTS[j]), wz)

    def sum_third(values):
        before = pltpu.roll(values, 1, values.ndim - 1)
        after = pltpu.roll(values, LANES - 1, values.ndim - 1)
        return values + jnp.where(z_low, before, jnp.where(z_high, after, 0.0))

    def one_if(flag):
        return jnp.where(flag, 1, 0)

    halo_x = [sub < 4 * one_if(in_x[0]), sub >= 8 - 4 * one_if(in_x[1])]
    halo_y = [ey < one_if(in_y[0]), ey >= 4 - one_if(in_y[1])]
    halo_d = [
        jnp.logical_and(halo_x[0], halo_y[0]),
        jnp.logical_and(halo_x[0], halo_y[1]),
        jnp.logical_and(halo_x[1], halo_y[0]),
        jnp.logical_and(halo_x[1], halo_y[1]),
    ]
    node_d = ((0, 0, 1), (0, 7, -1), (7, 0, 1), (7, 7, -1))

    def join_x(first, last):
        return (
            first + jnp.where(low_x, 0.0, roll_sub(last, 4)),
            last + jnp.where(low_x, roll_sub(first, 4), 0.0),
        )

    def join_y(first, last):
        return (
            first + jnp.where(ey == 0, 0.0, roll_sub(last, 1)),
            last + jnp.where(ey == 3, 0.0, roll_sub(first, 7)),
        )

    def pack_x(first, last):
        return (
            jnp.where(low_x, first[0:4], roll_sub(first[4:8], 4)),
            jnp.where(low_x, roll_sub(last[0:4], 4), last[4:8]),
        )

    def unpack_x(side, packed):
        turned = roll_sub(packed, 4)
        pair = [packed, turned] if side == 0 else [turned, packed]
        return jnp.concatenate(pair, axis=0)

    def pack_y(first, last):
        first = first.reshape(2, 4, 8, LANES)
        last = last.reshape(2, 4, 8, LANES)
        low, high = first[:, 0], roll_sub(last[:, 0], 5)
        for j in range(1, 4):
            low = jnp.where(ey == j, roll_sub(first[:, j], j), low)
            high = jnp.where(ey == j, roll_sub(last[:, j], 5 + j), high)
        return low, high

    def unpack_y(side, packed):
        rows = [roll_sub(packed, 3 * side - j) for j in range(4)]
        return jnp.stack(rows, axis=1).reshape(8, 8, LANES)

    def corner_lines(n00, n07, n70, n77):
        return jnp.where(low_x, jnp.where(ey == 0, n00, n07), jnp.where(ey == 0, n70, n77))

    def copy(src, dst, ssem, rsem, device):
        return pltpu.make_async_remote_copy(
            src_ref=src,
            dst_ref=dst,
            send_sem=ssem,
            recv_sem=rsem,
            device_id=device,
            device_id_type=MESH,
        )

    def post_faces(out, into, ssem, rsem, lead=()):
        for side, (device, slot) in enumerate(targets_y):
            src, dst = out.at[(*lead, pl.ds(8 + 2 * side, 2))], into.at[(*lead, pl.ds(8 + 2 * slot, 2))]
            copy(src, dst, ssem, rsem, device).start()
        for side, (device, slot) in enumerate(targets_x):
            src, dst = out.at[(*lead, pl.ds(4 * side, 4))], into.at[(*lead, pl.ds(4 * slot, 4))]
            copy(src, dst, ssem, rsem, device).start()

    def post_lines(line, into, ssem, rsem, lead=()):
        for row, (device, slot) in zip((0, 3, 4, 7), targets_d):
            src = line.at[(*lead, pl.ds(row, 1))]
            dst = into.at[(*lead, 12 + slot, pl.ds(row, 1))]
            copy(src, dst, ssem, rsem, device).start()

    def received(into, rsem):
        copy(into, into, rsem, rsem, targets_x[0][0]).wait_recv()

    def sent(out, ssem):
        copy(out, out, ssem, ssem, targets_x[0][0]).wait_send()

    def put_faces(out, fx0, fx1, fy0, fy1):
        out[0:4], out[4:8] = pack_x(fx0, fx1)
        out[8:10], out[10:12] = pack_y(fy0, fy1)

    def read_x(into, side):
        return jnp.where(halo_x[side], unpack_x(side, into[4 * side : 4 * side + 4]), 0.0)

    def read_y(into, side):
        return jnp.where(halo_y[side], unpack_y(side, into[8 + 2 * side : 10 + 2 * side]), 0.0)

    def read_line(into, k):
        return jnp.where(halo_d[k], roll_sub(into[12 + k], node_d[k][2]), 0.0)

    homes = (cz, uf, scale, keep, vf.at[1], aa.at[8], va)
    places = (0, 1, 2, None, 3, 4, 5)
    groups = ((0, 1), (2, 3, 4), (5, 6))

    def natural(k, ix, iy):
        return nat[k, ix, pl.ds(iy, 8, stride=8), :]

    half_x = [jnp.where(jnp.logical_or(halo_x[0], jnp.logical_not(low_x)), 0.5, 1.0), 1.0]
    half_x_high = jnp.where(jnp.logical_or(halo_x[1], low_x), 0.5, 1.0)
    half_y_low = jnp.where(jnp.logical_or(halo_y[0], ey != 0), 0.5, 1.0)
    half_y_high = jnp.where(jnp.logical_or(halo_y[1], ey != 3), 0.5, 1.0)
    half_z = jnp.where(jnp.logical_or(z_low, z_high), 0.5, 1.0)

    def share(ix, iy):
        value = half_z
        if ix == 0:
            value = value * half_x[0]
        if ix == 7:
            value = value * half_x_high
        if iy == 0:
            value = value * half_y_low
        if iy == 7:
            value = value * half_y_high
        return value

    def fill_tables():
        tiles = [zero, zero]
        for i in range(8):
            for j in range(8):
                value = F32(DERIVATIVE[i, j])
                tiles[0] = jnp.where(jnp.logical_and(sub == j, zplace == i), value, tiles[0])
                tiles[1] = jnp.where(jnp.logical_and(sub == i, zplace == j), value, tiles[1])
        for which in range(2):
            rows = [jnp.where(lane // 8 == k, tiles[which], 0.0) for k in range(LANES // 8)]
            if which == 1:
                rows = [sum_third(row) for row in rows]
            block = jnp.concatenate(rows, axis=0)
            high = block.astype(BF16)
            low = (block - high.astype(F32)).astype(BF16)
            for half in range(2):
                here = slice(LANES * half, LANES * half + LANES)
                table[which, here, :LANES] = high
                table[which, here, LANES:] = low

    faces_at = [(ix, iy) for ix in range(8) for iy in range(8) if ix in (0, 7) or iy in (0, 7)]
    inside_at = [(ix, iy) for ix in range(1, 7) for iy in range(1, 7)]
    face_parts = ((0,), (7,), (slice(1, 7), 0), (slice(1, 7), 7))
    inside = (slice(1, 7), slice(1, 7))

    def arrived_here(f):
        for load in loads[2 * places[f] : 2 * places[f] + 2]:
            load.wait()

    def fill(f, nodes):
        for ix, iy in nodes:
            weight = float(GLL_WEIGHTS[ix] * GLL_WEIGHTS[iy])
            if f == 0:
                raw = natural(0, ix, iy) * (wz * weight)
                summed = sum_third(raw)
                cz[ix, iy] = raw
                cx[ix, iy] = summed
                cy[ix, iy] = summed
            elif f == 2:
                scale[ix, iy] = sum_third(natural(2, ix, iy) * (wz * weight))
            elif f == 3:
                value = third_face * weight
                if ix == 0:
                    value = value + faces[0] * float(GLL_WEIGHTS[iy])
                if ix == 7:
                    value = value + faces[1] * float(GLL_WEIGHTS[iy])
                if iy == 0:
                    value = value + faces[2] * float(GLL_WEIGHTS[ix])
                if iy == 7:
                    value = value + faces[3] * float(GLL_WEIGHTS[ix])
                keep[ix, iy] = value
            else:
                homes[f][ix, iy] = sum_third(natural(places[f], ix, iy) * share(ix, iy))

    def damping_faces():
        spread = jnp.where(
            lax.broadcasted_iota(jnp.int32, (16, LANES), 1) // 8
            == lax.broadcasted_iota(jnp.int32, (16, LANES), 0),
            1.0,
            0.0,
        ).astype(F32)
        cells = [
            jnp.dot(
                jnp.concatenate([mask[f, 0], mask[f, 1]], axis=0).astype(F32),
                spread,
                preferred_element_type=F32,
            )
            for f in range(6)
        ]
        ends = jnp.where(zplace == 0, cells[4], jnp.where(zplace == 7, cells[5], 0.0))
        return [sum_third(wz * cell) for cell in cells[:4]], sum_third(ends)

    def join_first(home):
        first, last = join_x(home[0], home[7])
        home[0] = first
        home[7] = last

    def join_second(home):
        first, last = join_y(home[:, 0], home[:, 7])
        home[:, 0] = first
        home[:, 7] = last

    def pack_field(f):
        home = homes[f]
        if f > 0:
            join_first(home)
            join_second(home)
        put_faces(outs0.at[f], home[0], home[7], home[:, 0], home[:, 7])
        lines0[f] = corner_lines(home[0, 0], home[0, 7], home[7, 0], home[7, 7])

    def post_group(g):
        here = pl.ds(groups[g][0], len(groups[g]))
        every = (pl.ds(0, len(groups[g])),)
        out, into = outs0.at[here], ins0.at[here]
        post_lines(lines0.at[here], into, send0.at[4 + g], recv0.at[4 + g], every)
        post_faces(out, into, send0.at[g], recv0.at[g], every)

    def receive_group(g):
        here = pl.ds(groups[g][0], len(groups[g]))
        received(ins0.at[here, pl.ds(0, 12)], recv0.at[g])
        received(lines0.at[here, pl.ds(0, 4)], recv0.at[4 + g])

    for f in groups[0]:
        arrived_here(f)
        fill(f, faces_at)
        pack_field(f)
    pl.semaphore_wait(barrier, 8)
    post_group(0)
    loads[12].wait()
    faces, third_face = damping_faces()
    for f in groups[1]:
        if f != 3:
            arrived_here(f)
        fill(f, faces_at)
        pack_field(f)
    post_group(1)
    for home, joins in ((cz, (join_first, join_second)), (cy, (join_first,)), (cx, (join_second,))):
        for join in joins:
            join(home)

    def rates(here):
        one_over = 1.0 / scale[here]
        scale[here] = (TIME_STEP * TIME_STEP) * one_over
        keep[here] = 1.0 - TIME_STEP * keep[here] * one_over

    end_x = [jnp.where(low_x, F32(DERIVATIVE[i, 0]), F32(DERIVATIVE[i, 7])) for i in range(8)]
    end_y = [jnp.where(ey < 2, F32(DERIVATIVE[i, 0]), F32(DERIVATIVE[i, 7])) for i in range(8)]

    def fill_rows(here):
        rows = apply_eight([end_x[i] * cx[i, here] for i in range(8)], BACKWARD)
        for j in range(8):
            kx[j, here] = rows[j]
        rows = apply_eight([end_y[i] * cy[here, i] for i in range(8)], BACKWARD)
        for j in range(8):
            ky[here, j] = rows[j]

    for f in range(5):
        fill(f, inside_at)
    fill_tables()
    rates(inside)
    vf[1, 1:7, 1:7] = uf[inside] - vf[1, 1:7, 1:7]
    for c in range(1, 7, CHUNK):
        fill_rows(slice(c, c + CHUNK))

    for f in groups[2]:
        arrived_here(f)
        fill(f, faces_at)
        pack_field(f)
    post_group(2)
    for f in groups[2]:
        fill(f, inside_at)
    va[inside] = aa[8, 1:7, 1:7] - va[inside]

    def add_x(home, parts):
        for node, part in zip((0, 7), parts):
            home[node] = home[node] + part

    def add_y(home, parts):
        for node, part in zip((0, 7), parts):
            home[:, node] = home[:, node] + part

    def add_field(f):
        home = homes[f]
        parts_x = [read_x(ins0.at[f], side) for side in range(2)]
        parts_y = [read_y(ins0.at[f], side) for side in range(2)]
        add_x(home, parts_x)
        add_y(home, parts_y)
        if f == 0:
            add_x(cy, [sum_third(part) for part in parts_x])
            add_y(cx, [sum_third(part) for part in parts_y])
            for node, part in zip((0, 7), parts_x):
                first, last = join_y(part[0], part[7])
                cz[node, 0] = cz[node, 0] + (first - part[0])
                cz[node, 7] = cz[node, 7] + (last - part[7])
            for node, part in zip((0, 7), parts_y):
                first, last = join_x(part[0], part[7])
                cz[0, node] = cz[0, node] + (first - part[0])
                cz[7, node] = cz[7, node] + (last - part[7])
        for k, (ix, iy, _) in enumerate(node_d):
            home[ix, iy] = home[ix, iy] + read_line(ins0.at[f], k)

    receive_group(0)
    add_field(0)
    for c in (0, 7):
        fill_rows(slice(c, c + 1))

    add_field(1)

    def rest_of_setup():
        put_faces(ends_out, kx[0], kx[7], ky[:, 0], ky[:, 7])
        post_faces(ends_out, ends_in, send0.at[3], recv0.at[3])
        receive_group(1)
        for f in groups[1]:
            add_field(f)
        for here in face_parts:
            rates(here)
            vf[(1, *here)] = uf[here] - vf[(1, *here)]

    def times(values, which):
        high = values.astype(BF16)
        low = (values - high.astype(F32)).astype(BF16)
        both = jnp.dot(
            jnp.concatenate([high, low], axis=1), table[which], preferred_element_type=F32
        )
        return both[:, :LANES] + both[:, LANES:]

    def advance(source, gradient, v_from, u_to, v_to, between=None):
        slope = times(source[...].reshape(512, LANES), 0)
        gradient[2] = slope.reshape(8, 8, 8, LANES)
        acc[...] = times(cz[...].reshape(512, LANES) * slope, 1).reshape(8, 8, 8, LANES)
        for c in range(0, 8, CHUNK):
            here = slice(c, c + CHUNK)
            slopes = apply_eight([source[j, here] for j in range(8)], FORWARD)
            for j in range(8):
                gradient[0, j, here] = slopes[j]
            image = apply_eight([cx[j, here] * slopes[j] for j in range(8)], BACKWARD)
            image[0], image[7] = join_x(image[0], image[7])
            for j in range(8):
                acc[j, here] = acc[j, here] + image[j]
        if between is not None:
            between()
        for c in range(0, 8, CHUNK):
            here = slice(c, c + CHUNK)
            now = [source[here, j] for j in range(8)]
            slopes = apply_eight(now, FORWARD)
            for j in range(8):
                gradient[1, here, j] = slopes[j]
            image = apply_eight([cy[here, j] * slopes[j] for j in range(8)], BACKWARD)
            image[0], image[7] = join_y(image[0], image[7])
            for j in range(8):
                change = keep[here, j] * v_from[here, j] - scale[here, j] * (acc[here, j] + image[j])
                v_to[here, j] = change
                u_to[here, j] = now[j] + change

    def face_rows(u):
        along_x, along_y = kx[0] * u[0], ky[:, 0] * u[:, 0]
        for j in range(1, 8):
            along_x = along_x + kx[j] * u[j]
            along_y = along_y + ky[:, j] * u[:, j]
        return along_x, along_y

    def begin(field, turn, source, gradient, v_from, u_to, v_to, between=None):
        slot = turn % 2
        out, into = outs.at[field, slot], ins.at[field, slot]
        ssem, rsem = send.at[field, slot], recv.at[field, slot]

        def if_needed(post):
            if field == 0 or turn < STEPS // 2 - 1:
                post()

        own_x, own_y = face_rows(source)
        put_faces(out.at[0], own_x, own_x, own_y, own_y)
        post_faces(out.at[0], into.at[0], ssem.at[0], rsem.at[0])

        def send_corners():
            for side, node in ((0, 0), (1, 7)):
                sp_x[field, side] = scale[node] * own_x
                sp_y[field, side] = scale[:, node] * own_y
            lines_x = [jnp.sum(kx[:, n] * sp_y[field, s], axis=0) for s, n in ((0, 0), (1, 7))]
            lines_y = [jnp.sum(ky[n] * sp_x[field, s], axis=0) for s, n in ((0, 0), (1, 7))]
            lines[field, slot] = -(
                jnp.where(ey == 0, lines_x[0], lines_x[1])
                + jnp.where(low_x, lines_y[0], lines_y[1])
            )

            @if_needed
            def _():
                post_lines(lines.at[field, slot], into.at[1], ssem.at[2], rsem.at[2])

        if between is None:
            send_corners()
            advance(source, gradient, v_from, u_to, v_to)
        else:

            def both():
                between()
                send_corners()

            advance(source, gradient, v_from, u_to, v_to, both)

        @if_needed
        def _():
            next_x, next_y = face_rows(u_to)
            put_faces(out.at[1], next_x, next_x, next_y, next_y)
            post_faces(out.at[1], into.at[1], ssem.at[1], rsem.at[1])

    def mend(u, v, parts_x, parts_y):
        for node, part in zip((0, 7), parts_x):
            part = scale[node] * part
            u[node] = u[node] - part
            v[node] = v[node] - part
        for node, part in zip((0, 7), parts_y):
            part = scale[:, node] * part
            u[:, node] = u[:, node] - part
            v[:, node] = v[:, node] - part

    def complete(field, turn, u, v, second=True):
        slot = turn % 2
        out, into = outs.at[field, slot], ins.at[field, slot]
        sent(out.at[0], send.at[field, slot, 0])
        if second:
            sent(out.at[1], send.at[field, slot, 1])
            sent(lines.at[field, slot, pl.ds(0, 4)], send.at[field, slot, 2])
        received(into.at[0, pl.ds(0, 12)], recv.at[field, slot, 0])
        parts_x = [read_x(into.at[0], side) for side in range(2)]
        mend(u, v, parts_x, [read_y(into.at[0], side) for side in range(2)])

    def finish(field, turn, source, gradient, v_from, u_to, v_to):
        slot = turn % 2
        into = ins.at[field, slot, 1]
        advance(source, gradient, v_from, u_to, v_to)
        received(into.at[pl.ds(0, 12)], recv.at[field, slot, 1])
        parts_x, parts_y = [], []
        for s in range(2):
            part = read_x(into, s) - kn_x[s] * sp_x[field, s]
            parts_x.append(part)
            part = read_y(into, s) - kn_y[s] * sp_y[field, s]
            parts_y.append(part)
        mend(u_to, v_to, parts_x, parts_y)
        received(lines.at[field, slot, pl.ds(0, 4)], recv.at[field, slot, 2])
        for k, (ix, iy, _) in enumerate(node_d):
            part = scale[ix, iy] * read_line(into, k)
            u_to[ix, iy] = u_to[ix, iy] - part
            v_to[ix, iy] = v_to[ix, iy] - part

    def begin_u(turn, between=None):
        n = 2 * turn + 1
        begin(0, turn, uf, gu.at[n], vf.at[n], uf, vf.at[n + 1], between)

    def begin_a(turn):
        n = 8 - 2 * turn
        begin(1, turn, aa.at[n], ga.at[n], va, aa.at[n - 1], va)

    def finish_u(turn):
        n = 2 * turn + 2
        complete(0, turn, uf, vf.at[n])
        finish(0, turn, uf, gu.at[n], vf.at[n], uf, vf.at[n + 1])

    def finish_a(turn):
        n = 7 - 2 * turn
        complete(1, turn, aa.at[n], va)
        finish(1, turn, aa.at[n], ga.at[n], va, aa.at[n - 1], va)

    begin_u(0, rest_of_setup)
    receive_group(2)
    for f in groups[2]:
        add_field(f)
    for here in face_parts:
        va[here] = aa[(8, *here)] - va[here]
    begin_a(0)
    received(ends_in, recv0.at[3])
    for side in range(2):
        kn_x[side] = read_x(ends_in, side)
        kn_y[side] = read_y(ends_in, side)
    sent(ends_out, send0.at[3])
    for g, group in enumerate(groups):
        here = pl.ds(group[0], len(group))
        sent(outs0.at[here], send0.at[g])
        sent(lines0.at[here, pl.ds(0, 4)], send0.at[4 + g])

    def cycle(turn, carry):
        finish_u(turn)
        begin_u(turn + 1)
        finish_a(turn)
        begin_a(turn + 1)
        return carry

    for turn in range(STEPS // 2 - 1):
        cycle(turn, 0)

    def density_of(ns, ix):
        total = None
        for n in ns:
            for d in range(3):
                term = gu[n, d, ix] * ga[n, d, ix]
                total = term if total is None else total + term
        return total

    def moduli_of(ns, ix):
        modulus, impedance = None, None
        for n in ns:
            now, before, after = aa[n, ix], vf[n, ix], vf[n + 1, ix]
            a, b = now * (after - before), now * (after + before)
            modulus = a if modulus is None else modulus + a
            impedance = b if impedance is None else impedance + b
        return modulus, impedance

    for ix in range(8):
        sums[0, ix] = density_of(range(2, 8), ix)
        sums[1, ix], sums[2, ix] = moduli_of(range(2, 7), ix)

    last = STEPS // 2 - 1
    finish_u(last)
    for ix in range(8):
        sums[0, ix] = sums[0, ix] + density_of((8,), ix)
        modulus, impedance = moduli_of((7, 8), ix)
        sums[1, ix] = sums[1, ix] + modulus
        sums[2, ix] = sums[2, ix] + impedance
    complete(1, last, aa.at[1], va, second=False)
    source, gradient = aa.at[1], ga.at[1]
    gradient[2] = times(source[...].reshape(512, LANES), 0).reshape(8, 8, 8, LANES)
    for c in range(0, 8, CHUNK):
        here = slice(c, c + CHUNK)
        slopes = apply_eight([source[j, here] for j in range(8)], FORWARD)
        for j in range(8):
            gradient[0, j, here] = slopes[j]
        slopes = apply_eight([source[here, j] for j in range(8)], FORWARD)
        for j in range(8):
            gradient[1, here, j] = slopes[j]

    for ix in range(8):
        density = sums[0, ix] + density_of((1,), ix)
        modulus, impedance = moduli_of((1,), ix)
        modulus = sums[1, ix] + modulus
        impedance = (sums[2, ix] + impedance) * (1.0 - keep[ix])
        for iy in range(8):
            weight = wz * float(TIME_STEP * GLL_WEIGHTS[ix] * GLL_WEIGHTS[iy])
            rows = pl.ds(iy, 8, stride=8)
            dens_ref[ix, rows, :] = weight * density[iy]
            mod_ref[ix, rows, :] = modulus[iy]
            imp_ref[ix, rows, :] = impedance[iy]


def deliver(*refs):
    parts, outs, sem = refs[:3], refs[3:6], refs[6]
    stores = [
        pltpu.make_async_copy(
            parts[k].at[:, pl.ds(32 * half, 32), :],
            outs[k].at[pl.ds(8 * half, 8)],
            sem.at[2 * k + half],
        )
        for k in range(3)
        for half in range(2)
    ]
    for store in stores:
        store.start()
    for store in stores:
        store.wait()


def field(*lead):
    return pltpu.VMEM((*lead, 8, 8, 8, LANES), F32)


def per_device(shape_xy, *args):
    vectors = lambda *lead: pltpu.VMEM((*lead, 8, LANES), F32)
    hbm = pl.BlockSpec(memory_space=pltpu.HBM)
    vmem = pl.BlockSpec(memory_space=pltpu.VMEM)
    operands = [pltpu.with_memory_space_constraint(a, pltpu.HBM) for a in args]
    parts = pl.pallas_call(
        functools.partial(kernel, shape_xy),
        out_shape=(pltpu.VMEM((8, 64, LANES), F32),) * 3,
        in_specs=[hbm] * 7,
        out_specs=(vmem,) * 3,
        scratch_shapes=[
            pltpu.VMEM((6, 8, 64, LANES), F32),
            pltpu.VMEM(args[6].shape, jnp.int32),
            pltpu.VMEM((2, 2 * LANES, 2 * LANES), BF16),
            field(),
            field(),
            field(),
            field(),
            field(),
            field(),
            field(),
            field(),
            field(10),
            field(9),
            field(),
            field(9, 3),
            field(9, 3),
            field(),
            vectors(2, 2, 8),
            vectors(2, 2, 8),
            vectors(2, 8),
            vectors(2, 8),
            field(3),
            vectors(7, 12),
            vectors(7),
            vectors(7, 16),
            vectors(12),
            vectors(12),
            vectors(2, 2, 2, 12),
            vectors(2, 2),
            vectors(2, 2, 2, 16),
            pltpu.SemaphoreType.DMA((13,)),
            pltpu.SemaphoreType.DMA((7,)),
            pltpu.SemaphoreType.DMA((7,)),
            pltpu.SemaphoreType.DMA((2, 2, 3)),
            pltpu.SemaphoreType.DMA((2, 2, 3)),
        ],
        compiler_params=pltpu.CompilerParams(
            collective_id=0, has_side_effects=True, vmem_limit_bytes=48 * 1024 * 1024
        ),
    )(*operands)
    return pl.pallas_call(
        deliver,
        out_shape=(pltpu.HBM(args[0].shape, F32),) * 3,
        in_specs=[pl.BlockSpec(memory_space=pl.ANY)] * 3,
        out_specs=(hbm,) * 3,
        scratch_shapes=[pltpu.SemaphoreType.DMA((6,))],
    )(*[pltpu.with_memory_space_constraint(part, pltpu.VMEM) for part in parts])


def solution(mesh):
    shape_xy = (mesh.shape["gx"], mesh.shape["gy"])
    in_specs = (P("gx", "gy", None),) * 6 + (P(None, "gx", "gy", None),)
    out_specs = (P("gx", "gy", None),) * 3
    return jax.shard_map(
        functools.partial(per_device, shape_xy),
        mesh=mesh,
        in_specs=in_specs,
        out_specs=out_specs,
        check_vma=False,
    )
```
